512 devices in a mesh: row: 16 (over z_hi, x), col: 32 (over z_lo, y, core).
Axes of the slice: x: 4, y: 8, z: 8 (z_hi: 4, z_lo: 2; z = z_hi * 2 + z_lo), core: 2. Of those that a mesh axis runs over, the one named last changes fastest.
Arguments:
- pair_rep: bfloat16 [1024, 1024, 128], P('row', 'col'), may hold values from -400 to 400
- true_bins: int32 [1024, 1024], P('row', 'col'), may hold values from 0 to 63, as said below
- w_in: bfloat16 [128, 512], replicated, may hold values from -0.5 to 0.5
- w_out: bfloat16 [512, 128], replicated, may hold values from -0.25 to 0.25
- w_head: bfloat16 [128, 64], replicated, may hold values from -1 to 1
Outputs:
- grad_pair: bfloat16 [1024, 1024, 128], P('row', 'col')
- grad_in: float32 [128, 512], P('row', 'col')
- grad_out: float32 [512, 128], P('row', 'col')
- grad_head: float32 [128, 64], P('row', 'col')
The draws below stay inside these ranges and needn't reach their ends.
Inputs may be any that keep to these rules, and one draw needn't show every extreme that they name: The bins are symmetric over tokens: true_bins equals mirror(true_bins).
All inputs are finite; a program needn't handle non-finite values.
Results may differ from the reference program's by a relative error of at most 0.0095.
The reference program's roundings to bfloat16 on the way (of `normed`, `hidden`, `residual`, `d_sym`, `d_logit`, `d_update` and `d_hidden`) count: a program that leaves them out, or rounds other values in their place, can miss the bound.
Values may be sent and summed in bfloat16 or wider, within the bound.
No kernel may reach another device: no remote copies, remote signals or barrier semaphores. Data moves between devices by JAX's collectives and lax.ppermute only.
A program may use at most 64 MiB of HBM per device.

```python
import math
import jax
import jax.numpy as jnp
from jax import lax

C = 128
F = 512
K = 64
ROWS_TILE = 64
COLS_TILE = 32
CROP = 1024
N_ROW = 16
N_COL = 32


def token_maps():
    index = jnp.arange(CROP, dtype=jnp.int32)
    row_token = (index % ROWS_TILE // N_COL * N_ROW + index // ROWS_TILE) * N_COL + index % N_COL
    col_token = index % COLS_TILE * N_COL + index // COLS_TILE
    return (row_token, col_token)


def tile_factor(key):
    key_pick, key_first = jax.random.split(key, 2)
    tiles = N_ROW * N_COL
    picked = jax.random.randint(key_pick, (tiles,), 0, 32) == 0
    first = jax.random.randint(key_first, (), 0, tiles)
    picked = jnp.logical_or(picked, jnp.arange(tiles, dtype=jnp.int32) == first)
    factor = jnp.where(picked, 30.0, 1.0).astype(jnp.float32).reshape(N_ROW, 1, N_COL, 1, 1)
    return factor


def draw_pair_rep(key, part):
    key = jax.random.fold_in(key, 11)
    key_base = jax.random.fold_in(key, 0)
    key_tile = jax.random.fold_in(key, 4)
    values = jax.random.normal(key_base, (CROP, CROP, C), jnp.float32)
    shaped = values.reshape(N_ROW, ROWS_TILE, N_COL, COLS_TILE, C) * tile_factor(key_tile)
    values = shaped.reshape(CROP, CROP, C)
    return jnp.clip(values, -400.0, 400.0).astype(jnp.bfloat16)


def draw_w_head(key, part):
    key = jax.random.fold_in(key, 23)
    key_base = jax.random.fold_in(key, 0)
    values = jax.random.normal(key_base, (C, K), jnp.float32) / math.sqrt(C)
    return jnp.clip(values, -1.0, 1.0).astype(jnp.bfloat16)


def draw_true_bins(key, part):
    key = jax.random.fold_in(key, 37)
    raw_bins = jax.random.randint(key, (CROP, CROP), 0, K, dtype=jnp.int32)
    index = jnp.arange(CROP, dtype=jnp.int32)
    symmetric = jnp.where(index[:, None] <= index[None, :], raw_bins, raw_bins.T)
    row_token, col_token = token_maps()
    return symmetric[row_token][:, col_token]


def gaussian(key, extent, scale, bound, kind=jnp.bfloat16):
    values = scale * jax.random.normal(key, extent, jnp.float32)
    return jnp.clip(values, min=-bound, max=bound).astype(kind)


def setup_inputs(seed: int = 0) -> dict:
    key_list = jax.random.split(jax.random.key(seed), 6)
    pair_rep = draw_pair_rep(jax.random.fold_in(key_list[5], 71), 0)
    true_bins = draw_true_bins(jax.random.fold_in(key_list[5], 71), 0)
    w_in = gaussian(key_list[2], (C, F), C ** -0.5, 0.5)
    w_out = gaussian(key_list[3], (F, C), F ** -0.5, 0.25)
    w_head = draw_w_head(jax.random.fold_in(key_list[5], 71), 0)
    return dict(pair_rep=pair_rep, true_bins=true_bins, w_in=w_in, w_out=w_out, w_head=w_head)


epsilon = 1e-05

def normalize(values):
    centred = values - lax.optimization_barrier(jnp.mean(values, axis=-1, keepdims=True))
    variance = lax.optimization_barrier(jnp.mean(centred * centred, axis=-1, keepdims=True))
    inv_std = lax.rsqrt(variance + epsilon)
    return (centred * inv_std, inv_std)

def row_place(token):
    return token // N_COL % N_ROW * ROWS_TILE + token // (N_COL * N_ROW) * N_COL + token % N_COL

def col_place(token):
    return token % N_COL * COLS_TILE + token // N_COL

def mirror(values):
    index = jnp.arange(CROP, dtype=jnp.int32)
    col_token = index % COLS_TILE * N_COL + index // COLS_TILE
    row_token = (index % ROWS_TILE // N_COL * N_ROW + index // ROWS_TILE) * N_COL + index % N_COL
    source_rows = row_place(col_token).astype(jnp.int32)
    source_cols = col_place(row_token).astype(jnp.int32)
    return jnp.transpose(values[source_rows][:, source_cols], (1, 0, 2))

def forward_block(pair_block, w_in, w_out, w_head):
    x_hat, inv_std = normalize(pair_block.astype(jnp.float32))
    normed = x_hat.astype(jnp.bfloat16)
    hidden = jnp.maximum(jnp.dot(normed, w_in, preferred_element_type=jnp.float32), 0.0).astype(jnp.bfloat16)
    update = jnp.dot(hidden, w_out, preferred_element_type=jnp.float32)
    residual = (pair_block.astype(jnp.float32) + update).astype(jnp.bfloat16)
    logits = jnp.dot(residual, w_head, preferred_element_type=jnp.float32)
    return (residual, logits)

def backward_block(pair_block, residual, d_logit, w_in, w_out, w_head):
    x_hat, inv_std = normalize(pair_block.astype(jnp.float32))
    normed = x_hat.astype(jnp.bfloat16)
    pre_act = jnp.dot(normed, w_in, preferred_element_type=jnp.float32)
    hidden = jnp.maximum(pre_act, 0.0).astype(jnp.bfloat16)
    d_resid = jnp.dot(d_logit, w_head.T, preferred_element_type=jnp.float32)
    d_update = d_resid.astype(jnp.bfloat16)
    g_out = jnp.dot(hidden.T, d_update, preferred_element_type=jnp.float32)
    back_hidden = jnp.dot(d_update, w_out.T, preferred_element_type=jnp.float32)
    d_hidden = jnp.where(pre_act > 0.0, back_hidden, 0.0).astype(jnp.bfloat16)
    g_in = jnp.dot(normed.T, d_hidden, preferred_element_type=jnp.float32)
    d_normed = jnp.dot(d_hidden, w_in.T, preferred_element_type=jnp.float32)
    first_mean = lax.optimization_barrier(jnp.mean(d_normed, axis=-1, keepdims=True))
    second_mean = lax.optimization_barrier(jnp.mean(d_normed * x_hat, axis=-1, keepdims=True))
    d_input = inv_std * (d_normed - first_mean - x_hat * second_mean)
    g_head = jnp.dot(residual.T, d_logit, preferred_element_type=jnp.float32)
    return ((d_resid + d_input).astype(jnp.bfloat16), g_in, g_out, g_head)

def reference(pair_rep, true_bins, w_in, w_out, w_head):
    count = CROP // N_COL
    blocks = pair_rep.reshape(count, N_COL * CROP, C)

    def forward(pair_block):
        return forward_block(pair_block, w_in, w_out, w_head)
    residual, logits = lax.map(forward, blocks)
    logits = logits.reshape(CROP, CROP, K)
    sym_logits = logits + mirror(logits)
    probability = jax.nn.softmax(sym_logits, axis=-1)
    onehot = (true_bins[:, :, None] == jnp.arange(K, dtype=jnp.int32)).astype(jnp.float32)
    d_sym = (probability - onehot).astype(jnp.bfloat16)
    d_logit = (d_sym.astype(jnp.float32) + mirror(d_sym).astype(jnp.float32)).astype(jnp.bfloat16)
    d_blocks = d_logit.reshape(count, N_COL * CROP, K)

    def backward(totals, inputs):
        d_pair, g_in, g_out, g_head = backward_block(inputs[0], inputs[1], inputs[2], w_in, w_out, w_head)
        return ((totals[0] + g_in, totals[1] + g_out, totals[2] + g_head), d_pair)
    start = (jnp.zeros((C, F), jnp.float32), jnp.zeros((F, C), jnp.float32), jnp.zeros((C, K), jnp.float32))
    totals, d_pair = lax.scan(backward, start, (blocks, residual, d_blocks))
    return (d_pair.reshape(CROP, CROP, C), totals[0] / CROP, totals[1] / CROP, totals[2] / CROP)
```

```python
import jax
import jax.numpy as jnp
from jax import lax
from jax.sharding import PartitionSpec as P

epsilon = 1e-05


def normalize(values):
    centred = values - jnp.mean(values, axis=-1, keepdims=True)
    variance = jnp.mean(centred * centred, axis=-1, keepdims=True)
    inv_std = lax.rsqrt(variance + epsilon)
    return (centred * inv_std, inv_std)


def as_tiles(gradient, n_row, n_col):
    first, second = gradient.shape
    split = gradient.reshape(n_row, first // n_row, n_col, second // n_col)
    return jnp.transpose(split, (0, 2, 1, 3)).reshape(
        n_row * n_col, first // n_row * (second // n_col)
    )


def shards(pair_rep, true_bins, w_in, w_out, w_head):
    row_count, col_count, channels = pair_rep.shape
    n_row = lax.axis_size("row")
    n_col = lax.axis_size("col")
    cycles = row_count // n_col
    span = n_col * col_count
    bins_count = w_head.shape[1]
    blocks = pair_rep.reshape(cycles, span, channels)

    def forward(pair_block):
        x_hat, inv_std = normalize(pair_block.astype(jnp.float32))
        normed = x_hat.astype(jnp.bfloat16)
        hidden = jnp.maximum(jnp.dot(normed, w_in, preferred_element_type=jnp.float32), 0.0).astype(
            jnp.bfloat16
        )
        update = jnp.dot(hidden, w_out, preferred_element_type=jnp.float32)
        residual = (pair_block.astype(jnp.float32) + update).astype(jnp.bfloat16)
        logits = jnp.dot(residual, w_head, preferred_element_type=jnp.float32)
        return (residual, logits)

    residual, logits = lax.map(forward, blocks)
    folded = logits.reshape(cycles, n_col, cycles, n_row, bins_count)
    outgoing = jnp.transpose(folded, (3, 1, 0, 2, 4)).reshape(n_row * n_col, -1)
    incoming = lax.all_to_all(
        outgoing, ("row", "col"), split_axis=0, concat_axis=0, tiled=True
    ).reshape(n_row, n_col, cycles, cycles, bins_count)
    mirrored = jnp.transpose(incoming, (3, 1, 2, 0, 4)).reshape(cycles, span, bins_count)
    sym_logits = logits + mirrored
    probability = jax.nn.softmax(sym_logits, axis=-1)
    bin_blocks = true_bins.reshape(cycles, span)
    onehot = (bin_blocks[:, :, None] == jnp.arange(bins_count, dtype=jnp.int32)).astype(jnp.float32)
    d_sym = (probability - onehot).astype(jnp.bfloat16)
    d_logit = d_sym + d_sym

    def backward(totals, inputs):
        pair_block, resid_block, d_block = inputs
        x_hat, inv_std = normalize(pair_block.astype(jnp.float32))
        normed = x_hat.astype(jnp.bfloat16)
        pre_act = jnp.dot(normed, w_in, preferred_element_type=jnp.float32)
        hidden = jnp.maximum(pre_act, 0.0).astype(jnp.bfloat16)
        d_resid = jnp.dot(d_block, w_head.T, preferred_element_type=jnp.float32)
        d_update = d_resid.astype(jnp.bfloat16)
        g_out = jnp.dot(hidden.T, d_update, preferred_element_type=jnp.float32)
        back_hidden = jnp.dot(d_update, w_out.T, preferred_element_type=jnp.float32)
        d_hidden = jnp.where(pre_act > 0.0, back_hidden, 0.0).astype(jnp.bfloat16)
        g_in = jnp.dot(normed.T, d_hidden, preferred_element_type=jnp.float32)
        d_normed = jnp.dot(d_hidden, w_in.T, preferred_element_type=jnp.float32)
        first_mean = jnp.mean(d_normed, axis=-1, keepdims=True)
        second_mean = jnp.mean(d_normed * x_hat, axis=-1, keepdims=True)
        d_input = inv_std * (d_normed - first_mean - x_hat * second_mean)
        g_head = jnp.dot(resid_block.T, d_block, preferred_element_type=jnp.float32)
        new_totals = (totals[0] + g_in, totals[1] + g_out, totals[2] + g_head)
        return (new_totals, (d_resid + d_input).astype(jnp.bfloat16))

    start = (
        jnp.zeros(w_in.shape, jnp.float32),
        jnp.zeros(w_out.shape, jnp.float32),
        jnp.zeros(w_head.shape, jnp.float32),
    )
    totals, d_pair = lax.scan(backward, start, (blocks, residual, d_logit))
    packed = jnp.concatenate(
        [
            as_tiles(totals[0], n_row, n_col),
            as_tiles(totals[1], n_row, n_col),
            as_tiles(totals[2], n_row, n_col),
        ],
        axis=1,
    )
    shares = lax.all_to_all(
        packed.astype(jnp.bfloat16), ("row", "col"), split_axis=0, concat_axis=0, tiled=True
    )
    own_share = jnp.sum(shares.astype(jnp.float32), axis=0) / (row_count * n_row)
    in_shape = (w_in.shape[0] // n_row, w_in.shape[1] // n_col)
    out_shape = (w_out.shape[0] // n_row, w_out.shape[1] // n_col)
    head_shape = (w_head.shape[0] // n_row, w_head.shape[1] // n_col)
    in_size = in_shape[0] * in_shape[1]
    out_size = out_shape[0] * out_shape[1]
    grad_in = own_share[:in_size].reshape(in_shape)
    grad_out = own_share[in_size : in_size + out_size].reshape(out_shape)
    grad_head = own_share[in_size + out_size :].reshape(head_shape)
    return (d_pair.reshape(row_count, col_count, channels), grad_in, grad_out, grad_head)


def solution(mesh):
    placed = (P("row", "col", None), P("row", "col"), P(), P(), P())
    return jax.shard_map(
        shards,
        mesh=mesh,
        in_specs=placed,
        out_specs=(P("row", "col", None), P("row", "col"), P("row", "col"), P("row", "col")),
        check_vma=False,
    )
```

```python
import functools

import jax
import jax.numpy as jnp
from jax import lax
from jax.experimental import pallas as pl
from jax.experimental.pallas import tpu as pltpu
from jax.sharding import PartitionSpec as P

epsilon = 1e-05
f32 = jnp.float32
bf16 = jnp.bfloat16

code_gain = 16.0
code_steps = 1850.0

CYCLES = 2
STEPS = 4


def dot(first, second):
    return jnp.dot(first, second, preferred_element_type=f32)


def encode(values):
    size = jnp.log(1.0 + jnp.abs(values) * code_gain) * code_steps + 0.5
    return jnp.where(values < 0.0, -size, size).astype(jnp.int32)


def decode(codes):
    codes = codes.astype(f32)
    size = (jnp.exp(jnp.abs(codes) * (1.0 / code_steps)) - 1.0) * (1.0 / code_gain)
    return jnp.where(codes < 0.0, -size, size)


def normalize(values):
    centred = values - jnp.mean(values, axis=-1, keepdims=True)
    variance = jnp.mean(centred * centred, axis=-1, keepdims=True)
    inv_std = lax.rsqrt(variance + epsilon)
    return (centred * inv_std, inv_std)


def send_kernel(pair_ref, w_in_ref, w_out_ref, w_wide_ref, send_ref, rows_ref):
    n_row = send_ref.shape[0]
    span = send_ref.shape[1]
    channels = pair_ref.shape[-1]
    values = pair_ref[...].reshape(-1, channels).astype(f32)
    half = values.shape[0] // CYCLES
    x_hat, _ = normalize(values)
    hidden = jnp.maximum(dot(x_hat.astype(bf16), w_in_ref[...]), 0.0).astype(bf16)
    residual = (values + dot(hidden, w_out_ref[...])).astype(bf16)
    wide = jnp.concatenate([residual[:half], residual[half:]], axis=1)
    rows_ref[...] = encode(dot(wide, w_wide_ref[...]))
    for r in range(n_row):
        send_ref[r] = rows_ref[pl.ds(r, span, stride=n_row), :].astype(jnp.int16)


def prepare_kernel(
    pair_ref,
    bins_ref,
    w_in_ref,
    w_out_ref,
    w_wide_ref,
    hidden_ref,
    hidden_t_ref,
    normed_t_ref,
    residual_t_ref,
    x_hat_ref,
    inv_ref,
    logits_ref,
    bins_wide_ref,
    values_ref,
):
    channels = pair_ref.shape[-1]
    n_row = pair_ref.shape[2] // CYCLES
    count = pair_ref.shape[1]
    for a in range(CYCLES):
        for b in range(CYCLES):
            values_ref[a, :, b] = pair_ref[b, :, a * n_row : (a + 1) * n_row, :].astype(f32)
    values = values_ref[...].reshape(-1, channels)
    half = values.shape[0] // CYCLES
    x_hat, inv_std = normalize(values)
    normed = x_hat.astype(bf16)
    hidden = jnp.maximum(dot(normed, w_in_ref[...]), 0.0).astype(bf16)
    residual = (values + dot(hidden, w_out_ref[...])).astype(bf16)
    hidden_ref[...] = hidden
    hidden_t_ref[...] = hidden.T
    normed_t_ref[...] = normed.T
    residual_t_ref[...] = residual.T
    x_hat_ref[...] = x_hat
    inv_ref[...] = jnp.broadcast_to(inv_std, x_hat.shape)
    logits_ref[...] = dot(
        jnp.concatenate([residual[:half], residual[half:]], axis=1), w_wide_ref[...]
    )
    columns = bins_ref.shape[-1]
    row_of = lax.broadcasted_iota(jnp.int32, (1, n_row, columns), 1)
    column_of = lax.broadcasted_iota(jnp.int32, (1, n_row, columns), 2)
    own = column_of % n_row == row_of
    lane = lax.broadcasted_iota(jnp.int32, (columns, channels), 1)
    source = lax.broadcasted_iota(jnp.int32, (columns, channels), 0)
    spread = (lane // (channels // CYCLES) == source // n_row).astype(f32).astype(bf16)
    for b in range(CYCLES):
        bins = bins_ref[b].astype(f32)
        picked = jnp.where(own, jnp.broadcast_to(bins[:, None, :], (count, n_row, columns)), 0.0)
        wide = dot(picked.reshape(count * n_row, columns).astype(bf16), spread)
        bins_wide_ref[:, b] = wide.reshape(count, n_row, channels)


def backward_kernel(
    recv_ref,
    hidden_ref,
    hidden_t_ref,
    normed_t_ref,
    residual_t_ref,
    x_hat_ref,
    inv_ref,
    logits_ref,
    bins_wide_ref,
    w_in_t_ref,
    w_out_t_ref,
    w_head_wide_ref,
    grad_ref,
    part_ref,
    rows_ref,
    in_ref,
    out_ref,
    head_ref,
):
    step = pl.program_id(0)
    n_row = recv_ref.shape[0]
    span = recv_ref.shape[1]
    count = span // CYCLES
    channels = grad_ref.shape[-1]
    bins_count = channels // CYCLES
    half = span * n_row

    for r in range(n_row):
        rows_ref[pl.ds(r, span, stride=n_row), :] = decode(recv_ref[r])
    sym = logits_ref[...] + rows_ref[...]
    lane = lax.broadcasted_iota(jnp.int32, (1, channels), 1)
    left = lane < bins_count
    low = jnp.max(jnp.where(left, sym, -jnp.inf), axis=-1, keepdims=True)
    high = jnp.max(jnp.where(left, -jnp.inf, sym), axis=-1, keepdims=True)
    grown = jnp.exp(sym - jnp.where(left, low, high))
    low = jnp.sum(jnp.where(left, grown, 0.0), axis=-1, keepdims=True)
    high = jnp.sum(jnp.where(left, 0.0, grown), axis=-1, keepdims=True)
    probability = grown / jnp.where(left, low, high)
    own_bin = (lane % bins_count).astype(f32)
    onehot = jnp.where(bins_wide_ref[...].reshape(half, channels) == own_bin, 1.0, 0.0)
    d_sym = probability - onehot
    d_logit = (d_sym + d_sym).astype(bf16)

    wide = dot(d_logit, w_head_wide_ref[...])
    d_resid = jnp.concatenate([wide[:, :channels], wide[:, channels:]], axis=0)
    d_update = d_resid.astype(bf16)
    back = dot(d_update, w_out_t_ref[...]).astype(bf16)
    hidden = hidden_ref[...]
    d_hidden = jnp.where(hidden > 0, back, jnp.zeros_like(back))
    d_normed = dot(d_hidden, w_in_t_ref[...])
    x_hat = x_hat_ref[...]
    first_mean = jnp.mean(d_normed, axis=-1, keepdims=True)
    second_mean = jnp.mean(d_normed * x_hat, axis=-1, keepdims=True)
    d_pair = d_resid + inv_ref[...] * (d_normed - first_mean - x_hat * second_mean)
    d_pair = d_pair.astype(bf16).reshape(CYCLES, count, CYCLES, n_row, channels)
    for a in range(CYCLES):
        for b in range(CYCLES):
            grad_ref[b, :, a * n_row : (a + 1) * n_row, :] = d_pair[a, :, b]

    g_in = dot(normed_t_ref[...], d_hidden)
    g_out = dot(hidden_t_ref[...], d_update)
    g_head = jnp.where(
        left,
        dot(residual_t_ref[:, :half], d_logit),
        dot(residual_t_ref[:, half:], d_logit),
    )

    @pl.when(step == 0)
    def _():
        in_ref[...] = g_in
        out_ref[...] = g_out
        head_ref[...] = g_head

    @pl.when(step > 0)
    def _():
        in_ref[...] += g_in
        out_ref[...] += g_out
        head_ref[...] += g_head

    @pl.when(step == STEPS - 1)
    def _():
        rows = channels // n_row
        tiles = in_ref.shape[1] // channels
        long = tiles * rows
        for r in range(n_row):
            mine = in_ref[r * rows : (r + 1) * rows, :]
            part_ref[r, 0:long, :] = jnp.concatenate(
                [mine[:, t * channels : (t + 1) * channels] for t in range(tiles)], axis=0
            ).astype(bf16)
            part_ref[r, long : 2 * long, :] = out_ref[r * long : (r + 1) * long, :].astype(bf16)
            mine = head_ref[r * rows : (r + 1) * rows, :]
            part_ref[r, 2 * long : 2 * long + 2 * rows, :] = jnp.concatenate(
                [mine, jnp.zeros_like(mine)], axis=0
            ).astype(bf16)


def lanes_of(shape, axis):
    return lax.broadcasted_iota(jnp.int32, shape, axis)


def fold_matrix(width, kind):
    shape = (128, 128)
    return (lanes_of(shape, 0) % width == lanes_of(shape, 1) % width).astype(f32).astype(kind)


def middle_kernel(recv_ref, send_ref):
    n_col = send_ref.shape[0]
    total = recv_ref[0].astype(f32)
    for r in range(1, recv_ref.shape[0]):
        total = total + recv_ref[r].astype(f32)
    rows, tiles = 8, 4
    mine = total[: rows * tiles]
    group = lanes_of((1, rows, 128), 2) // 16 == lanes_of((1, rows, 128), 1)
    spread = jnp.where(group, jnp.broadcast_to(mine[:, None, :], (rows * tiles, rows, 128)), 0.0)
    folded = dot(spread.reshape(-1, 128).astype(bf16), fold_matrix(16, bf16))
    folded = folded.reshape(tiles, rows, rows, 128)
    slot = lanes_of((1, rows, 1, 128), 3) // 16 == lanes_of((1, rows, 1, 128), 1)
    part_in = jnp.sum(jnp.where(slot, folded, 0.0), axis=1).reshape(n_col, 128)
    mine = total[32:64]
    group = lanes_of((1, n_col, 128), 2) // 4 == lanes_of((1, n_col, 128), 1)
    spread = jnp.where(group, jnp.broadcast_to(mine[:, None, :], (32, n_col, 128)), 0.0)
    folded = dot(spread.reshape(-1, 128).astype(bf16), fold_matrix(4, bf16))
    folded = folded.reshape(32, n_col, 128)
    slot = lanes_of((32, 1, 128), 2) // 4 == lanes_of((32, 1, 128), 0)
    part_out = jnp.sum(jnp.where(slot, folded, 0.0), axis=0)
    mine = total[64:72]
    group = lanes_of((1, n_col, 128), 2) % 64 // 2 == lanes_of((1, n_col, 128), 1)
    spread = jnp.where(group, jnp.broadcast_to(mine[:, None, :], (8, n_col, 128)), 0.0)
    folded = dot(spread.reshape(-1, 128).astype(bf16), fold_matrix(2, bf16))
    folded = folded.reshape(8, n_col, 128)
    slot = lanes_of((8, 1, 128), 2) // 2 == lanes_of((8, 1, 128), 0)
    part_head = jnp.sum(jnp.where(slot, folded, 0.0), axis=0)
    send_ref[:, 0:128] = part_in
    send_ref[:, 128:256] = part_out
    send_ref[:, 256:384] = part_head


def final_kernel(scale, recv_ref, in_ref, out_ref, head_ref):
    total = jnp.sum(recv_ref[...], axis=0, keepdims=True) * scale

    def unfold(row, out):
        count, width = out.shape
        shape = (count, 128)
        lane = lanes_of(shape, 1)
        picked = jnp.where(lane // width == lanes_of(shape, 0), jnp.broadcast_to(row, shape), 0.0)
        shape = (128, width)
        fold = (lanes_of(shape, 0) % width == lanes_of(shape, 1)).astype(f32)
        out[...] = jnp.dot(
            picked, fold, precision=lax.Precision.HIGHEST, preferred_element_type=f32
        )

    unfold(total[:, 0:128], in_ref)
    unfold(total[:, 128:256], out_ref)
    unfold(total[:, 256:384], head_ref)


def whole(array):
    return pl.BlockSpec(array.shape, lambda g: (0,) * array.ndim)


def params():
    return pltpu.CompilerParams(vmem_limit_bytes=40 * 1024 * 1024)


def shards(pair_rep, true_bins, w_in, w_out, w_head):
    row_count, col_count, channels = pair_rep.shape
    n_row = lax.axis_size("row")
    n_col = lax.axis_size("col")
    hidden_count = w_in.shape[1]
    bins_count = w_head.shape[1]
    pairs = row_count * col_count
    cycled = pair_rep.reshape(CYCLES, n_col, col_count, channels)
    bins = true_bins.reshape(CYCLES, n_col, col_count)
    blank = jnp.zeros_like(w_head)
    w_wide = jnp.concatenate(
        [jnp.concatenate([w_head, blank], axis=1), jnp.concatenate([blank, w_head], axis=1)],
        axis=0,
    )
    count = n_col // STEPS
    span = CYCLES * count
    block = pairs // STEPS
    half = block // CYCLES
    pair_spec = pl.BlockSpec((CYCLES, count, col_count, channels), lambda g: (0, g, 0, 0))
    send_spec = pl.BlockSpec((n_row, span, channels), lambda g: (0, g, 0))

    send = pl.pallas_call(
        send_kernel,
        grid=(STEPS,),
        in_specs=[pair_spec, whole(w_in), whole(w_out), whole(w_wide)],
        out_specs=send_spec,
        out_shape=jax.ShapeDtypeStruct((n_row, CYCLES * n_col, channels), jnp.int16),
        scratch_shapes=[pltpu.VMEM((half, channels), jnp.int32)],
        compiler_params=params(),
        name="forward",
    )(cycled, w_in, w_out, w_wide)

    recv = lax.all_to_all(
        send.reshape(n_row * n_col, CYCLES, channels),
        ("row", "col"),
        split_axis=0,
        concat_axis=0,
        tiled=True,
    ).reshape(n_row, CYCLES * n_col, channels)

    def rows_spec(width):
        return pl.BlockSpec((block, width), lambda g: (g, 0))

    def columns_spec(height):
        return pl.BlockSpec((height, block), lambda g: (0, g))

    logits_spec = pl.BlockSpec((half, channels), lambda g: (g, 0))
    bins_spec = pl.BlockSpec((count, CYCLES, n_row, channels), lambda g: (g, 0, 0, 0))
    kept_specs = [
        rows_spec(hidden_count),
        columns_spec(hidden_count),
        columns_spec(channels),
        columns_spec(channels),
        rows_spec(channels),
        rows_spec(channels),
        logits_spec,
        bins_spec,
    ]
    kept = pl.pallas_call(
        prepare_kernel,
        grid=(STEPS,),
        in_specs=[
            pair_spec,
            pl.BlockSpec((CYCLES, count, col_count), lambda g: (0, g, 0)),
            whole(w_in),
            whole(w_out),
            whole(w_wide),
        ],
        out_specs=kept_specs,
        out_shape=[
            jax.ShapeDtypeStruct((pairs, hidden_count), bf16),
            jax.ShapeDtypeStruct((hidden_count, pairs), bf16),
            jax.ShapeDtypeStruct((channels, pairs), bf16),
            jax.ShapeDtypeStruct((channels, pairs), bf16),
            jax.ShapeDtypeStruct((pairs, channels), f32),
            jax.ShapeDtypeStruct((pairs, channels), f32),
            jax.ShapeDtypeStruct((pairs // CYCLES, channels), f32),
            jax.ShapeDtypeStruct((n_col, CYCLES, n_row, channels), f32),
        ],
        scratch_shapes=[pltpu.VMEM((CYCLES, count, CYCLES, n_row, channels), f32)],
        compiler_params=params(),
        cost_estimate=pl.CostEstimate(
            flops=2 * pairs * 2 * channels * hidden_count, bytes_accessed=8 * 2**20, transcendentals=0
        ),
        name="prepare",
    )(cycled, bins, w_in, w_out, w_wide)

    w_in_t = w_in.T
    w_out_t = w_out.T
    w_head_wide = w_wide.T
    part_rows = 2 * (hidden_count // n_row) + 16
    d_pair, part = pl.pallas_call(
        backward_kernel,
        grid=(STEPS,),
        in_specs=[send_spec] + kept_specs + [whole(w_in_t), whole(w_out_t), whole(w_head_wide)],
        out_specs=[pair_spec, pl.BlockSpec((n_row, part_rows, channels), lambda g: (0, 0, 0))],
        out_shape=[
            jax.ShapeDtypeStruct(cycled.shape, bf16),
            jax.ShapeDtypeStruct((n_row, part_rows, channels), bf16),
        ],
        scratch_shapes=[
            pltpu.VMEM((half, channels), f32),
            pltpu.VMEM((channels, hidden_count), f32),
            pltpu.VMEM((hidden_count, channels), f32),
            pltpu.VMEM((channels, channels), f32),
        ],
        compiler_params=params(),
        name="backward",
    )(recv, *kept, w_in_t, w_out_t, w_head_wide)

    part = lax.all_to_all(part, "row", split_axis=0, concat_axis=0, tiled=True)
    share = pl.pallas_call(
        middle_kernel,
        out_shape=jax.ShapeDtypeStruct((n_col, 3 * channels), f32),
        name="sum_rows",
    )(part)
    share = lax.all_to_all(share, "col", split_axis=0, concat_axis=0, tiled=True)
    grad_in, grad_out, grad_head = pl.pallas_call(
        functools.partial(final_kernel, 1.0 / (row_count * n_row)),
        out_shape=[
            jax.ShapeDtypeStruct((channels // n_row, hidden_count // n_col), f32),
            jax.ShapeDtypeStruct((hidden_count // n_row, channels // n_col), f32),
            jax.ShapeDtypeStruct((channels // n_row, bins_count // n_col), f32),
        ],
        name="sum_columns",
    )(share)
    return (d_pair.reshape(row_count, col_count, channels), grad_in, grad_out, grad_head)


def solution(mesh):
    placed = (P("row", "col", None), P("row", "col"), P(), P(), P())
    return jax.shard_map(
        shards,
        mesh=mesh,
        in_specs=placed,
        out_specs=(P("row", "col", None), P("row", "col"), P("row", "col"), P("row", "col")),
        check_vma=False,
    )
```

```python
import functools

import jax
import jax.numpy as jnp
from jax import lax
from jax.experimental import pallas as pl
from jax.experimental.pallas import tpu as pltpu
from jax.sharding import PartitionSpec as P

epsilon = 1e-05
f32 = jnp.float32
bf16 = jnp.bfloat16

code_gain = 16.0
code_steps = 1850.0

CYCLES = 2
STEPS = 4


def dot(first, second):
    return jnp.dot(first, second, preferred_element_type=f32)


def dot_t(first, second):
    return lax.dot_general(first, second, (((1,), (1,)), ((), ())), preferred_element_type=f32)


def widen(w_head_t):
    blank = jnp.zeros_like(w_head_t)
    return jnp.concatenate(
        [
            jnp.concatenate([w_head_t, blank], axis=1),
            jnp.concatenate([blank, w_head_t], axis=1),
        ],
        axis=0,
    )


def encode(values):
    size = jnp.log(1.0 + jnp.abs(values) * code_gain) * code_steps + 0.5
    return jnp.where(values < 0.0, -size, size).astype(jnp.int32)


def decode(codes):
    codes = codes.astype(f32)
    size = (jnp.exp(jnp.abs(codes) * (1.0 / code_steps)) - 1.0) * (1.0 / code_gain)
    return jnp.where(codes < 0.0, -size, size)


def normalize(values):
    centred = values - jnp.mean(values, axis=-1, keepdims=True)
    variance = jnp.mean(centred * centred, axis=-1, keepdims=True)
    inv_std = lax.rsqrt(variance + epsilon)
    return (centred * inv_std, inv_std)


def send_kernel(pair_ref, w_in_ref, w_out_ref, w_head_t_ref, send_ref, rows_ref):
    n_row = send_ref.shape[0]
    span = send_ref.shape[1]
    channels = pair_ref.shape[-1]
    values = pair_ref[...].reshape(-1, channels).astype(f32)
    half = values.shape[0] // CYCLES
    x_hat, _ = normalize(values)
    hidden = jnp.maximum(dot(x_hat.astype(bf16), w_in_ref[...]), 0.0).astype(bf16)
    residual = (values + dot(hidden, w_out_ref[...])).astype(bf16)
    wide = jnp.concatenate([residual[:half], residual[half:]], axis=1)
    rows_ref[...] = encode(dot_t(wide, widen(w_head_t_ref[...])))
    for r in range(n_row):
        send_ref[r] = rows_ref[pl.ds(r, span, stride=n_row), :].astype(jnp.int16)


def prepare_kernel(
    pair_ref,
    bins_ref,
    w_in_ref,
    w_out_ref,
    w_head_t_ref,
    hidden_ref,
    normed_t_ref,
    residual_t_ref,
    x_hat_ref,
    inv_ref,
    logits_ref,
    bins_wide_ref,
    values_ref,
):
    channels = pair_ref.shape[-1]
    n_row = pair_ref.shape[2] // CYCLES
    count = pair_ref.shape[1]
    for a in range(CYCLES):
        for b in range(CYCLES):
            values_ref[a, :, b] = pair_ref[b, :, a * n_row : (a + 1) * n_row, :].astype(f32)
    values = values_ref[...].reshape(-1, channels)
    half = values.shape[0] // CYCLES
    x_hat, inv_std = normalize(values)
    normed = x_hat.astype(bf16)
    hidden = jnp.maximum(dot(normed, w_in_ref[...]), 0.0).astype(bf16)
    residual = (values + dot(hidden, w_out_ref[...])).astype(bf16)
    hidden_ref[...] = hidden
    normed_t_ref[...] = normed.T
    residual_t_ref[...] = residual.T
    x_hat_ref[...] = x_hat
    inv_ref[...] = jnp.broadcast_to(inv_std, x_hat.shape)
    logits_ref[...] = dot_t(
        jnp.concatenate([residual[:half], residual[half:]], axis=1), widen(w_head_t_ref[...])
    )
    columns = bins_ref.shape[-1]
    row_of = lax.broadcasted_iota(jnp.int32, (1, n_row, columns), 1)
    column_of = lax.broadcasted_iota(jnp.int32, (1, n_row, columns), 2)
    own = column_of % n_row == row_of
    lane = lax.broadcasted_iota(jnp.int32, (columns, channels), 1)
    source = lax.broadcasted_iota(jnp.int32, (columns, channels), 0)
    spread = (lane // (channels // CYCLES) == source // n_row).astype(f32).astype(bf16)
    for b in range(CYCLES):
        bins = bins_ref[b].astype(f32)
        picked = jnp.where(own, jnp.broadcast_to(bins[:, None, :], (count, n_row, columns)), 0.0)
        wide = dot(picked.reshape(count * n_row, columns).astype(bf16), spread)
        bins_wide_ref[:, b] = wide.astype(bf16).reshape(count, n_row, channels)


def pair_gradient(d_logit, w_head_wide):
    wide = dot(d_logit, w_head_wide)
    channels = wide.shape[1] // CYCLES
    return jnp.concatenate([wide[:, :channels], wide[:, channels:]], axis=0)


def hidden_gradient(d_update, hidden, w_out):
    back = dot_t(d_update, w_out).astype(bf16)
    return jnp.where(hidden > 0, back, jnp.zeros_like(back))


def weights_kernel(
    recv_ref,
    hidden_ref,
    normed_t_ref,
    residual_t_ref,
    logits_ref,
    bins_wide_ref,
    w_out_ref,
    w_head_t_ref,
    d_logit_ref,
    part_ref,
    rows_ref,
    in_ref,
    out_ref,
    head_ref,
):
    step = pl.program_id(0)
    n_row = recv_ref.shape[0]
    span = recv_ref.shape[1]
    channels = logits_ref.shape[-1]
    bins_count = channels // CYCLES
    half = span * n_row

    for r in range(n_row):
        rows_ref[pl.ds(r, span, stride=n_row), :] = decode(recv_ref[r])
    sym = logits_ref[...] + rows_ref[...]
    lane = lax.broadcasted_iota(jnp.int32, (1, channels), 1)
    left = lane < bins_count
    low = jnp.max(jnp.where(left, sym, -jnp.inf), axis=-1, keepdims=True)
    high = jnp.max(jnp.where(left, -jnp.inf, sym), axis=-1, keepdims=True)
    grown = jnp.exp(sym - jnp.where(left, low, high))
    low = jnp.sum(jnp.where(left, grown, 0.0), axis=-1, keepdims=True)
    high = jnp.sum(jnp.where(left, 0.0, grown), axis=-1, keepdims=True)
    probability = grown / jnp.where(left, low, high)
    own_bin = (lane % bins_count).astype(f32)
    bins = bins_wide_ref[...].reshape(half, channels).astype(f32)
    d_sym = probability - jnp.where(bins == own_bin, 1.0, 0.0)
    d_logit = (d_sym + d_sym).astype(bf16)
    d_logit_ref[...] = d_logit

    d_update = pair_gradient(d_logit, widen(w_head_t_ref[...])).astype(bf16)
    hidden = hidden_ref[...]
    d_hidden = hidden_gradient(d_update, hidden, w_out_ref[...])
    g_in = dot(normed_t_ref[...], d_hidden)
    g_out = dot(d_update.T, hidden)
    g_head = jnp.where(
        left,
        dot(residual_t_ref[:, :half], d_logit),
        dot(residual_t_ref[:, half:], d_logit),
    )

    @pl.when(step == 0)
    def _():
        in_ref[...] = g_in
        out_ref[...] = g_out
        head_ref[...] = g_head

    @pl.when(step > 0)
    def _():
        in_ref[...] += g_in
        out_ref[...] += g_out
        head_ref[...] += g_head

    @pl.when(step == STEPS - 1)
    def _():
        rows = channels // n_row
        tiles = in_ref.shape[1] // channels
        long = tiles * rows
        total_out = out_ref[...].T
        for r in range(n_row):
            mine = in_ref[r * rows : (r + 1) * rows, :]
            part_ref[r, 0:long, :] = jnp.concatenate(
                [mine[:, t * channels : (t + 1) * channels] for t in range(tiles)], axis=0
            ).astype(bf16)
            part_ref[r, long : 2 * long, :] = total_out[r * long : (r + 1) * long, :].astype(bf16)
            mine = head_ref[r * rows : (r + 1) * rows, :]
            part_ref[r, 2 * long : 2 * long + 2 * rows, :] = jnp.concatenate(
                [mine, jnp.zeros_like(mine)], axis=0
            ).astype(bf16)


def pair_kernel(
    d_logit_ref, hidden_ref, x_hat_ref, inv_ref, w_in_ref, w_out_ref, w_head_t_ref, grad_ref
):
    channels = grad_ref.shape[-1]
    count = grad_ref.shape[1]
    n_row = grad_ref.shape[2] // CYCLES
    d_resid = pair_gradient(d_logit_ref[...], widen(w_head_t_ref[...]))
    d_hidden = hidden_gradient(d_resid.astype(bf16), hidden_ref[...], w_out_ref[...])
    d_normed = dot_t(d_hidden, w_in_ref[...])
    x_hat = x_hat_ref[...]
    first_mean = jnp.mean(d_normed, axis=-1, keepdims=True)
    second_mean = jnp.mean(d_normed * x_hat, axis=-1, keepdims=True)
    d_pair = d_resid + inv_ref[...] * (d_normed - first_mean - x_hat * second_mean)
    d_pair = d_pair.astype(bf16).reshape(CYCLES, count, CYCLES, n_row, channels)
    for a in range(CYCLES):
        for b in range(CYCLES):
            grad_ref[b, :, a * n_row : (a + 1) * n_row, :] = d_pair[a, :, b]


def lanes_of(shape, axis):
    return lax.broadcasted_iota(jnp.int32, shape, axis)


def fold_matrix(width, kind):
    shape = (128, 128)
    return (lanes_of(shape, 0) % width == lanes_of(shape, 1) % width).astype(f32).astype(kind)


def middle_kernel(recv_ref, send_ref):
    n_col = send_ref.shape[0] // 4
    total = recv_ref[0].astype(f32)
    for r in range(1, recv_ref.shape[0]):
        total = total + recv_ref[r].astype(f32)
    rows, tiles = 8, 4
    mine = total[: rows * tiles]
    group = lanes_of((1, rows, 128), 2) // 16 == lanes_of((1, rows, 128), 1)
    spread = jnp.where(group, jnp.broadcast_to(mine[:, None, :], (rows * tiles, rows, 128)), 0.0)
    folded = dot(spread.reshape(-1, 128).astype(bf16), fold_matrix(16, bf16))
    folded = folded.reshape(tiles, rows, rows, 128)
    slot = lanes_of((1, rows, 1, 128), 3) // 16 == lanes_of((1, rows, 1, 128), 1)
    part_in = jnp.sum(jnp.where(slot, folded, 0.0), axis=1).reshape(n_col, 128)
    mine = total[32:64]
    group = lanes_of((1, n_col, 128), 2) // 4 == lanes_of((1, n_col, 128), 1)
    spread = jnp.where(group, jnp.broadcast_to(mine[:, None, :], (32, n_col, 128)), 0.0)
    folded = dot(spread.reshape(-1, 128).astype(bf16), fold_matrix(4, bf16))
    folded = folded.reshape(32, n_col, 128)
    slot = lanes_of((32, 1, 128), 2) // 4 == lanes_of((32, 1, 128), 0)
    part_out = jnp.sum(jnp.where(slot, folded, 0.0), axis=0)
    mine = total[64:72]
    group = lanes_of((1, n_col, 128), 2) % 64 // 2 == lanes_of((1, n_col, 128), 1)
    spread = jnp.where(group, jnp.broadcast_to(mine[:, None, :], (8, n_col, 128)), 0.0)
    folded = dot(spread.reshape(-1, 128).astype(bf16), fold_matrix(2, bf16))
    folded = folded.reshape(8, n_col, 128)
    slot = lanes_of((8, 1, 128), 2) // 2 == lanes_of((8, 1, 128), 0)
    part_head = jnp.sum(jnp.where(slot, folded, 0.0), axis=0)
    send_ref[pl.ds(0, n_col, stride=4), :] = part_in
    send_ref[pl.ds(1, n_col, stride=4), :] = part_out
    send_ref[pl.ds(2, n_col, stride=4), :] = part_head
    send_ref[pl.ds(3, n_col, stride=4), :] = jnp.zeros_like(part_head)


def final_kernel(scale, recv_ref, in_ref, out_t_ref, head_t_ref):
    total = recv_ref[0:8, :]
    for c in range(1, recv_ref.shape[0] // 8):
        total = total + recv_ref[c * 8 : (c + 1) * 8, :]
    total = (total[0:4] + total[4:8]) * scale

    def unfold(row, out, row_of, column_of):
        count, width = out.shape
        shape = (count, 128)
        picked = jnp.where(
            row_of(lanes_of(shape, 1)) == lanes_of(shape, 0), jnp.broadcast_to(row, shape), 0.0
        )
        shape = (128, width)
        fold = (column_of(lanes_of(shape, 0)) == lanes_of(shape, 1)).astype(f32)
        out[...] = jnp.dot(
            picked, fold, precision=lax.Precision.HIGHEST, preferred_element_type=f32
        )

    unfold(total[0:1], in_ref, lambda lane: lane // 16, lambda lane: lane % 16)
    unfold(total[1:2], out_t_ref, lambda lane: lane % 4, lambda lane: lane // 4)
    unfold(total[2:3], head_t_ref, lambda lane: lane % 2, lambda lane: lane // 2)


def whole(array):
    return pl.BlockSpec(array.shape, lambda g: (0,) * array.ndim)


def params():
    return pltpu.CompilerParams(vmem_limit_bytes=62 * 1024 * 1024)


def shards(pair_rep, true_bins, w_in, w_out, w_head):
    row_count, col_count, channels = pair_rep.shape
    n_row = lax.axis_size("row")
    n_col = lax.axis_size("col")
    hidden_count = w_in.shape[1]
    bins_count = w_head.shape[1]
    pairs = row_count * col_count
    cycled = pair_rep.reshape(CYCLES, n_col, col_count, channels)
    bins = true_bins.reshape(CYCLES, n_col, col_count)
    w_head_t = w_head.T
    count = n_col // STEPS
    span = CYCLES * count
    block = pairs // STEPS
    half = block // CYCLES
    pair_spec = pl.BlockSpec((CYCLES, count, col_count, channels), lambda g: (0, g, 0, 0))
    send_spec = pl.BlockSpec((n_row, span, channels), lambda g: (0, g, 0))

    send = pl.pallas_call(
        send_kernel,
        grid=(STEPS,),
        in_specs=[pair_spec, whole(w_in), whole(w_out), whole(w_head_t)],
        out_specs=send_spec,
        out_shape=jax.ShapeDtypeStruct((n_row, CYCLES * n_col, channels), jnp.int16),
        scratch_shapes=[pltpu.VMEM((half, channels), jnp.int32)],
        compiler_params=params(),
        name="forward",
    )(cycled, w_in, w_out, w_head_t)

    recv = lax.all_to_all(
        send.reshape(n_row * n_col, CYCLES, channels),
        ("row", "col"),
        split_axis=0,
        concat_axis=0,
        tiled=True,
    ).reshape(n_row, CYCLES * n_col, channels)

    def rows_spec(width):
        return pl.BlockSpec((block, width), lambda g: (g, 0))

    def columns_spec(height):
        return pl.BlockSpec((height, block), lambda g: (0, g))

    logits_spec = pl.BlockSpec((half, channels), lambda g: (g, 0))
    bins_spec = pl.BlockSpec((count, CYCLES, n_row, channels), lambda g: (g, 0, 0, 0))
    kept_specs = [
        rows_spec(hidden_count),
        columns_spec(channels),
        columns_spec(channels),
        rows_spec(channels),
        rows_spec(channels),
        logits_spec,
        bins_spec,
    ]
    hidden, normed_t, residual_t, x_hat, inv_std, logits, bins_wide = pl.pallas_call(
        prepare_kernel,
        grid=(STEPS,),
        in_specs=[
            pair_spec,
            pl.BlockSpec((CYCLES, count, col_count), lambda g: (0, g, 0)),
            whole(w_in),
            whole(w_out),
            whole(w_head_t),
        ],
        out_specs=kept_specs,
        out_shape=[
            jax.ShapeDtypeStruct((pairs, hidden_count), bf16),
            jax.ShapeDtypeStruct((channels, pairs), bf16),
            jax.ShapeDtypeStruct((channels, pairs), bf16),
            jax.ShapeDtypeStruct((pairs, channels), f32),
            jax.ShapeDtypeStruct((pairs, channels), f32),
            jax.ShapeDtypeStruct((pairs // CYCLES, channels), f32),
            jax.ShapeDtypeStruct((n_col, CYCLES, n_row, channels), bf16),
        ],
        scratch_shapes=[pltpu.VMEM((CYCLES, count, CYCLES, n_row, channels), f32)],
        compiler_params=params(),
        cost_estimate=pl.CostEstimate(
            flops=2 * pairs * 2 * channels * hidden_count, bytes_accessed=8 * 2**20, transcendentals=0
        ),
        name="prepare",
    )(cycled, bins, w_in, w_out, w_head_t)

    part_rows = 2 * (hidden_count // n_row) + 16
    d_logit, part = pl.pallas_call(
        weights_kernel,
        grid=(STEPS,),
        in_specs=[
            send_spec,
            rows_spec(hidden_count),
            columns_spec(channels),
            columns_spec(channels),
            logits_spec,
            bins_spec,
            whole(w_out),
            whole(w_head_t),
        ],
        out_specs=[
            logits_spec,
            pl.BlockSpec((n_row, part_rows, channels), lambda g: (0, 0, 0)),
        ],
        out_shape=[
            jax.ShapeDtypeStruct((pairs // CYCLES, channels), bf16),
            jax.ShapeDtypeStruct((n_row, part_rows, channels), bf16),
        ],
        scratch_shapes=[
            pltpu.VMEM((half, channels), f32),
            pltpu.VMEM((channels, hidden_count), f32),
            pltpu.VMEM((channels, hidden_count), f32),
            pltpu.VMEM((channels, channels), f32),
        ],
        compiler_params=params(),
        name="weights",
    )(recv, hidden, normed_t, residual_t, logits, bins_wide, w_out, w_head_t)

    part = lax.all_to_all(part, "row", split_axis=0, concat_axis=0, tiled=True)

    d_pair = pl.pallas_call(
        pair_kernel,
        grid=(STEPS,),
        in_specs=[
            logits_spec,
            rows_spec(hidden_count),
            rows_spec(channels),
            rows_spec(channels),
            whole(w_in),
            whole(w_out),
            whole(w_head_t),
        ],
        out_specs=pair_spec,
        out_shape=jax.ShapeDtypeStruct(cycled.shape, bf16),
        compiler_params=params(),
        cost_estimate=pl.CostEstimate(
            flops=2 * pairs * 2 * channels * hidden_count, bytes_accessed=5 * 2**20, transcendentals=0
        ),
        name="pair",
    )(d_logit, hidden, x_hat, inv_std, w_in, w_out, w_head_t)

    share = pl.pallas_call(
        middle_kernel,
        out_shape=jax.ShapeDtypeStruct((4 * n_col, channels), f32),
        compiler_params=params(),
        name="sum_rows",
    )(part)
    share = lax.all_to_all(
        share.reshape(n_col, 4, channels), "col", split_axis=0, concat_axis=0, tiled=True
    ).reshape(4 * n_col, channels)
    grad_in, grad_out_t, grad_head_t = pl.pallas_call(
        functools.partial(final_kernel, 1.0 / (row_count * n_row)),
        out_shape=[
            jax.ShapeDtypeStruct((channels // n_row, hidden_count // n_col), f32),
            jax.ShapeDtypeStruct((channels // n_col, hidden_count // n_row), f32),
            jax.ShapeDtypeStruct((bins_count // n_col, channels // n_row), f32),
        ],
        compiler_params=params(),
        name="sum_columns",
    )(share)
    return (
        d_pair.reshape(row_count, col_count, channels),
        grad_in,
        grad_out_t.T,
        grad_head_t.T,
    )


def solution(mesh):
    placed = (P("row", "col", None), P("row", "col"), P(), P(), P())
    return jax.shard_map(
        shards,
        mesh=mesh,
        in_specs=placed,
        out_specs=(P("row", "col", None), P("row", "col"), P("row", "col"), P("row", "col")),
        check_vma=False,
    )
```

```python
import functools

import jax
import jax.numpy as jnp
from jax import lax
from jax.experimental import pallas as pl
from jax.experimental.pallas import tpu as pltpu
from jax.sharding import PartitionSpec as P

epsilon = 1e-05
f32 = jnp.float32
bf16 = jnp.bfloat16

code_gain = 16.0
code_steps = 1850.0

CYCLES = 2
FORWARD_STEPS = 1
STEPS = 2


def dot(first, second):
    return jnp.dot(first, second, preferred_element_type=f32)


def dot_t(first, second):
    return lax.dot_general(first, second, (((1,), (1,)), ((), ())), preferred_element_type=f32)


def widen(w_head_t):
    blank = jnp.zeros_like(w_head_t)
    return jnp.concatenate(
        [
            jnp.concatenate([w_head_t, blank], axis=1),
            jnp.concatenate([blank, w_head_t], axis=1),
        ],
        axis=0,
    )


def encode(values):
    size = jnp.log(1.0 + jnp.abs(values) * code_gain) * code_steps + 0.5
    return jnp.where(values < 0.0, -size, size).astype(jnp.int32)


def decode(codes):
    codes = codes.astype(f32)
    size = (jnp.exp(jnp.abs(codes) * (1.0 / code_steps)) - 1.0) * (1.0 / code_gain)
    return jnp.where(codes < 0.0, -size, size)


def normalize(values):
    centred = values - jnp.mean(values, axis=-1, keepdims=True)
    variance = jnp.mean(centred * centred, axis=-1, keepdims=True)
    inv_std = lax.rsqrt(variance + epsilon)
    return (centred * inv_std, inv_std)


def send_kernel(pair_ref, w_in_ref, w_out_ref, w_head_t_ref, send_ref, rows_ref):
    n_row = send_ref.shape[0]
    span = send_ref.shape[1]
    channels = pair_ref.shape[-1]
    values = pair_ref[...].reshape(-1, channels).astype(f32)
    half = values.shape[0] // CYCLES
    x_hat, _ = normalize(values)
    hidden = jnp.maximum(dot(x_hat.astype(bf16), w_in_ref[...]), 0.0).astype(bf16)
    residual = (values + dot(hidden, w_out_ref[...])).astype(bf16)
    wide = jnp.concatenate([residual[:half], residual[half:]], axis=1)
    rows_ref[...] = encode(dot_t(wide, widen(w_head_t_ref[...])))
    for r in range(n_row):
        send_ref[r] = rows_ref[pl.ds(r, span, stride=n_row), :].astype(jnp.int16)


def prepare_kernel(
    pair_ref,
    bins_ref,
    w_in_ref,
    w_out_ref,
    w_head_t_ref,
    hidden_ref,
    normed_t_ref,
    residual_t_ref,
    x_hat_ref,
    inv_ref,
    logits_ref,
    bins_wide_ref,
    values_ref,
):
    channels = pair_ref.shape[-1]
    n_row = pair_ref.shape[2] // CYCLES
    count = pair_ref.shape[1]
    for a in range(CYCLES):
        for b in range(CYCLES):
            values_ref[a, :, b] = pair_ref[b, :, a * n_row : (a + 1) * n_row, :].astype(f32)
    values = values_ref[...].reshape(-1, channels)
    half = values.shape[0] // CYCLES
    x_hat, inv_std = normalize(values)
    normed = x_hat.astype(bf16)
    hidden = jnp.maximum(dot(normed, w_in_ref[...]), 0.0).astype(bf16)
    residual = (values + dot(hidden, w_out_ref[...])).astype(bf16)
    hidden_ref[...] = hidden
    normed_t_ref[...] = normed.T
    residual_t_ref[...] = residual.T
    x_hat_ref[...] = x_hat
    inv_ref[...] = jnp.broadcast_to(inv_std, x_hat.shape)
    logits_ref[...] = dot_t(
        jnp.concatenate([residual[:half], residual[half:]], axis=1), widen(w_head_t_ref[...])
    )
    columns = bins_ref.shape[-1]
    row_of = lax.broadcasted_iota(jnp.int32, (1, n_row, columns), 1)
    column_of = lax.broadcasted_iota(jnp.int32, (1, n_row, columns), 2)
    own = column_of % n_row == row_of
    lane = lax.broadcasted_iota(jnp.int32, (columns, channels), 1)
    source = lax.broadcasted_iota(jnp.int32, (columns, channels), 0)
    spread = (lane // (channels // CYCLES) == source // n_row).astype(f32).astype(bf16)
    for b in range(CYCLES):
        bins = bins_ref[b].astype(f32)
        picked = jnp.where(own, jnp.broadcast_to(bins[:, None, :], (count, n_row, columns)), 0.0)
        wide = dot(picked.reshape(count * n_row, columns).astype(bf16), spread)
        bins_wide_ref[:, b] = wide.astype(bf16).reshape(count, n_row, channels)


def pair_gradient(d_logit, w_head_wide):
    wide = dot(d_logit, w_head_wide)
    channels = wide.shape[1] // CYCLES
    return jnp.concatenate([wide[:, :channels], wide[:, channels:]], axis=0)


def hidden_gradient(d_update, hidden, w_out):
    back = dot_t(d_update, w_out).astype(bf16)
    return jnp.where(hidden > 0, back, jnp.zeros_like(back))


def weights_kernel(
    recv_ref,
    hidden_ref,
    normed_t_ref,
    residual_t_ref,
    logits_ref,
    bins_wide_ref,
    w_out_ref,
    w_head_t_ref,
    d_logit_ref,
    part_ref,
    rows_ref,
    in_ref,
    out_ref,
    head_ref,
):
    step = pl.program_id(0)
    n_row = recv_ref.shape[0]
    span = recv_ref.shape[1]
    channels = logits_ref.shape[-1]
    bins_count = channels // CYCLES
    half = span * n_row

    for r in range(n_row):
        rows_ref[pl.ds(r, span, stride=n_row), :] = decode(recv_ref[r])
    sym = logits_ref[...] + rows_ref[...]
    lane = lax.broadcasted_iota(jnp.int32, (1, channels), 1)
    left = lane < bins_count
    low = jnp.max(jnp.where(left, sym, -jnp.inf), axis=-1, keepdims=True)
    high = jnp.max(jnp.where(left, -jnp.inf, sym), axis=-1, keepdims=True)
    grown = jnp.exp(sym - jnp.where(left, low, high))
    low = jnp.sum(jnp.where(left, grown, 0.0), axis=-1, keepdims=True)
    high = jnp.sum(jnp.where(left, 0.0, grown), axis=-1, keepdims=True)
    probability = grown / jnp.where(left, low, high)
    own_bin = (lane % bins_count).astype(f32)
    bins = bins_wide_ref[...].reshape(half, channels).astype(f32)
    d_sym = probability - jnp.where(bins == own_bin, 1.0, 0.0)
    d_logit = (d_sym + d_sym).astype(bf16)
    d_logit_ref[...] = d_logit

    d_update = pair_gradient(d_logit, widen(w_head_t_ref[...])).astype(bf16)
    hidden = hidden_ref[...]
    d_hidden = hidden_gradient(d_update, hidden, w_out_ref[...])
    g_in = dot(normed_t_ref[...], d_hidden)
    g_out = dot(d_update.T, hidden)
    g_head = jnp.where(
        left,
        dot(residual_t_ref[:, :half], d_logit),
        dot(residual_t_ref[:, half:], d_logit),
    )

    @pl.when(step == 0)
    def _():
        in_ref[...] = g_in
        out_ref[...] = g_out
        head_ref[...] = g_head

    @pl.when(step > 0)
    def _():
        in_ref[...] += g_in
        out_ref[...] += g_out
        head_ref[...] += g_head

    @pl.when(step == pl.num_programs(0) - 1)
    def _():
        rows = channels // n_row
        tiles = in_ref.shape[1] // channels
        long = tiles * rows
        total_out = out_ref[...].T
        for r in range(n_row):
            mine = in_ref[r * rows : (r + 1) * rows, :]
            part_ref[r, 0:long, :] = jnp.concatenate(
                [mine[:, t * channels : (t + 1) * channels] for t in range(tiles)], axis=0
            ).astype(bf16)
            part_ref[r, long : 2 * long, :] = total_out[r * long : (r + 1) * long, :].astype(bf16)
            mine = head_ref[r * rows : (r + 1) * rows, :]
            part_ref[r, 2 * long : 2 * long + 2 * rows, :] = jnp.concatenate(
                [mine, jnp.zeros_like(mine)], axis=0
            ).astype(bf16)


def pair_kernel(
    d_logit_ref, hidden_ref, x_hat_ref, inv_ref, w_in_ref, w_out_ref, w_head_t_ref, grad_ref
):
    channels = grad_ref.shape[-1]
    count = grad_ref.shape[1]
    n_row = grad_ref.shape[2] // CYCLES
    d_resid = pair_gradient(d_logit_ref[...], widen(w_head_t_ref[...]))
    d_hidden = hidden_gradient(d_resid.astype(bf16), hidden_ref[...], w_out_ref[...])
    d_normed = dot_t(d_hidden, w_in_ref[...])
    x_hat = x_hat_ref[...]
    first_mean = jnp.mean(d_normed, axis=-1, keepdims=True)
    second_mean = jnp.mean(d_normed * x_hat, axis=-1, keepdims=True)
    d_pair = d_resid + inv_ref[...] * (d_normed - first_mean - x_hat * second_mean)
    d_pair = d_pair.astype(bf16).reshape(CYCLES, count, CYCLES, n_row, channels)
    for a in range(CYCLES):
        for b in range(CYCLES):
            grad_ref[b, :, a * n_row : (a + 1) * n_row, :] = d_pair[a, :, b]


def lanes_of(shape, axis):
    return lax.broadcasted_iota(jnp.int32, shape, axis)


def fold_matrix(width, kind):
    shape = (128, 128)
    return (lanes_of(shape, 0) % width == lanes_of(shape, 1) % width).astype(f32).astype(kind)


def middle_kernel(recv_ref, done_ref, send_ref, rows_ref):
    n_col = send_ref.shape[0] // 4
    total = recv_ref[0].astype(f32)
    for r in range(1, recv_ref.shape[0]):
        total = total + recv_ref[r].astype(f32)
    rows, tiles = 8, 4
    mine = total[: rows * tiles]
    group = lanes_of((1, rows, 128), 2) // 16 == lanes_of((1, rows, 128), 1)
    spread = jnp.where(group, jnp.broadcast_to(mine[:, None, :], (rows * tiles, rows, 128)), 0.0)
    folded = dot(spread.reshape(-1, 128).astype(bf16), fold_matrix(16, bf16))
    folded = folded.reshape(tiles, rows, rows, 128)
    slot = lanes_of((1, rows, 1, 128), 3) // 16 == (8 - lanes_of((1, rows, 1, 128), 1)) % 8
    part_in = jnp.sum(jnp.where(slot, folded, 0.0), axis=1).reshape(n_col, 128)
    send_ref[pl.ds(0, n_col, stride=4), :] = part_in
    rows_ref[...] = jnp.concatenate([total[32:64]] * 4, axis=0).T
    lane = lanes_of((1, 128), 1)
    part_out = rows_ref[pl.ds(0, n_col, stride=4), :]
    for j in range(1, 4):
        part_out = jnp.where(
            lane // 32 == 4 - j, rows_ref[pl.ds(j, n_col, stride=4), :], part_out
        )
    send_ref[pl.ds(1, n_col, stride=4), :] = part_out
    mine = total[64:72]
    mine = mine + pltpu.roll(mine, 64, 1)
    rows_ref[...] = jnp.concatenate([mine] * 16, axis=0).T
    part_head = jnp.where(
        lane // 8 == 15,
        rows_ref[pl.ds(1, n_col, stride=2), :],
        rows_ref[pl.ds(0, n_col, stride=2), :],
    )
    send_ref[pl.ds(2, n_col, stride=4), :] = part_head
    send_ref[pl.ds(3, n_col, stride=4), :] = jnp.zeros_like(part_head)


def final_kernel(scale, recv_ref, in_ref, out_t_ref, head_t_ref):
    total = recv_ref[0:8, :]
    for c in range(1, recv_ref.shape[0] // 8):
        total = total + recv_ref[c * 8 : (c + 1) * 8, :]
    total = (total[0:4] + total[4:8]) * scale

    def unfold(row, out):
        count, width = out.shape
        if width * 8 <= 128:
            spread = jnp.broadcast_to(row, (8, 128))
            spread = pltpu.roll(spread, 0, 1, stride=width, stride_axis=0)
        else:
            spread = jnp.concatenate(
                [pltpu.roll(row, i * width, 1) if i else row for i in range(count)], axis=0
            )
        out[...] = spread[:count, :width]

    unfold(total[0:1], in_ref)
    unfold(total[1:2], out_t_ref)
    unfold(total[2:3], head_t_ref)


def whole(array):
    return pl.BlockSpec(array.shape, lambda g: (0,) * array.ndim)


ROOM = 48 * 1024 * 1024


def whole_array(array):
    return pl.BlockSpec(array.shape, lambda: (0,) * array.ndim)


def params(limit=62 * 1024 * 1024):
    return pltpu.CompilerParams(vmem_limit_bytes=limit)


def in_hbm(array):
    return pltpu.with_memory_space_constraint(array, pltpu.HBM)


def forward_call(pair_rep, w_in, w_out, w_head_t, n_row, n_col):
    row_count, col_count, channels = pair_rep.shape
    count = n_col // FORWARD_STEPS
    return pl.pallas_call(
        send_kernel,
        grid=(FORWARD_STEPS,),
        in_specs=[
            pl.BlockSpec((CYCLES, count, col_count, channels), lambda g: (0, g, 0, 0)),
            whole(w_in),
            whole(w_out),
            whole(w_head_t),
        ],
        out_specs=pl.BlockSpec((n_row, CYCLES * count, channels), lambda g: (0, g, 0)),
        out_shape=jax.ShapeDtypeStruct((n_row, CYCLES * n_col, channels), jnp.int16),
        scratch_shapes=[pltpu.VMEM((CYCLES * count * n_row, channels), jnp.int32)],
        compiler_params=params(),
        name="forward",
    )(pair_rep.reshape(CYCLES, n_col, col_count, channels), w_in, w_out, w_head_t)


def rows_spec(block, width):
    return pl.BlockSpec((block, width), lambda g: (g, 0))


def columns_spec(height, block):
    return pl.BlockSpec((height, block), lambda g: (0, g))


def prepare_call(pair_rep, true_bins, w_in, w_out, w_head_t, n_row, n_col):
    row_count, col_count, channels = pair_rep.shape
    pairs = row_count * col_count
    hidden_count = w_in.shape[1]
    count = n_col // STEPS
    block = pairs // STEPS
    half = block // CYCLES
    return pl.pallas_call(
        prepare_kernel,
        grid=(STEPS,),
        in_specs=[
            pl.BlockSpec((CYCLES, count, col_count, channels), lambda g: (0, g, 0, 0)),
            pl.BlockSpec((CYCLES, count, col_count), lambda g: (0, g, 0)),
            whole(w_in),
            whole(w_out),
            whole(w_head_t),
        ],
        out_specs=[
            rows_spec(block, hidden_count),
            columns_spec(channels, block),
            columns_spec(channels, block),
            rows_spec(block, channels),
            rows_spec(block, channels),
            rows_spec(half, channels),
            pl.BlockSpec((count, CYCLES, n_row, channels), lambda g: (g, 0, 0, 0)),
        ],
        out_shape=[
            jax.ShapeDtypeStruct((pairs, hidden_count), bf16),
            jax.ShapeDtypeStruct((channels, pairs), bf16),
            jax.ShapeDtypeStruct((channels, pairs), bf16),
            jax.ShapeDtypeStruct((pairs, channels), f32),
            jax.ShapeDtypeStruct((pairs, channels), f32),
            jax.ShapeDtypeStruct((pairs // CYCLES, channels), f32),
            jax.ShapeDtypeStruct((n_col, CYCLES, n_row, channels), bf16),
        ],
        scratch_shapes=[pltpu.VMEM((CYCLES, count, CYCLES, n_row, channels), f32)],
        compiler_params=params(),
        cost_estimate=pl.CostEstimate(
            flops=2 * pairs * 2 * channels * hidden_count, bytes_accessed=8 * 2**20, transcendentals=0
        ),
        name="prepare",
    )(
        pair_rep.reshape(CYCLES, n_col, col_count, channels),
        true_bins.reshape(CYCLES, n_col, col_count),
        w_in,
        w_out,
        w_head_t,
    )


def weights_call(recv, hidden, normed_t, residual_t, logits, bins_wide, w_out, w_head_t):
    n_row, span, channels = recv.shape
    pairs, hidden_count = hidden.shape
    count = span // CYCLES // STEPS
    block = pairs // STEPS
    half = block // CYCLES
    part_rows = 2 * (hidden_count // n_row) + 16
    kept = [in_hbm(x) for x in (hidden, normed_t, residual_t, logits, bins_wide, w_out, w_head_t)]
    return pl.pallas_call(
        weights_kernel,
        grid=(STEPS,),
        in_specs=[
            pl.BlockSpec((n_row, CYCLES * count, channels), lambda g: (0, g, 0)),
            rows_spec(block, hidden_count),
            columns_spec(channels, block),
            columns_spec(channels, block),
            rows_spec(half, channels),
            pl.BlockSpec((count, CYCLES, n_row, channels), lambda g: (g, 0, 0, 0)),
            whole(w_out),
            whole(w_head_t),
        ],
        out_specs=[
            rows_spec(half, channels),
            pl.BlockSpec((n_row, part_rows, channels), lambda g: (0, 0, 0)),
        ],
        out_shape=[
            jax.ShapeDtypeStruct((pairs // CYCLES, channels), bf16),
            jax.ShapeDtypeStruct((n_row, part_rows, channels), bf16),
        ],
        scratch_shapes=[
            pltpu.VMEM((half, channels), f32),
            pltpu.VMEM((channels, hidden_count), f32),
            pltpu.VMEM((channels, hidden_count), f32),
            pltpu.VMEM((channels, channels), f32),
        ],
        compiler_params=params(ROOM),
        name="weights",
    )(recv, *kept)


def pair_call(d_logit, hidden, x_hat, inv_std, w_in, w_out, w_head_t, shape, n_row, n_col):
    row_count, col_count, channels = shape
    pairs, hidden_count = hidden.shape
    count = n_col // STEPS
    block = pairs // STEPS
    return pl.pallas_call(
        pair_kernel,
        grid=(STEPS,),
        in_specs=[
            rows_spec(block // CYCLES, channels),
            rows_spec(block, hidden_count),
            rows_spec(block, channels),
            rows_spec(block, channels),
            whole(w_in),
            whole(w_out),
            whole(w_head_t),
        ],
        out_specs=pl.BlockSpec((CYCLES, count, col_count, channels), lambda g: (0, g, 0, 0)),
        out_shape=jax.ShapeDtypeStruct((CYCLES, n_col, col_count, channels), bf16),
        compiler_params=params(),
        cost_estimate=pl.CostEstimate(
            flops=2 * pairs * 2 * channels * hidden_count, bytes_accessed=5 * 2**20, transcendentals=0
        ),
        name="pair",
    )(in_hbm(d_logit), hidden, x_hat, inv_std, w_in, w_out, w_head_t)


def middle_call(part, done, n_col):
    return pl.pallas_call(
        middle_kernel,
        in_specs=[whole_array(part), pl.BlockSpec(memory_space=pl.ANY)],
        out_shape=jax.ShapeDtypeStruct((4 * n_col, part.shape[-1]), f32),
        scratch_shapes=[pltpu.VMEM((128, 128), f32)],
        compiler_params=params(ROOM),
        name="sum_rows",
    )(part, in_hbm(done))


def final_call(share, scale, shapes):
    return pl.pallas_call(
        functools.partial(final_kernel, scale),
        out_shape=[jax.ShapeDtypeStruct(shape, f32) for shape in shapes],
        compiler_params=params(ROOM),
        name="sum_columns",
    )(share)


def shards(pair_rep, true_bins, w_in, w_out, w_head):
    row_count, col_count, channels = pair_rep.shape
    n_row = lax.axis_size("row")
    n_col = lax.axis_size("col")
    hidden_count = w_in.shape[1]
    bins_count = w_head.shape[1]
    w_head_t = w_head.T

    send = forward_call(pair_rep, w_in, w_out, w_head_t, n_row, n_col)
    recv = lax.all_to_all(
        send.reshape(n_row * n_col, CYCLES, channels),
        ("row", "col"),
        split_axis=0,
        concat_axis=0,
        tiled=True,
    ).reshape(n_row, CYCLES * n_col, channels)
    hidden, normed_t, residual_t, x_hat, inv_std, logits, bins_wide = prepare_call(
        pair_rep, true_bins, w_in, w_out, w_head_t, n_row, n_col
    )
    d_logit, part = weights_call(
        recv, hidden, normed_t, residual_t, logits, bins_wide, w_out, w_head_t
    )
    part = lax.all_to_all(part, "row", split_axis=0, concat_axis=0, tiled=True)
    d_pair = pair_call(
        d_logit, hidden, x_hat, inv_std, w_in, w_out, w_head_t, pair_rep.shape, n_row, n_col
    )
    share = middle_call(part, d_pair, n_col)
    share = lax.all_to_all(
        share.reshape(n_col, 4, channels), "col", split_axis=0, concat_axis=0, tiled=True
    ).reshape(4 * n_col, channels)
    grad_in, grad_out_t, grad_head_t = final_call(
        share,
        1.0 / (row_count * n_row),
        [
            (channels // n_row, hidden_count // n_col),
            (channels // n_col, hidden_count // n_row),
            (bins_count // n_col, channels // n_row),
        ],
    )
    return (
        d_pair.reshape(row_count, col_count, channels),
        grad_in,
        grad_out_t.T,
        grad_head_t.T,
    )


def solution(mesh):
    placed = (P("row", "col", None), P("row", "col"), P(), P(), P())
    return jax.shard_map(
        shards,
        mesh=mesh,
        in_specs=placed,
        out_specs=(P("row", "col", None), P("row", "col"), P("row", "col"), P("row", "col")),
        check_vma=False,
    )
```

```python
import functools

import jax
import jax.numpy as jnp
from jax import lax
from jax.experimental import pallas as pl
from jax.experimental.pallas import tpu as pltpu
from jax.sharding import PartitionSpec as P

epsilon = 1e-05
f32 = jnp.float32
bf16 = jnp.bfloat16

code_gain = 16.0
code_steps = 1850.0

CYCLES = 2


def dot(first, second):
    return jnp.dot(first, second, preferred_element_type=f32)


def dot_t(first, second):
    return lax.dot_general(first, second, (((1,), (1,)), ((), ())), preferred_element_type=f32)


def widen(w_head_t):
    blank = jnp.zeros_like(w_head_t)
    return jnp.concatenate(
        [
            jnp.concatenate([w_head_t, blank], axis=1),
            jnp.concatenate([blank, w_head_t], axis=1),
        ],
        axis=0,
    )


def encode(values):
    size = jnp.log(1.0 + jnp.abs(values) * code_gain) * code_steps + 0.5
    return jnp.where(values < 0.0, -size, size).astype(jnp.int32)


def decode(codes):
    codes = codes.astype(f32)
    size = (jnp.exp(jnp.abs(codes) * (1.0 / code_steps)) - 1.0) * (1.0 / code_gain)
    return jnp.where(codes < 0.0, -size, size)


def normalize(values):
    centred = values - jnp.mean(values, axis=-1, keepdims=True)
    variance = jnp.mean(centred * centred, axis=-1, keepdims=True)
    inv_std = lax.rsqrt(variance + epsilon)
    return (centred * inv_std, inv_std)


def send_kernel(pair_ref, w_in_ref, w_out_ref, w_head_t_ref, send_ref, rows_ref):
    n_row = send_ref.shape[0]
    span = send_ref.shape[1]
    channels = pair_ref.shape[-1]
    values = pair_ref[...].reshape(-1, channels).astype(f32)
    half = values.shape[0] // CYCLES
    x_hat, _ = normalize(values)
    hidden = jnp.maximum(dot(x_hat.astype(bf16), w_in_ref[...]), 0.0).astype(bf16)
    residual = (values + dot(hidden, w_out_ref[...])).astype(bf16)
    wide = jnp.concatenate([residual[:half], residual[half:]], axis=1)
    rows_ref[...] = encode(dot_t(wide, widen(w_head_t_ref[...])))
    for r in range(n_row):
        send_ref[r] = rows_ref[pl.ds(r, span, stride=n_row), :].astype(jnp.int16)


def prepare_kernel(
    pair_ref,
    bins_ref,
    w_in_ref,
    w_out_ref,
    w_head_t_ref,
    hidden_ref,
    normed_t_ref,
    residual_t_ref,
    x_hat_ref,
    inv_ref,
    logits_ref,
    bins_wide_ref,
    values_ref,
):
    channels = pair_ref.shape[-1]
    n_row = pair_ref.shape[2] // CYCLES
    count = pair_ref.shape[1]
    for a in range(CYCLES):
        for b in range(CYCLES):
            values_ref[a, :, b] = pair_ref[b, :, a * n_row : (a + 1) * n_row, :].astype(f32)
    values = values_ref[...].reshape(-1, channels)
    half = values.shape[0] // CYCLES
    x_hat, inv_std = normalize(values)
    normed = x_hat.astype(bf16)
    hidden = jnp.maximum(dot(normed, w_in_ref[...]), 0.0).astype(bf16)
    residual = (values + dot(hidden, w_out_ref[...])).astype(bf16)
    hidden_ref[...] = hidden
    normed_t_ref[...] = normed.T
    residual_t_ref[...] = residual.T
    x_hat_ref[...] = x_hat
    inv_ref[...] = jnp.broadcast_to(inv_std, x_hat.shape)
    logits_ref[...] = dot_t(
        jnp.concatenate([residual[:half], residual[half:]], axis=1), widen(w_head_t_ref[...])
    )
    columns = bins_ref.shape[-1]
    row_of = lax.broadcasted_iota(jnp.int32, (1, n_row, columns), 1)
    column_of = lax.broadcasted_iota(jnp.int32, (1, n_row, columns), 2)
    own = column_of % n_row == row_of
    lane = lax.broadcasted_iota(jnp.int32, (columns, channels), 1)
    source = lax.broadcasted_iota(jnp.int32, (columns, channels), 0)
    spread = (lane // (channels // CYCLES) == source // n_row).astype(f32).astype(bf16)
    for b in range(CYCLES):
        bins = bins_ref[b].astype(f32)
        picked = jnp.where(own, jnp.broadcast_to(bins[:, None, :], (count, n_row, columns)), 0.0)
        wide = dot(picked.reshape(count * n_row, columns).astype(bf16), spread)
        bins_wide_ref[:, b] = wide.astype(bf16).reshape(count, n_row, channels)


def backward_kernel(
    recv_ref,
    logits_ref,
    bins_wide_ref,
    hidden_ref,
    x_hat_hbm,
    inv_hbm,
    normed_t_hbm,
    residual_t_hbm,
    w_in_ref,
    w_out_ref,
    w_head_t_ref,
    grad_hbm,
    part_ref,
    x_hat_ref,
    inv_ref,
    normed_t_ref,
    residual_t_ref,
    grad_ref,
    rows_ref,
    sems,
):
    n_row, span, channels = recv_ref.shape
    count = span // CYCLES
    bins_count = channels // CYCLES
    half = span * n_row
    copies = [
        pltpu.make_async_copy(source, target, sems.at[i])
        for i, (source, target) in enumerate(
            (
                (x_hat_hbm, x_hat_ref),
                (inv_hbm, inv_ref),
                (residual_t_hbm, residual_t_ref),
                (normed_t_hbm, normed_t_ref),
            )
        )
    ]
    for copy in copies:
        copy.start()

    for r in range(n_row):
        rows_ref[pl.ds(r, span, stride=n_row), :] = decode(recv_ref[r])
    sym = logits_ref[...] + rows_ref[...]
    lane = lax.broadcasted_iota(jnp.int32, (1, channels), 1)
    left = lane < bins_count
    low = jnp.max(jnp.where(left, sym, -jnp.inf), axis=-1, keepdims=True)
    high = jnp.max(jnp.where(left, -jnp.inf, sym), axis=-1, keepdims=True)
    grown = jnp.exp(sym - jnp.where(left, low, high))
    low = jnp.sum(jnp.where(left, grown, 0.0), axis=-1, keepdims=True)
    high = jnp.sum(jnp.where(left, 0.0, grown), axis=-1, keepdims=True)
    probability = grown / jnp.where(left, low, high)
    own_bin = (lane % bins_count).astype(f32)
    bins = bins_wide_ref[...].reshape(half, channels).astype(f32)
    d_sym = probability - jnp.where(bins == own_bin, 1.0, 0.0)
    d_logit = (d_sym + d_sym).astype(bf16)

    wide = dot(d_logit, widen(w_head_t_ref[...]))
    d_resid = jnp.concatenate([wide[:, :channels], wide[:, channels:]], axis=0)
    d_update = d_resid.astype(bf16)
    hidden = hidden_ref[...]
    back = dot_t(d_update, w_out_ref[...]).astype(bf16)
    d_hidden = jnp.where(hidden > 0, back, jnp.zeros_like(back))
    d_normed = dot_t(d_hidden, w_in_ref[...])
    for copy in copies:
        copy.wait()
    x_hat = x_hat_ref[...]
    first_mean = jnp.mean(d_normed, axis=-1, keepdims=True)
    second_mean = jnp.mean(d_normed * x_hat, axis=-1, keepdims=True)
    d_pair = d_resid + inv_ref[...] * (d_normed - first_mean - x_hat * second_mean)
    d_pair = d_pair.astype(bf16).reshape(CYCLES, count, CYCLES, n_row, channels)
    for a in range(CYCLES):
        for b in range(CYCLES):
            grad_ref[b, :, a * n_row : (a + 1) * n_row, :] = d_pair[a, :, b]
    grad_copy = pltpu.make_async_copy(grad_ref, grad_hbm, sems.at[len(copies)])
    grad_copy.start()

    g_out = dot(d_update.T, hidden).T
    g_head = jnp.where(
        left,
        dot(residual_t_ref[:, :half], d_logit),
        dot(residual_t_ref[:, half:], d_logit),
    )
    g_in = dot(normed_t_ref[...], d_hidden)
    rows = channels // n_row
    tiles = hidden.shape[1] // channels
    long = tiles * rows
    for r in range(n_row):
        mine = g_in[r * rows : (r + 1) * rows, :]
        part_ref[r, 0:long, :] = jnp.concatenate(
            [mine[:, t * channels : (t + 1) * channels] for t in range(tiles)], axis=0
        ).astype(bf16)
        part_ref[r, long : 2 * long, :] = g_out[r * long : (r + 1) * long, :].astype(bf16)
        mine = g_head[r * rows : (r + 1) * rows, :]
        part_ref[r, 2 * long : 2 * long + 2 * rows, :] = jnp.concatenate(
            [mine, jnp.zeros_like(mine)], axis=0
        ).astype(bf16)
    grad_copy.wait()


def lanes_of(shape, axis):
    return lax.broadcasted_iota(jnp.int32, shape, axis)


def fold_matrix(width, kind):
    shape = (128, 128)
    return (lanes_of(shape, 0) % width == lanes_of(shape, 1) % width).astype(f32).astype(kind)


def middle_kernel(recv_ref, send_ref, rows_ref):
    n_col = send_ref.shape[0] // 4
    total = recv_ref[0].astype(f32)
    for r in range(1, recv_ref.shape[0]):
        total = total + recv_ref[r].astype(f32)
    rows, tiles = 8, 4
    mine = total[: rows * tiles]
    group = lanes_of((1, rows, 128), 2) // 16 == lanes_of((1, rows, 128), 1)
    spread = jnp.where(group, jnp.broadcast_to(mine[:, None, :], (rows * tiles, rows, 128)), 0.0)
    folded = dot(spread.reshape(-1, 128).astype(bf16), fold_matrix(16, bf16))
    folded = folded.reshape(tiles, rows, rows, 128)
    slot = lanes_of((1, rows, 1, 128), 3) // 16 == (8 - lanes_of((1, rows, 1, 128), 1)) % 8
    part_in = jnp.sum(jnp.where(slot, folded, 0.0), axis=1).reshape(n_col, 128)
    send_ref[pl.ds(0, n_col, stride=4), :] = part_in
    rows_ref[...] = jnp.concatenate([total[32:64]] * 4, axis=0).T
    lane = lanes_of((1, 128), 1)
    part_out = rows_ref[pl.ds(0, n_col, stride=4), :]
    for j in range(1, 4):
        part_out = jnp.where(
            lane // 32 == 4 - j, rows_ref[pl.ds(j, n_col, stride=4), :], part_out
        )
    send_ref[pl.ds(1, n_col, stride=4), :] = part_out
    mine = total[64:72]
    mine = mine + pltpu.roll(mine, 64, 1)
    rows_ref[...] = jnp.concatenate([mine] * 16, axis=0).T
    part_head = jnp.where(
        lane // 8 == 15,
        rows_ref[pl.ds(1, n_col, stride=2), :],
        rows_ref[pl.ds(0, n_col, stride=2), :],
    )
    send_ref[pl.ds(2, n_col, stride=4), :] = part_head
    send_ref[pl.ds(3, n_col, stride=4), :] = jnp.zeros_like(part_head)


def final_kernel(scale, recv_ref, in_ref, out_t_ref, head_t_ref):
    total = recv_ref[0:8, :]
    for c in range(1, recv_ref.shape[0] // 8):
        total = total + recv_ref[c * 8 : (c + 1) * 8, :]
    total = (total[0:4] + total[4:8]) * scale

    def unfold(row, out):
        count, width = out.shape
        if width * 8 <= 128:
            spread = jnp.broadcast_to(row, (8, 128))
            spread = pltpu.roll(spread, 0, 1, stride=width, stride_axis=0)
        else:
            spread = jnp.concatenate(
                [pltpu.roll(row, i * width, 1) if i else row for i in range(count)], axis=0
            )
        out[...] = spread[:count, :width]

    unfold(total[0:1], in_ref)
    unfold(total[1:2], out_t_ref)
    unfold(total[2:3], head_t_ref)


ROOM = 48 * 1024 * 1024


def params(limit=62 * 1024 * 1024):
    return pltpu.CompilerParams(vmem_limit_bytes=limit)


def in_hbm(array):
    return pltpu.with_memory_space_constraint(array, pltpu.HBM)


def forward_call(pair_rep, w_in, w_out, w_head_t, n_row, n_col):
    row_count, col_count, channels = pair_rep.shape
    return pl.pallas_call(
        send_kernel,
        out_shape=jax.ShapeDtypeStruct((n_row, CYCLES * n_col, channels), jnp.int16),
        scratch_shapes=[pltpu.VMEM((CYCLES * n_col * n_row, channels), jnp.int32)],
        compiler_params=params(),
        name="forward",
    )(pair_rep.reshape(CYCLES, n_col, col_count, channels), w_in, w_out, w_head_t)


def prepare_call(pair_rep, true_bins, w_in, w_out, w_head_t, n_row, n_col):
    row_count, col_count, channels = pair_rep.shape
    pairs = row_count * col_count
    hidden_count = w_in.shape[1]
    return pl.pallas_call(
        prepare_kernel,
        out_shape=[
            jax.ShapeDtypeStruct((pairs, hidden_count), bf16),
            jax.ShapeDtypeStruct((channels, pairs), bf16),
            jax.ShapeDtypeStruct((channels, pairs), bf16),
            jax.ShapeDtypeStruct((pairs, channels), f32),
            jax.ShapeDtypeStruct((pairs, channels), f32),
            jax.ShapeDtypeStruct((pairs // CYCLES, channels), f32),
            jax.ShapeDtypeStruct((n_col, CYCLES, n_row, channels), bf16),
        ],
        scratch_shapes=[pltpu.VMEM((CYCLES, n_col, CYCLES, n_row, channels), f32)],
        compiler_params=params(ROOM),
        cost_estimate=pl.CostEstimate(
            flops=2 * pairs * 2 * channels * hidden_count, bytes_accessed=8 * 2**20, transcendentals=0
        ),
        name="prepare",
    )(
        in_hbm(pair_rep.reshape(CYCLES, n_col, col_count, channels)),
        true_bins.reshape(CYCLES, n_col, col_count),
        in_hbm(w_in),
        in_hbm(w_out),
        in_hbm(w_head_t),
    )


def backward_call(
    recv, logits, bins_wide, hidden, x_hat, inv_std, normed_t, residual_t, w_in, w_out, w_head_t
):
    n_row, span, channels = recv.shape
    pairs, hidden_count = hidden.shape
    part_rows = 2 * (hidden_count // n_row) + 16
    grad = jax.ShapeDtypeStruct((CYCLES, span // CYCLES, CYCLES * n_row, channels), bf16)
    late = [in_hbm(x) for x in (x_hat, inv_std, normed_t, residual_t)]
    here = pl.BlockSpec()
    there = pl.BlockSpec(memory_space=pl.ANY)
    return pl.pallas_call(
        backward_kernel,
        in_specs=[here] * 4 + [there] * 4 + [here] * 3,
        out_specs=[there, here],
        out_shape=[grad, jax.ShapeDtypeStruct((n_row, part_rows, channels), bf16)],
        scratch_shapes=[pltpu.VMEM(x.shape, x.dtype) for x in (*late, grad)]
        + [
            pltpu.VMEM((pairs // CYCLES, channels), f32),
            pltpu.SemaphoreType.DMA((len(late) + 1,)),
        ],
        compiler_params=params(ROOM),
        name="backward",
    )(recv, logits, bins_wide, hidden, *late, w_in, w_out, w_head_t)


def middle_call(part, n_col):
    return pl.pallas_call(
        middle_kernel,
        out_shape=jax.ShapeDtypeStruct((4 * n_col, part.shape[-1]), f32),
        scratch_shapes=[pltpu.VMEM((128, 128), f32)],
        compiler_params=params(ROOM),
        name="sum_rows",
    )(part)


def final_call(share, scale, shapes):
    return pl.pallas_call(
        functools.partial(final_kernel, scale),
        out_shape=[jax.ShapeDtypeStruct(shape, f32) for shape in shapes],
        compiler_params=params(ROOM),
        name="sum_columns",
    )(share)


def shards(pair_rep, true_bins, w_in, w_out, w_head):
    row_count, col_count, channels = pair_rep.shape
    n_row = lax.axis_size("row")
    n_col = lax.axis_size("col")
    hidden_count = w_in.shape[1]
    bins_count = w_head.shape[1]
    w_head_t = w_head.T

    send = forward_call(pair_rep, w_in, w_out, w_head_t, n_row, n_col)
    recv = lax.all_to_all(
        send.reshape(n_row * n_col, CYCLES, channels),
        ("row", "col"),
        split_axis=0,
        concat_axis=0,
        tiled=True,
    ).reshape(n_row, CYCLES * n_col, channels)
    hidden, normed_t, residual_t, x_hat, inv_std, logits, bins_wide = prepare_call(
        pair_rep, true_bins, w_in, w_out, w_head_t, n_row, n_col
    )
    d_pair, part = backward_call(
        recv,
        logits,
        bins_wide,
        hidden,
        x_hat,
        inv_std,
        normed_t,
        residual_t,
        w_in,
        w_out,
        w_head_t,
    )
    part = lax.all_to_all(part, "row", split_axis=0, concat_axis=0, tiled=True)
    share = middle_call(part, n_col)
    share = lax.all_to_all(
        share.reshape(n_col, 4, channels), "col", split_axis=0, concat_axis=0, tiled=True
    ).reshape(4 * n_col, channels)
    grad_in, grad_out_t, grad_head_t = final_call(
        share,
        1.0 / (row_count * n_row),
        [
            (channels // n_row, hidden_count // n_col),
            (channels // n_col, hidden_count // n_row),
            (bins_count // n_col, channels // n_row),
        ],
    )
    return (
        d_pair.reshape(row_count, col_count, channels),
        grad_in,
        grad_out_t.T,
        grad_head_t.T,
    )


def solution(mesh):
    placed = (P("row", "col", None), P("row", "col"), P(), P(), P())
    return jax.shard_map(
        shards,
        mesh=mesh,
        in_specs=placed,
        out_specs=(P("row", "col", None), P("row", "col"), P("row", "col"), P("row", "col")),
        check_vma=False,
    )
```

```python
import functools

import jax
import jax.numpy as jnp
from jax import lax
from jax.experimental import pallas as pl
from jax.experimental.pallas import tpu as pltpu
from jax.sharding import PartitionSpec as P

epsilon = 1e-05
f32 = jnp.float32
bf16 = jnp.bfloat16

code_gain = 16.0
code_steps = 1850.0

CYCLES = 2


def dot(first, second):
    return jnp.dot(first, second, preferred_element_type=f32)


def dot_t(first, second):
    return lax.dot_general(first, second, (((1,), (1,)), ((), ())), preferred_element_type=f32)


def widen(w_head_t):
    blank = jnp.zeros_like(w_head_t)
    return jnp.concatenate(
        [
            jnp.concatenate([w_head_t, blank], axis=1),
            jnp.concatenate([blank, w_head_t], axis=1),
        ],
        axis=0,
    )


def encode(values):
    size = jnp.log(1.0 + jnp.abs(values) * code_gain) * code_steps + 0.5
    return jnp.where(values < 0.0, -size, size).astype(jnp.int32)


def decode(codes):
    codes = codes.astype(f32)
    size = (jnp.exp(jnp.abs(codes) * (1.0 / code_steps)) - 1.0) * (1.0 / code_gain)
    return jnp.where(codes < 0.0, -size, size)


def normalize(values):
    centred = values - jnp.mean(values, axis=-1, keepdims=True)
    variance = jnp.mean(centred * centred, axis=-1, keepdims=True)
    inv_std = lax.rsqrt(variance + epsilon)
    return (centred * inv_std, inv_std)


def send_kernel(pair_ref, w_in_ref, w_out_ref, w_head_t_ref, send_ref, rows_ref):
    n_row = send_ref.shape[0]
    span = send_ref.shape[1]
    channels = pair_ref.shape[-1]
    values = pair_ref[...].reshape(-1, channels).astype(f32)
    half = values.shape[0] // CYCLES
    x_hat, _ = normalize(values)
    hidden = jnp.maximum(dot(x_hat.astype(bf16), w_in_ref[...]), 0.0).astype(bf16)
    residual = (values + dot(hidden, w_out_ref[...])).astype(bf16)
    wide = jnp.concatenate([residual[:half], residual[half:]], axis=1)
    rows_ref[...] = encode(dot_t(wide, widen(w_head_t_ref[...])))
    for r in range(n_row):
        send_ref[r] = rows_ref[pl.ds(r, span, stride=n_row), :].astype(jnp.int16)


def prepare_kernel(
    pair_ref,
    bins_ref,
    w_in_ref,
    w_out_ref,
    w_head_t_ref,
    hidden_ref,
    logits_ref,
    bins_wide_ref,
    w_out_t_ref,
    hidden_hbm,
    normed_t_hbm,
    residual_t_hbm,
    normed_t_ref,
    residual_t_ref,
    values_ref,
    sems,
):
    kept = (
        (hidden_ref, hidden_hbm),
        (normed_t_ref, normed_t_hbm),
        (residual_t_ref, residual_t_hbm),
    )
    copies = [
        pltpu.make_async_copy(source, target, sems.at[i])
        for i, (source, target) in enumerate(kept)
    ]
    channels = pair_ref.shape[-1]
    n_row = pair_ref.shape[2] // CYCLES
    count = pair_ref.shape[1]
    for a in range(CYCLES):
        for b in range(CYCLES):
            values_ref[a, :, b] = pair_ref[b, :, a * n_row : (a + 1) * n_row, :].astype(f32)
    values = values_ref[...].reshape(-1, channels)
    half = values.shape[0] // CYCLES
    x_hat, _ = normalize(values)
    normed = x_hat.astype(bf16)
    hidden = jnp.maximum(dot(normed, w_in_ref[...]), 0.0).astype(bf16)
    residual = (values + dot(hidden, w_out_ref[...])).astype(bf16)
    hidden_ref[...] = hidden
    w_out_t_ref[...] = w_out_ref[...].T
    normed_t_ref[...] = normed.T
    residual_t_ref[...] = residual.T
    logits_ref[...] = dot_t(
        jnp.concatenate([residual[:half], residual[half:]], axis=1), widen(w_head_t_ref[...])
    )
    for copy in copies:
        copy.start()
    columns = bins_ref.shape[-1]
    row_of = lax.broadcasted_iota(jnp.int32, (1, n_row, columns), 1)
    column_of = lax.broadcasted_iota(jnp.int32, (1, n_row, columns), 2)
    own = column_of % n_row == row_of
    lane = lax.broadcasted_iota(jnp.int32, (columns, channels), 1)
    source = lax.broadcasted_iota(jnp.int32, (columns, channels), 0)
    spread = (lane // (channels // CYCLES) == source // n_row).astype(f32).astype(bf16)
    for b in range(CYCLES):
        bins = bins_ref[b].astype(f32)
        picked = jnp.where(own, jnp.broadcast_to(bins[:, None, :], (count, n_row, columns)), 0.0)
        wide = dot(picked.reshape(count * n_row, columns).astype(bf16), spread)
        bins_wide_ref[:, b] = wide.astype(bf16).reshape(count, n_row, channels)
    for copy in copies:
        copy.wait()


def weights_kernel(
    recv_ref,
    logits_ref,
    bins_wide_ref,
    hidden_ref,
    w_out_t_ref,
    normed_t_hbm,
    residual_t_hbm,
    w_head_t_ref,
    d_logit_ref,
    part_ref,
    normed_t_ref,
    residual_t_ref,
    rows_ref,
    sems,
):
    n_row, span, channels = recv_ref.shape
    bins_count = channels // CYCLES
    half = span * n_row
    copies = [
        pltpu.make_async_copy(source, target, sems.at[i])
        for i, (source, target) in enumerate(
            ((normed_t_hbm, normed_t_ref), (residual_t_hbm, residual_t_ref))
        )
    ]
    for copy in copies:
        copy.start()

    for r in range(n_row):
        rows_ref[pl.ds(r, span, stride=n_row), :] = decode(recv_ref[r])
    sym = logits_ref[...] + rows_ref[...]
    lane = lax.broadcasted_iota(jnp.int32, (1, channels), 1)
    left = lane < bins_count
    low = jnp.max(jnp.where(left, sym, -jnp.inf), axis=-1, keepdims=True)
    high = jnp.max(jnp.where(left, -jnp.inf, sym), axis=-1, keepdims=True)
    grown = jnp.exp(sym - jnp.where(left, low, high))
    low = jnp.sum(jnp.where(left, grown, 0.0), axis=-1, keepdims=True)
    high = jnp.sum(jnp.where(left, 0.0, grown), axis=-1, keepdims=True)
    probability = grown / jnp.where(left, low, high)
    own_bin = (lane % bins_count).astype(f32)
    bins = bins_wide_ref[...].reshape(half, channels).astype(f32)
    d_sym = probability - jnp.where(bins == own_bin, 1.0, 0.0)
    d_logit = (d_sym + d_sym).astype(bf16)
    d_logit_ref[...] = d_logit

    d_update = pair_gradient(d_logit, w_head_t_ref[...]).astype(bf16)
    hidden = hidden_ref[...]
    d_hidden = hidden_gradient(dot(d_update, w_out_t_ref[...]), hidden)
    d_logit_t = d_logit.T
    g_mid = (
        dot(d_logit_t, hidden[:half])[:bins_count] + dot(d_logit_t, hidden[half:])[bins_count:]
    )
    for copy in copies:
        copy.wait()
    g_head = jnp.where(
        left,
        dot(residual_t_ref[:, :half], d_logit),
        dot(residual_t_ref[:, half:], d_logit),
    )
    g_in = dot(normed_t_ref[...], d_hidden)
    rows = channels // n_row
    tiles = hidden.shape[1] // channels
    long = tiles * rows
    paired = jnp.concatenate([g_mid, jnp.roll(g_mid, -long // 2, axis=1)], axis=0).T
    for r in range(n_row):
        mine = g_in[r * rows : (r + 1) * rows, :]
        part_ref[r, 0:long, :] = jnp.concatenate(
            [mine[:, t * channels : (t + 1) * channels] for t in range(tiles)], axis=0
        ).astype(bf16)
        part_ref[r, long : long + long // 2, :] = paired[
            r * long : r * long + long // 2, :
        ].astype(bf16)
        mine = g_head[r * rows : (r + 1) * rows, :]
        part_ref[r, long + long // 2 :, :] = jnp.concatenate(
            [mine, jnp.zeros_like(mine)], axis=0
        ).astype(bf16)


def pair_gradient(d_logit, w_head_t):
    wide = dot(d_logit, widen(w_head_t))
    channels = wide.shape[1] // CYCLES
    return jnp.concatenate([wide[:, :channels], wide[:, channels:]], axis=0)


def hidden_gradient(back, hidden):
    back = back.astype(bf16)
    return jnp.where(hidden > 0, back, jnp.zeros_like(back))


def pair_kernel(
    d_logit_ref, hidden_ref, pair_ref, w_in_ref, w_out_ref, w_head_t_ref, grad_ref, values_ref
):
    channels = grad_ref.shape[-1]
    count = grad_ref.shape[1]
    n_row = grad_ref.shape[2] // CYCLES
    d_resid = pair_gradient(d_logit_ref[...], w_head_t_ref[...])
    d_hidden = hidden_gradient(dot_t(d_resid.astype(bf16), w_out_ref[...]), hidden_ref[...])
    d_normed = dot_t(d_hidden, w_in_ref[...])
    for a in range(CYCLES):
        for b in range(CYCLES):
            values_ref[a, :, b] = pair_ref[b, :, a * n_row : (a + 1) * n_row, :].astype(f32)
    x_hat, inv_std = normalize(values_ref[...].reshape(-1, channels))
    first_mean = jnp.mean(d_normed, axis=-1, keepdims=True)
    second_mean = jnp.mean(d_normed * x_hat, axis=-1, keepdims=True)
    d_pair = d_resid + inv_std * (d_normed - first_mean - x_hat * second_mean)
    d_pair = d_pair.astype(bf16).reshape(CYCLES, count, CYCLES, n_row, channels)
    for a in range(CYCLES):
        for b in range(CYCLES):
            grad_ref[b, :, a * n_row : (a + 1) * n_row, :] = d_pair[a, :, b]


def lanes_of(shape, axis):
    return lax.broadcasted_iota(jnp.int32, shape, axis)


def fold_matrix(width, kind):
    shape = (128, 128)
    return (lanes_of(shape, 0) % width == lanes_of(shape, 1) % width).astype(f32).astype(kind)


def middle_kernel(recv_ref, w_head_t_ref, send_ref, rows_ref):
    n_col = send_ref.shape[0] // 4
    total = recv_ref[0].astype(f32)
    for r in range(1, recv_ref.shape[0]):
        total = total + recv_ref[r].astype(f32)
    rows, tiles = 8, 4
    mine = total[: rows * tiles]
    group = lanes_of((1, rows, 128), 2) // 16 == lanes_of((1, rows, 128), 1)
    spread = jnp.where(group, jnp.broadcast_to(mine[:, None, :], (rows * tiles, rows, 128)), 0.0)
    folded = dot(spread.reshape(-1, 128).astype(bf16), fold_matrix(16, bf16))
    folded = folded.reshape(tiles, rows, rows, 128)
    slot = lanes_of((1, rows, 1, 128), 3) // 16 == (8 - lanes_of((1, rows, 1, 128), 1)) % 8
    part_in = jnp.sum(jnp.where(slot, folded, 0.0), axis=1).reshape(n_col, 128)
    send_ref[pl.ds(0, n_col, stride=4), :] = part_in
    lane = lanes_of((1, 128), 1)
    mid = total[32:48]
    mid = jnp.concatenate([jnp.where(lane < 64, mid, 0.0), jnp.where(lane < 64, 0.0, mid)], axis=0)
    w_head_t = w_head_t_ref[...]
    twice = jnp.concatenate([w_head_t, w_head_t], axis=0)
    high = mid.astype(bf16)
    low = (mid - high.astype(f32)).astype(bf16)
    mine = dot(high, twice) + dot(low, twice)
    rows_ref[...] = jnp.concatenate([mine] * 4, axis=0).T
    part_out = rows_ref[pl.ds(0, n_col, stride=4), :]
    for j in range(1, 4):
        part_out = jnp.where(
            lane // 32 == 4 - j, rows_ref[pl.ds(j, n_col, stride=4), :], part_out
        )
    send_ref[pl.ds(1, n_col, stride=4), :] = part_out
    mine = total[48:56]
    mine = mine + pltpu.roll(mine, 64, 1)
    rows_ref[...] = jnp.concatenate([mine] * 16, axis=0).T
    part_head = jnp.where(
        lane // 8 == 15,
        rows_ref[pl.ds(1, n_col, stride=2), :],
        rows_ref[pl.ds(0, n_col, stride=2), :],
    )
    send_ref[pl.ds(2, n_col, stride=4), :] = part_head
    send_ref[pl.ds(3, n_col, stride=4), :] = jnp.zeros_like(part_head)


def final_kernel(scale, recv_ref, in_ref, out_t_ref, head_t_ref):
    total = recv_ref[0:8, :]
    for c in range(1, recv_ref.shape[0] // 8):
        total = total + recv_ref[c * 8 : (c + 1) * 8, :]
    total = (total[0:4] + total[4:8]) * scale

    def unfold(row, out):
        count, width = out.shape
        if width * 8 <= 128:
            spread = jnp.broadcast_to(row, (8, 128))
            spread = pltpu.roll(spread, 0, 1, stride=width, stride_axis=0)
        else:
            spread = jnp.concatenate(
                [pltpu.roll(row, i * width, 1) if i else row for i in range(count)], axis=0
            )
        out[...] = spread[:count, :width]

    unfold(total[0:1], in_ref)
    unfold(total[1:2], out_t_ref)
    unfold(total[2:3], head_t_ref)


ROOM = 48 * 1024 * 1024


def params(limit=62 * 1024 * 1024):
    return pltpu.CompilerParams(vmem_limit_bytes=limit)


def in_hbm(array):
    return pltpu.with_memory_space_constraint(array, pltpu.HBM)


def forward_call(pair_rep, w_in, w_out, w_head_t, n_row, n_col):
    row_count, col_count, channels = pair_rep.shape
    return pl.pallas_call(
        send_kernel,
        out_shape=jax.ShapeDtypeStruct((n_row, CYCLES * n_col, channels), jnp.int16),
        scratch_shapes=[pltpu.VMEM((CYCLES * n_col * n_row, channels), jnp.int32)],
        compiler_params=params(),
        name="forward",
    )(pair_rep.reshape(CYCLES, n_col, col_count, channels), w_in, w_out, w_head_t)


HERE = pl.BlockSpec()
THERE = pl.BlockSpec(memory_space=pl.ANY)


def prepare_call(pair_rep, true_bins, w_in, w_out, w_head_t, n_row, n_col):
    row_count, col_count, channels = pair_rep.shape
    pairs = row_count * col_count
    hidden_count = w_in.shape[1]
    away = [
        jax.ShapeDtypeStruct((pairs, hidden_count), bf16),
        jax.ShapeDtypeStruct((channels, pairs), bf16),
        jax.ShapeDtypeStruct((channels, pairs), bf16),
    ]
    results = pl.pallas_call(
        prepare_kernel,
        in_specs=[HERE] * 5,
        out_specs=[HERE] * 4 + [pl.BlockSpec(memory_space=pltpu.HBM)] * 3,
        out_shape=[
            jax.ShapeDtypeStruct((pairs, hidden_count), bf16),
            jax.ShapeDtypeStruct((pairs // CYCLES, channels), f32),
            jax.ShapeDtypeStruct((n_col, CYCLES, n_row, channels), bf16),
            jax.ShapeDtypeStruct((channels, hidden_count), bf16),
            *away,
        ],
        scratch_shapes=[pltpu.VMEM(x.shape, x.dtype) for x in away[1:]]
        + [
            pltpu.VMEM((CYCLES, n_col, CYCLES, n_row, channels), f32),
            pltpu.SemaphoreType.DMA((len(away),)),
        ],
        compiler_params=params(ROOM),
        cost_estimate=pl.CostEstimate(
            flops=2 * pairs * 2 * channels * hidden_count, bytes_accessed=8 * 2**20, transcendentals=0
        ),
        name="prepare",
    )(
        in_hbm(pair_rep.reshape(CYCLES, n_col, col_count, channels)),
        true_bins.reshape(CYCLES, n_col, col_count),
        in_hbm(w_in),
        in_hbm(w_out),
        in_hbm(w_head_t),
    )
    return results[:4], [in_hbm(x) for x in results[4:]]


def weights_call(recv, near, normed_t, residual_t, w_head_t):
    logits, bins_wide, hidden, w_out_t = near
    n_row, span, channels = recv.shape
    pairs, hidden_count = hidden.shape
    part_rows = 2 * (hidden_count // n_row)
    d_logit = jax.ShapeDtypeStruct((pairs // CYCLES, channels), bf16)
    late = (normed_t, residual_t)
    return pl.pallas_call(
        weights_kernel,
        in_specs=[HERE] * 5 + [THERE] * 2 + [HERE],
        out_specs=[HERE, HERE],
        out_shape=[d_logit, jax.ShapeDtypeStruct((n_row, part_rows, channels), bf16)],
        scratch_shapes=[pltpu.VMEM(x.shape, x.dtype) for x in late]
        + [
            pltpu.VMEM((pairs // CYCLES, channels), f32),
            pltpu.SemaphoreType.DMA((len(late),)),
        ],
        compiler_params=params(ROOM),
        name="weights",
    )(recv, logits, bins_wide, hidden, w_out_t, normed_t, residual_t, w_head_t)


def pair_call(d_logit, hidden, pair_rep, w_in, w_out, w_head_t, n_row, n_col):
    row_count, col_count, channels = pair_rep.shape
    pairs, hidden_count = hidden.shape
    cycled = pair_rep.reshape(CYCLES, n_col, col_count, channels)
    return pl.pallas_call(
        pair_kernel,
        out_shape=jax.ShapeDtypeStruct(cycled.shape, bf16),
        scratch_shapes=[pltpu.VMEM((CYCLES, n_col, CYCLES, n_row, channels), f32)],
        compiler_params=params(ROOM),
        cost_estimate=pl.CostEstimate(
            flops=2 * pairs * 2 * channels * hidden_count, bytes_accessed=5 * 2**20, transcendentals=0
        ),
        name="pair",
    )(d_logit, *[in_hbm(x) for x in (hidden, cycled, w_in, w_out, w_head_t)])


def middle_call(part, w_head_t, done, n_col):
    part, _ = lax.optimization_barrier((part, done))
    return pl.pallas_call(
        middle_kernel,
        out_shape=jax.ShapeDtypeStruct((4 * n_col, part.shape[-1]), f32),
        scratch_shapes=[pltpu.VMEM((128, 128), f32)],
        compiler_params=params(ROOM),
        name="sum_rows",
    )(part, w_head_t)


def final_call(share, scale, shapes):
    return pl.pallas_call(
        functools.partial(final_kernel, scale),
        out_shape=[jax.ShapeDtypeStruct(shape, f32) for shape in shapes],
        compiler_params=params(ROOM),
        name="sum_columns",
    )(share)


def shards(pair_rep, true_bins, w_in, w_out, w_head):
    row_count, col_count, channels = pair_rep.shape
    n_row = lax.axis_size("row")
    n_col = lax.axis_size("col")
    hidden_count = w_in.shape[1]
    bins_count = w_head.shape[1]
    w_head_t = w_head.T

    send = forward_call(pair_rep, w_in, w_out, w_head_t, n_row, n_col)
    recv = lax.all_to_all(
        send.reshape(n_row * n_col, CYCLES, channels),
        ("row", "col"),
        split_axis=0,
        concat_axis=0,
        tiled=True,
    ).reshape(n_row, CYCLES * n_col, channels)
    (hidden, logits, bins_wide, w_out_t), (hidden_far, normed_t, residual_t) = (
        prepare_call(pair_rep, true_bins, w_in, w_out, w_head_t, n_row, n_col)
    )
    d_logit, part = weights_call(
        recv, (logits, bins_wide, hidden, w_out_t), normed_t, residual_t, w_head_t
    )
    part = lax.all_to_all(part, "row", split_axis=0, concat_axis=0, tiled=True)
    d_pair = pair_call(
        d_logit, hidden_far, pair_rep, w_in, w_out, w_head_t, n_row, n_col
    )
    share = middle_call(part, w_head_t, d_pair, n_col)
    share = lax.all_to_all(
        share.reshape(n_col, 4, channels), "col", split_axis=0, concat_axis=0, tiled=True
    ).reshape(4 * n_col, channels)
    grad_in, grad_out_t, grad_head_t = final_call(
        share,
        1.0 / (row_count * n_row),
        [
            (channels // n_row, hidden_count // n_col),
            (channels // n_col, hidden_count // n_row),
            (bins_count // n_col, channels // n_row),
        ],
    )
    return (
        d_pair.reshape(row_count, col_count, channels),
        grad_in,
        grad_out_t.T,
        grad_head_t.T,
    )


def solution(mesh):
    placed = (P("row", "col", None), P("row", "col"), P(), P(), P())
    return jax.shard_map(
        shards,
        mesh=mesh,
        in_specs=placed,
        out_specs=(P("row", "col", None), P("row", "col"), P("row", "col"), P("row", "col")),
        check_vma=False,
    )
```

```python
import functools

import jax
import jax.numpy as jnp
from jax import lax
from jax.experimental import pallas as pl
from jax.experimental.pallas import tpu as pltpu
from jax.sharding import PartitionSpec as P

epsilon = 1e-05
f32 = jnp.float32
bf16 = jnp.bfloat16

code_steps = 2350.0

CYCLES = 2


def dot(first, second):
    return jnp.dot(first, second, preferred_element_type=f32)


def dot_t(first, second):
    return lax.dot_general(first, second, (((1,), (1,)), ((), ())), preferred_element_type=f32)


def widen(w_head_t):
    blank = jnp.zeros_like(w_head_t)
    return jnp.concatenate(
        [
            jnp.concatenate([w_head_t, blank], axis=1),
            jnp.concatenate([blank, w_head_t], axis=1),
        ],
        axis=0,
    )


def encode(values):
    size = jnp.log(1.0 + jnp.abs(values)) * code_steps + 0.5
    return jnp.where(values < 0.0, -size, size).astype(jnp.int32)


def decode(codes):
    codes = codes.astype(f32)
    size = jnp.exp(jnp.abs(codes) * (1.0 / code_steps)) - 1.0
    return jnp.where(codes < 0.0, -size, size)


def normalize(values):
    centred = values - jnp.mean(values, axis=-1, keepdims=True)
    variance = jnp.mean(centred * centred, axis=-1, keepdims=True)
    inv_std = lax.rsqrt(variance + epsilon)
    return (centred * inv_std, inv_std)


def send_kernel(pair_ref, w_in_ref, w_out_ref, w_head_t_ref, send_ref, rows_ref):
    n_row = send_ref.shape[0]
    span = send_ref.shape[1]
    channels = pair_ref.shape[-1]
    values = pair_ref[...].reshape(-1, channels).astype(f32)
    half = values.shape[0] // CYCLES
    x_hat, _ = normalize(values)
    hidden = jnp.maximum(dot(x_hat.astype(bf16), w_in_ref[...]), 0.0).astype(bf16)
    residual = (values + dot(hidden, w_out_ref[...])).astype(bf16)
    wide = jnp.concatenate([residual[:half], residual[half:]], axis=1)
    rows_ref[...] = encode(dot_t(wide, widen(w_head_t_ref[...])))
    for r in range(n_row):
        send_ref[r] = rows_ref[pl.ds(r, span, stride=n_row), :].astype(jnp.int16)


def prepare_kernel(
    pair_ref,
    bins_ref,
    w_in_ref,
    w_out_ref,
    w_head_t_ref,
    hidden_ref,
    logits_ref,
    bins_wide_ref,
    w_out_t_ref,
    hidden_hbm,
    normed_t_hbm,
    residual_t_hbm,
    normed_t_ref,
    residual_t_ref,
    values_ref,
    sems,
):
    kept = (
        (hidden_ref, hidden_hbm),
        (normed_t_ref, normed_t_hbm),
        (residual_t_ref, residual_t_hbm),
    )
    copies = [
        pltpu.make_async_copy(source, target, sems.at[i])
        for i, (source, target) in enumerate(kept)
    ]
    channels = pair_ref.shape[-1]
    n_row = pair_ref.shape[2] // CYCLES
    count = pair_ref.shape[1]
    for a in range(CYCLES):
        for b in range(CYCLES):
            values_ref[a, :, b] = pair_ref[b, :, a * n_row : (a + 1) * n_row, :].astype(f32)
    values = values_ref[...].reshape(-1, channels)
    half = values.shape[0] // CYCLES
    x_hat, _ = normalize(values)
    normed = x_hat.astype(bf16)
    hidden = jnp.maximum(dot(normed, w_in_ref[...]), 0.0).astype(bf16)
    residual = (values + dot(hidden, w_out_ref[...])).astype(bf16)
    hidden_ref[...] = hidden
    w_out_t_ref[...] = w_out_ref[...].T
    normed_t_ref[...] = normed.T
    residual_t_ref[...] = residual.T
    logits_ref[...] = dot_t(
        jnp.concatenate([residual[:half], residual[half:]], axis=1), widen(w_head_t_ref[...])
    )
    for copy in copies:
        copy.start()
    columns = bins_ref.shape[-1]
    row_of = lax.broadcasted_iota(jnp.int32, (1, n_row, columns), 1)
    column_of = lax.broadcasted_iota(jnp.int32, (1, n_row, columns), 2)
    own = column_of % n_row == row_of
    lane = lax.broadcasted_iota(jnp.int32, (columns, channels), 1)
    source = lax.broadcasted_iota(jnp.int32, (columns, channels), 0)
    spread = (lane // (channels // CYCLES) == source // n_row).astype(f32).astype(bf16)
    for b in range(CYCLES):
        bins = bins_ref[b].astype(f32)
        picked = jnp.where(own, jnp.broadcast_to(bins[:, None, :], (count, n_row, columns)), 0.0)
        wide = dot(picked.reshape(count * n_row, columns).astype(bf16), spread)
        bins_wide_ref[:, b] = wide.astype(bf16).reshape(count, n_row, channels)
    for copy in copies:
        copy.wait()


def weights_kernel(
    recv_ref,
    logits_ref,
    bins_wide_ref,
    hidden_ref,
    w_out_t_ref,
    normed_t_hbm,
    residual_t_hbm,
    w_head_t_ref,
    d_logit_ref,
    part_ref,
    normed_t_ref,
    residual_t_ref,
    rows_ref,
    sems,
):
    n_row, span, channels = recv_ref.shape
    bins_count = channels // CYCLES
    half = span * n_row
    copies = [
        pltpu.make_async_copy(source, target, sems.at[i])
        for i, (source, target) in enumerate(
            ((normed_t_hbm, normed_t_ref), (residual_t_hbm, residual_t_ref))
        )
    ]
    for copy in copies:
        copy.start()

    for r in range(n_row):
        rows_ref[pl.ds(r, span, stride=n_row), :] = decode(recv_ref[r])
    sym = logits_ref[...] + rows_ref[...]
    lane = lax.broadcasted_iota(jnp.int32, (1, channels), 1)
    left = lane < bins_count
    low = jnp.max(jnp.where(left, sym, -jnp.inf), axis=-1, keepdims=True)
    high = jnp.max(jnp.where(left, -jnp.inf, sym), axis=-1, keepdims=True)
    grown = jnp.exp(sym - jnp.where(left, low, high))
    low = jnp.sum(jnp.where(left, grown, 0.0), axis=-1, keepdims=True)
    high = jnp.sum(jnp.where(left, 0.0, grown), axis=-1, keepdims=True)
    probability = grown / jnp.where(left, low, high)
    own_bin = (lane % bins_count).astype(f32)
    bins = bins_wide_ref[...].reshape(half, channels).astype(f32)
    d_sym = probability - jnp.where(bins == own_bin, 1.0, 0.0)
    d_logit = (d_sym + d_sym).astype(bf16)
    d_logit_ref[...] = d_logit

    d_update = pair_gradient(d_logit, w_head_t_ref[...]).astype(bf16)
    hidden = hidden_ref[...]
    d_hidden = hidden_gradient(dot(d_update, w_out_t_ref[...]), hidden)
    for copy in copies:
        copy.wait()
    g_head = jnp.where(
        left,
        dot(residual_t_ref[:, :half], d_logit),
        dot(residual_t_ref[:, half:], d_logit),
    )
    g_in = dot(normed_t_ref[...], d_hidden)
    d_logit_t = d_logit.T
    g_mid = (
        dot(d_logit_t, hidden[:half])[:bins_count] + dot(d_logit_t, hidden[half:])[bins_count:]
    )
    rows = channels // n_row
    tiles = hidden.shape[1] // channels
    long = tiles * rows
    paired = jnp.concatenate([g_mid, jnp.roll(g_mid, -long // 2, axis=1)], axis=0).T
    for r in range(n_row):
        mine = g_in[r * rows : (r + 1) * rows, :]
        part_ref[r, 0:long, :] = jnp.concatenate(
            [mine[:, t * channels : (t + 1) * channels] for t in range(tiles)], axis=0
        ).astype(bf16)
        part_ref[r, long : long + long // 2, :] = paired[
            r * long : r * long + long // 2, :
        ].astype(bf16)
        mine = g_head[r * rows : (r + 1) * rows, :]
        part_ref[r, long + long // 2 :, :] = jnp.concatenate(
            [mine, jnp.zeros_like(mine)], axis=0
        ).astype(bf16)


def pair_gradient(d_logit, w_head_t):
    wide = dot(d_logit, widen(w_head_t))
    channels = wide.shape[1] // CYCLES
    return jnp.concatenate([wide[:, :channels], wide[:, channels:]], axis=0)


def hidden_gradient(back, hidden):
    back = back.astype(bf16)
    return jnp.where(hidden > 0, back, jnp.zeros_like(back))


def pair_kernel(
    d_logit_ref, hidden_ref, pair_ref, w_in_ref, w_out_ref, w_head_t_ref, grad_ref, values_ref
):
    channels = grad_ref.shape[-1]
    count = grad_ref.shape[1]
    n_row = grad_ref.shape[2] // CYCLES
    d_resid = pair_gradient(d_logit_ref[...], w_head_t_ref[...])
    d_hidden = hidden_gradient(dot_t(d_resid.astype(bf16), w_out_ref[...]), hidden_ref[...])
    d_normed = dot_t(d_hidden, w_in_ref[...])
    for a in range(CYCLES):
        for b in range(CYCLES):
            values_ref[a, :, b] = pair_ref[b, :, a * n_row : (a + 1) * n_row, :].astype(f32)
    x_hat, inv_std = normalize(values_ref[...].reshape(-1, channels))
    first_mean = jnp.mean(d_normed, axis=-1, keepdims=True)
    second_mean = jnp.mean(d_normed * x_hat, axis=-1, keepdims=True)
    d_pair = d_resid + inv_std * (d_normed - first_mean - x_hat * second_mean)
    d_pair = d_pair.astype(bf16).reshape(CYCLES, count, CYCLES, n_row, channels)
    for a in range(CYCLES):
        for b in range(CYCLES):
            grad_ref[b, :, a * n_row : (a + 1) * n_row, :] = d_pair[a, :, b]


def lanes_of(shape, axis):
    return lax.broadcasted_iota(jnp.int32, shape, axis)


def fold_matrix(width, kind):
    shape = (128, 128)
    return (lanes_of(shape, 0) % width == lanes_of(shape, 1) % width).astype(f32).astype(kind)


def middle_kernel(recv_ref, w_head_t_ref, out_ref, rows_ref, send_ref):
    n_col = out_ref.shape[0] // 4
    total = recv_ref[0].astype(f32)
    for r in range(1, recv_ref.shape[0]):
        total = total + recv_ref[r].astype(f32)
    rows, tiles = 8, 4
    mine = total[: rows * tiles]
    group = lanes_of((1, rows, 128), 2) // 16 == lanes_of((1, rows, 128), 1)
    spread = jnp.where(group, jnp.broadcast_to(mine[:, None, :], (rows * tiles, rows, 128)), 0.0)
    folded = dot(spread.reshape(-1, 128).astype(bf16), fold_matrix(16, bf16))
    folded = folded.reshape(tiles, rows, rows, 128)
    slot = lanes_of((1, rows, 1, 128), 3) // 16 == (8 - lanes_of((1, rows, 1, 128), 1)) % 8
    part_in = jnp.sum(jnp.where(slot, folded, 0.0), axis=1).reshape(n_col, 128)
    send_ref[pl.ds(0, n_col, stride=4), :] = part_in
    lane = lanes_of((1, 128), 1)
    mid = total[32:48]
    mid = jnp.concatenate([jnp.where(lane < 64, mid, 0.0), jnp.where(lane < 64, 0.0, mid)], axis=0)
    w_head_t = w_head_t_ref[...]
    twice = jnp.concatenate([w_head_t, w_head_t], axis=0)
    high = mid.astype(bf16)
    low = (mid - high.astype(f32)).astype(bf16)
    mine = dot(high, twice) + dot(low, twice)
    rows_ref[...] = jnp.concatenate([mine] * 4, axis=0).T
    part_out = rows_ref[pl.ds(0, n_col, stride=4), :]
    for j in range(1, 4):
        part_out = jnp.where(
            lane // 32 == 4 - j, rows_ref[pl.ds(j, n_col, stride=4), :], part_out
        )
    send_ref[pl.ds(1, n_col, stride=4), :] = part_out
    mine = total[48:56]
    mine = mine + pltpu.roll(mine, 64, 1)
    rows_ref[...] = jnp.concatenate([mine] * 16, axis=0).T
    part_head = jnp.where(
        lane // 8 == 15,
        rows_ref[pl.ds(1, n_col, stride=2), :],
        rows_ref[pl.ds(0, n_col, stride=2), :],
    )
    send_ref[pl.ds(2, n_col, stride=4), :] = part_head
    send_ref[pl.ds(3, n_col, stride=4), :] = jnp.zeros_like(part_head)
    out_ref[...] = send_ref[...].astype(bf16)


def final_kernel(scale, recv_ref, in_ref, out_t_ref, head_t_ref):
    values = recv_ref[...].astype(f32)
    total = values[0:8]
    for c in range(1, values.shape[0] // 8):
        total = total + values[c * 8 : (c + 1) * 8]
    total = (total[0:4] + total[4:8]) * scale

    def unfold(row, out):
        count, width = out.shape
        if width * 8 <= 128:
            spread = jnp.broadcast_to(row, (8, 128))
            spread = pltpu.roll(spread, 0, 1, stride=width, stride_axis=0)
        else:
            spread = jnp.concatenate(
                [pltpu.roll(row, i * width, 1) if i else row for i in range(count)], axis=0
            )
        out[...] = spread[:count, :width]

    unfold(total[0:1], in_ref)
    unfold(total[1:2], out_t_ref)
    unfold(total[2:3], head_t_ref)


ROOM = 48 * 1024 * 1024


def params(limit=62 * 1024 * 1024):
    return pltpu.CompilerParams(vmem_limit_bytes=limit)


def in_hbm(array):
    return pltpu.with_memory_space_constraint(array, pltpu.HBM)


def forward_call(pair_rep, w_in, w_out, w_head_t, n_row, n_col):
    row_count, col_count, channels = pair_rep.shape
    return pl.pallas_call(
        send_kernel,
        out_shape=jax.ShapeDtypeStruct((n_row, CYCLES * n_col, channels), jnp.int16),
        scratch_shapes=[pltpu.VMEM((CYCLES * n_col * n_row, channels), jnp.int32)],
        compiler_params=params(),
        name="forward",
    )(pair_rep.reshape(CYCLES, n_col, col_count, channels), w_in, w_out, w_head_t)


HERE = pl.BlockSpec()
THERE = pl.BlockSpec(memory_space=pl.ANY)


def prepare_call(pair_rep, true_bins, w_in, w_out, w_head_t, n_row, n_col):
    row_count, col_count, channels = pair_rep.shape
    pairs = row_count * col_count
    hidden_count = w_in.shape[1]
    away = [
        jax.ShapeDtypeStruct((pairs, hidden_count), bf16),
        jax.ShapeDtypeStruct((channels, pairs), bf16),
        jax.ShapeDtypeStruct((channels, pairs), bf16),
    ]
    results = pl.pallas_call(
        prepare_kernel,
        in_specs=[HERE] * 5,
        out_specs=[HERE] * 4 + [pl.BlockSpec(memory_space=pltpu.HBM)] * 3,
        out_shape=[
            jax.ShapeDtypeStruct((pairs, hidden_count), bf16),
            jax.ShapeDtypeStruct((pairs // CYCLES, channels), f32),
            jax.ShapeDtypeStruct((n_col, CYCLES, n_row, channels), bf16),
            jax.ShapeDtypeStruct((channels, hidden_count), bf16),
            *away,
        ],
        scratch_shapes=[pltpu.VMEM(x.shape, x.dtype) for x in away[1:]]
        + [
            pltpu.VMEM((CYCLES, n_col, CYCLES, n_row, channels), f32),
            pltpu.SemaphoreType.DMA((len(away),)),
        ],
        compiler_params=params(ROOM),
        cost_estimate=pl.CostEstimate(
            flops=2 * pairs * 2 * channels * hidden_count, bytes_accessed=8 * 2**20, transcendentals=0
        ),
        name="prepare",
    )(
        in_hbm(pair_rep.reshape(CYCLES, n_col, col_count, channels)),
        true_bins.reshape(CYCLES, n_col, col_count),
        in_hbm(w_in),
        in_hbm(w_out),
        in_hbm(w_head_t),
    )
    return results[:4], [in_hbm(x) for x in results[4:]]


def weights_call(recv, near, normed_t, residual_t, w_head_t):
    logits, bins_wide, hidden, w_out_t = near
    n_row, span, channels = recv.shape
    pairs, hidden_count = hidden.shape
    part_rows = 2 * (hidden_count // n_row)
    d_logit = jax.ShapeDtypeStruct((pairs // CYCLES, channels), bf16)
    late = (normed_t, residual_t)
    return pl.pallas_call(
        weights_kernel,
        in_specs=[HERE] * 5 + [THERE] * 2 + [HERE],
        out_specs=[HERE, HERE],
        out_shape=[d_logit, jax.ShapeDtypeStruct((n_row, part_rows, channels), bf16)],
        scratch_shapes=[pltpu.VMEM(x.shape, x.dtype) for x in late]
        + [
            pltpu.VMEM((pairs // CYCLES, channels), f32),
            pltpu.SemaphoreType.DMA((len(late),)),
        ],
        compiler_params=params(ROOM),
        name="weights",
    )(recv, logits, bins_wide, hidden, w_out_t, normed_t, residual_t, w_head_t)


def pair_call(d_logit, hidden, pair_rep, w_in, w_out, w_head_t, n_row, n_col):
    row_count, col_count, channels = pair_rep.shape
    pairs, hidden_count = hidden.shape
    cycled = pair_rep.reshape(CYCLES, n_col, col_count, channels)
    return pl.pallas_call(
        pair_kernel,
        out_shape=jax.ShapeDtypeStruct(cycled.shape, bf16),
        scratch_shapes=[pltpu.VMEM((CYCLES, n_col, CYCLES, n_row, channels), f32)],
        compiler_params=params(ROOM),
        cost_estimate=pl.CostEstimate(
            flops=2 * pairs * 2 * channels * hidden_count, bytes_accessed=5 * 2**20, transcendentals=0
        ),
        name="pair",
    )(d_logit, *[in_hbm(x) for x in (hidden, cycled, w_in, w_out, w_head_t)])


def middle_call(part, w_head_t, done, n_col):
    part, _ = lax.optimization_barrier((part, done))
    return pl.pallas_call(
        middle_kernel,
        out_shape=jax.ShapeDtypeStruct((4 * n_col, part.shape[-1]), bf16),
        scratch_shapes=[pltpu.VMEM((128, 128), f32), pltpu.VMEM((4 * n_col, part.shape[-1]), f32)],
        compiler_params=params(ROOM),
        name="sum_rows",
    )(part, w_head_t)


def final_call(share, scale, shapes):
    return pl.pallas_call(
        functools.partial(final_kernel, scale),
        out_shape=[jax.ShapeDtypeStruct(shape, f32) for shape in shapes],
        compiler_params=params(ROOM),
        name="sum_columns",
    )(share)


def shards(pair_rep, true_bins, w_in, w_out, w_head):
    row_count, col_count, channels = pair_rep.shape
    n_row = lax.axis_size("row")
    n_col = lax.axis_size("col")
    hidden_count = w_in.shape[1]
    bins_count = w_head.shape[1]
    w_head_t = w_head.T

    send = forward_call(pair_rep, w_in, w_out, w_head_t, n_row, n_col)
    recv = lax.all_to_all(
        send.reshape(n_row * n_col, CYCLES, channels),
        ("row", "col"),
        split_axis=0,
        concat_axis=0,
        tiled=True,
    ).reshape(n_row, CYCLES * n_col, channels)
    (hidden, logits, bins_wide, w_out_t), (hidden_far, normed_t, residual_t) = (
        prepare_call(pair_rep, true_bins, w_in, w_out, w_head_t, n_row, n_col)
    )
    d_logit, part = weights_call(
        recv, (logits, bins_wide, hidden, w_out_t), normed_t, residual_t, w_head_t
    )
    part = lax.all_to_all(part, "row", split_axis=0, concat_axis=0, tiled=True)
    d_pair = pair_call(
        d_logit, hidden_far, pair_rep, w_in, w_out, w_head_t, n_row, n_col
    )
    share = middle_call(part, w_head_t, d_pair, n_col)
    share = lax.all_to_all(
        share.reshape(n_col, 4, channels), "col", split_axis=0, concat_axis=0, tiled=True
    ).reshape(4 * n_col, channels)
    grad_in, grad_out_t, grad_head_t = final_call(
        share,
        1.0 / (row_count * n_row),
        [
            (channels // n_row, hidden_count // n_col),
            (channels // n_col, hidden_count // n_row),
            (bins_count // n_col, channels // n_row),
        ],
    )
    return (
        d_pair.reshape(row_count, col_count, channels),
        grad_in,
        grad_out_t.T,
        grad_head_t.T,
    )


def solution(mesh):
    placed = (P("row", "col", None), P("row", "col"), P(), P(), P())
    return jax.shard_map(
        shards,
        mesh=mesh,
        in_specs=placed,
        out_specs=(P("row", "col", None), P("row", "col"), P("row", "col"), P("row", "col")),
        check_vma=False,
    )
```

```python
import functools

import jax
import jax.numpy as jnp
from jax import lax
from jax.experimental import pallas as pl
from jax.experimental.pallas import tpu as pltpu
from jax.sharding import PartitionSpec as P

epsilon = 1e-05
f32 = jnp.float32
bf16 = jnp.bfloat16

code_steps = 2350.0

CYCLES = 2

ACROSS = 4


def dot(first, second):
    return jnp.dot(first, second, preferred_element_type=f32)


def dot_t(first, second):
    return lax.dot_general(first, second, (((1,), (1,)), ((), ())), preferred_element_type=f32)


def widen(w_head_t):
    blank = jnp.zeros_like(w_head_t)
    return jnp.concatenate(
        [
            jnp.concatenate([w_head_t, blank], axis=1),
            jnp.concatenate([blank, w_head_t], axis=1),
        ],
        axis=0,
    )


def encode(values):
    size = jnp.log(1.0 + jnp.abs(values)) * code_steps + 0.5
    return jnp.where(values < 0.0, -size, size).astype(jnp.int32)


def decode(codes):
    codes = codes.astype(f32)
    size = jnp.exp(jnp.abs(codes) * (1.0 / code_steps)) - 1.0
    return jnp.where(codes < 0.0, -size, size)


def normalize(values):
    centred = values - jnp.mean(values, axis=-1, keepdims=True)
    variance = jnp.mean(centred * centred, axis=-1, keepdims=True)
    inv_std = lax.rsqrt(variance + epsilon)
    return (centred * inv_std, inv_std)


def send_kernel(pair_ref, w_in_ref, w_out_ref, w_head_t_ref, send_ref, rows_ref):
    n_row = send_ref.shape[0]
    span = send_ref.shape[1]
    channels = pair_ref.shape[-1]
    values = pair_ref[...].reshape(-1, channels).astype(f32)
    half = values.shape[0] // CYCLES
    x_hat, _ = normalize(values)
    hidden = jnp.maximum(dot(x_hat.astype(bf16), w_in_ref[...]), 0.0).astype(bf16)
    residual = (values + dot(hidden, w_out_ref[...])).astype(bf16)
    wide = jnp.concatenate([residual[:half], residual[half:]], axis=1)
    rows_ref[...] = encode(dot_t(wide, widen(w_head_t_ref[...])))
    for r in range(n_row):
        send_ref[r] = rows_ref[pl.ds(r, span, stride=n_row), :].astype(jnp.int16)


def prepare_kernel(
    pair_ref,
    bins_ref,
    w_in_ref,
    w_out_ref,
    w_head_t_ref,
    hidden_ref,
    logits_ref,
    bins_wide_ref,
    w_out_t_ref,
    hidden_hbm,
    normed_t_hbm,
    residual_t_hbm,
    normed_t_ref,
    residual_t_ref,
    values_ref,
    sems,
):
    kept = (
        (hidden_ref, hidden_hbm),
        (normed_t_ref, normed_t_hbm),
        (residual_t_ref, residual_t_hbm),
    )
    copies = [
        pltpu.make_async_copy(source, target, sems.at[i])
        for i, (source, target) in enumerate(kept)
    ]
    channels = pair_ref.shape[-1]
    n_row = pair_ref.shape[2] // CYCLES
    count = pair_ref.shape[1]
    for a in range(CYCLES):
        for b in range(CYCLES):
            values_ref[a, :, b] = pair_ref[b, :, a * n_row : (a + 1) * n_row, :].astype(f32)
    values = values_ref[...].reshape(-1, channels)
    half = values.shape[0] // CYCLES
    x_hat, _ = normalize(values)
    normed = x_hat.astype(bf16)
    hidden = jnp.maximum(dot(normed, w_in_ref[...]), 0.0).astype(bf16)
    residual = (values + dot(hidden, w_out_ref[...])).astype(bf16)
    hidden_ref[...] = hidden
    w_out_t_ref[...] = w_out_ref[...].T
    normed_t_ref[...] = normed.T
    residual_t_ref[...] = residual.T
    logits_ref[...] = dot_t(
        jnp.concatenate([residual[:half], residual[half:]], axis=1), widen(w_head_t_ref[...])
    )
    for copy in copies:
        copy.start()
    columns = bins_ref.shape[-1]
    row_of = lax.broadcasted_iota(jnp.int32, (1, n_row, columns), 1)
    column_of = lax.broadcasted_iota(jnp.int32, (1, n_row, columns), 2)
    own = column_of % n_row == row_of
    lane = lax.broadcasted_iota(jnp.int32, (columns, channels), 1)
    source = lax.broadcasted_iota(jnp.int32, (columns, channels), 0)
    spread = (lane // (channels // CYCLES) == source // n_row).astype(f32).astype(bf16)
    for b in range(CYCLES):
        bins = bins_ref[b].astype(f32)
        picked = jnp.where(own, jnp.broadcast_to(bins[:, None, :], (count, n_row, columns)), 0.0)
        wide = dot(picked.reshape(count * n_row, columns).astype(bf16), spread)
        bins_wide_ref[:, b] = wide.astype(bf16).reshape(count, n_row, channels)
    for copy in copies:
        copy.wait()


def weights_kernel(
    recv_ref,
    logits_ref,
    bins_wide_ref,
    hidden_ref,
    w_out_t_ref,
    normed_t_hbm,
    residual_t_hbm,
    w_head_t_ref,
    d_logit_ref,
    part_ref,
    normed_t_ref,
    residual_t_ref,
    rows_ref,
    sems,
):
    n_row, span, channels = recv_ref.shape
    bins_count = channels // CYCLES
    half = span * n_row
    copies = [
        pltpu.make_async_copy(source, target, sems.at[i])
        for i, (source, target) in enumerate(
            ((normed_t_hbm, normed_t_ref), (residual_t_hbm, residual_t_ref))
        )
    ]
    for copy in copies:
        copy.start()

    for r in range(n_row):
        rows_ref[pl.ds(r, span, stride=n_row), :] = decode(recv_ref[r])
    sym = logits_ref[...] + rows_ref[...]
    lane = lax.broadcasted_iota(jnp.int32, (1, channels), 1)
    left = lane < bins_count
    low = jnp.max(jnp.where(left, sym, -jnp.inf), axis=-1, keepdims=True)
    high = jnp.max(jnp.where(left, -jnp.inf, sym), axis=-1, keepdims=True)
    grown = jnp.exp(sym - jnp.where(left, low, high))
    low = jnp.sum(jnp.where(left, grown, 0.0), axis=-1, keepdims=True)
    high = jnp.sum(jnp.where(left, 0.0, grown), axis=-1, keepdims=True)
    probability = grown / jnp.where(left, low, high)
    own_bin = (lane % bins_count).astype(f32)
    bins = bins_wide_ref[...].reshape(half, channels).astype(f32)
    d_sym = probability - jnp.where(bins == own_bin, 1.0, 0.0)
    d_logit = (d_sym + d_sym).astype(bf16)
    d_logit_ref[...] = d_logit

    d_update = pair_gradient(d_logit, w_head_t_ref[...]).astype(bf16)
    hidden = hidden_ref[...]
    d_hidden = hidden_gradient(dot(d_update, w_out_t_ref[...]), hidden)
    for copy in copies:
        copy.wait()
    g_head = jnp.where(
        left,
        dot(residual_t_ref[:, :half], d_logit),
        dot(residual_t_ref[:, half:], d_logit),
    )
    g_in = dot(normed_t_ref[...], d_hidden)
    d_logit_t = d_logit.T
    g_mid = (
        dot(d_logit_t, hidden[:half])[:bins_count] + dot(d_logit_t, hidden[half:])[bins_count:]
    )
    rows = channels // n_row
    tiles = hidden.shape[1] // channels
    long = tiles * rows
    paired = jnp.concatenate([g_mid, jnp.roll(g_mid, -long // 2, axis=1)], axis=0).T
    for r in range(n_row):
        slot = r % ACROSS * (n_row // ACROSS) + r // ACROSS
        mine = g_in[r * rows : (r + 1) * rows, :]
        part_ref[slot, 0:long, :] = jnp.concatenate(
            [mine[:, t * channels : (t + 1) * channels] for t in range(tiles)], axis=0
        ).astype(bf16)
        part_ref[slot, long : long + long // 2, :] = paired[
            r * long : r * long + long // 2, :
        ].astype(bf16)
        mine = g_head[r * rows : (r + 1) * rows, :]
        part_ref[slot, long + long // 2 :, :] = jnp.concatenate(
            [mine, jnp.zeros_like(mine)], axis=0
        ).astype(bf16)


def pair_gradient(d_logit, w_head_t):
    wide = dot(d_logit, widen(w_head_t))
    channels = wide.shape[1] // CYCLES
    return jnp.concatenate([wide[:, :channels], wide[:, channels:]], axis=0)


def hidden_gradient(back, hidden):
    back = back.astype(bf16)
    return jnp.where(hidden > 0, back, jnp.zeros_like(back))


def pair_kernel(
    d_logit_ref, hidden_ref, pair_ref, w_in_ref, w_out_ref, w_head_t_ref, grad_ref, values_ref
):
    channels = grad_ref.shape[-1]
    count = grad_ref.shape[1]
    n_row = grad_ref.shape[2] // CYCLES
    d_resid = pair_gradient(d_logit_ref[...], w_head_t_ref[...])
    d_hidden = hidden_gradient(dot_t(d_resid.astype(bf16), w_out_ref[...]), hidden_ref[...])
    d_normed = dot_t(d_hidden, w_in_ref[...])
    for a in range(CYCLES):
        for b in range(CYCLES):
            values_ref[a, :, b] = pair_ref[b, :, a * n_row : (a + 1) * n_row, :].astype(f32)
    x_hat, inv_std = normalize(values_ref[...].reshape(-1, channels))
    first_mean = jnp.mean(d_normed, axis=-1, keepdims=True)
    second_mean = jnp.mean(d_normed * x_hat, axis=-1, keepdims=True)
    d_pair = d_resid + inv_std * (d_normed - first_mean - x_hat * second_mean)
    d_pair = d_pair.astype(bf16).reshape(CYCLES, count, CYCLES, n_row, channels)
    for a in range(CYCLES):
        for b in range(CYCLES):
            grad_ref[b, :, a * n_row : (a + 1) * n_row, :] = d_pair[a, :, b]


def lanes_of(shape, axis):
    return lax.broadcasted_iota(jnp.int32, shape, axis)


def fold_matrix(width, kind):
    shape = (128, 128)
    return (lanes_of(shape, 0) % width == lanes_of(shape, 1) % width).astype(f32).astype(kind)


def middle_kernel(recv_ref, w_head_t_ref, out_ref, rows_ref, send_ref):
    n_far = recv_ref.shape[0] // ACROSS
    for far in range(n_far):
        total = recv_ref[far].astype(f32)
        for x in range(1, ACROSS):
            total = total + recv_ref[x * n_far + far].astype(f32)
        pack(total, w_head_t_ref[...], rows_ref.at[far], send_ref, far)
    out_ref[...] = send_ref[...].astype(bf16)


def pack(total, w_head_t, rows_ref, send_ref, far):
    n_col = total.shape[0] // 2
    base = far * n_col * 4
    rows, tiles = 8, 4
    mine = total[: rows * tiles]
    group = lanes_of((1, rows, 128), 2) // 16 == lanes_of((1, rows, 128), 1)
    spread = jnp.where(group, jnp.broadcast_to(mine[:, None, :], (rows * tiles, rows, 128)), 0.0)
    folded = dot(spread.reshape(-1, 128).astype(bf16), fold_matrix(16, bf16))
    folded = folded.reshape(tiles, rows, rows, 128)
    slot = lanes_of((1, rows, 1, 128), 3) // 16 == (8 - lanes_of((1, rows, 1, 128), 1)) % 8
    part_in = jnp.sum(jnp.where(slot, folded, 0.0), axis=1).reshape(n_col, 128)
    send_ref[pl.ds(base + 0, n_col, stride=4), :] = part_in
    lane = lanes_of((1, 128), 1)
    mid = total[32:48]
    mid = jnp.concatenate([jnp.where(lane < 64, mid, 0.0), jnp.where(lane < 64, 0.0, mid)], axis=0)
    twice = jnp.concatenate([w_head_t, w_head_t], axis=0)
    high = mid.astype(bf16)
    low = (mid - high.astype(f32)).astype(bf16)
    mine = dot(high, twice) + dot(low, twice)
    rows_ref[0] = jnp.concatenate([mine] * 4, axis=0).T
    part_out = rows_ref[0, pl.ds(0, n_col, stride=4), :]
    for j in range(1, 4):
        part_out = jnp.where(
            lane // 32 == 4 - j, rows_ref[0, pl.ds(j, n_col, stride=4), :], part_out
        )
    send_ref[pl.ds(base + 1, n_col, stride=4), :] = part_out
    mine = total[48:56]
    mine = mine + pltpu.roll(mine, 64, 1)
    rows_ref[1] = jnp.concatenate([mine] * 16, axis=0).T
    part_head = jnp.where(
        lane // 8 == 15,
        rows_ref[1, pl.ds(1, n_col, stride=2), :],
        rows_ref[1, pl.ds(0, n_col, stride=2), :],
    )
    send_ref[pl.ds(base + 2, n_col, stride=4), :] = part_head
    send_ref[pl.ds(base + 3, n_col, stride=4), :] = jnp.zeros_like(part_head)


def final_kernel(scale, recv_ref, in_ref, out_t_ref, head_t_ref):
    values = recv_ref[...].astype(f32)
    total = values[0:8]
    for c in range(1, values.shape[0] // 8):
        total = total + values[c * 8 : (c + 1) * 8]
    total = (total[0:4] + total[4:8]) * scale

    def unfold(row, out):
        count, width = out.shape
        if width * 8 <= 128:
            spread = jnp.broadcast_to(row, (8, 128))
            spread = pltpu.roll(spread, 0, 1, stride=width, stride_axis=0)
        else:
            spread = jnp.concatenate(
                [pltpu.roll(row, i * width, 1) if i else row for i in range(count)], axis=0
            )
        out[...] = spread[:count, :width]

    unfold(total[0:1], in_ref)
    unfold(total[1:2], out_t_ref)
    unfold(total[2:3], head_t_ref)


ROOM = 48 * 1024 * 1024


def params(limit=62 * 1024 * 1024):
    return pltpu.CompilerParams(vmem_limit_bytes=limit)


def in_hbm(array):
    return pltpu.with_memory_space_constraint(array, pltpu.HBM)


def forward_call(pair_rep, w_in, w_out, w_head_t, n_row, n_col):
    row_count, col_count, channels = pair_rep.shape
    return pl.pallas_call(
        send_kernel,
        out_shape=jax.ShapeDtypeStruct((n_row, CYCLES * n_col, channels), jnp.int16),
        scratch_shapes=[pltpu.VMEM((CYCLES * n_col * n_row, channels), jnp.int32)],
        compiler_params=params(),
        name="forward",
    )(pair_rep.reshape(CYCLES, n_col, col_count, channels), w_in, w_out, w_head_t)


HERE = pl.BlockSpec()
THERE = pl.BlockSpec(memory_space=pl.ANY)


def prepare_call(pair_rep, true_bins, w_in, w_out, w_head_t, n_row, n_col):
    row_count, col_count, channels = pair_rep.shape
    pairs = row_count * col_count
    hidden_count = w_in.shape[1]
    away = [
        jax.ShapeDtypeStruct((pairs, hidden_count), bf16),
        jax.ShapeDtypeStruct((channels, pairs), bf16),
        jax.ShapeDtypeStruct((channels, pairs), bf16),
    ]
    results = pl.pallas_call(
        prepare_kernel,
        in_specs=[HERE] * 5,
        out_specs=[HERE] * 4 + [pl.BlockSpec(memory_space=pltpu.HBM)] * 3,
        out_shape=[
            jax.ShapeDtypeStruct((pairs, hidden_count), bf16),
            jax.ShapeDtypeStruct((pairs // CYCLES, channels), f32),
            jax.ShapeDtypeStruct((n_col, CYCLES, n_row, channels), bf16),
            jax.ShapeDtypeStruct((channels, hidden_count), bf16),
            *away,
        ],
        scratch_shapes=[pltpu.VMEM(x.shape, x.dtype) for x in away[1:]]
        + [
            pltpu.VMEM((CYCLES, n_col, CYCLES, n_row, channels), f32),
            pltpu.SemaphoreType.DMA((len(away),)),
        ],
        compiler_params=params(ROOM),
        cost_estimate=pl.CostEstimate(
            flops=2 * pairs * 2 * channels * hidden_count, bytes_accessed=8 * 2**20, transcendentals=0
        ),
        name="prepare",
    )(
        in_hbm(pair_rep.reshape(CYCLES, n_col, col_count, channels)),
        true_bins.reshape(CYCLES, n_col, col_count),
        in_hbm(w_in),
        in_hbm(w_out),
        in_hbm(w_head_t),
    )
    return results[:4], [in_hbm(x) for x in results[4:]]


def weights_call(recv, near, normed_t, residual_t, w_head_t):
    logits, bins_wide, hidden, w_out_t = near
    n_row, span, channels = recv.shape
    pairs, hidden_count = hidden.shape
    part_rows = 2 * (hidden_count // n_row)
    d_logit = jax.ShapeDtypeStruct((pairs // CYCLES, channels), bf16)
    late = (normed_t, residual_t)
    return pl.pallas_call(
        weights_kernel,
        in_specs=[HERE] * 5 + [THERE] * 2 + [HERE],
        out_specs=[HERE, HERE],
        out_shape=[d_logit, jax.ShapeDtypeStruct((n_row, part_rows, channels), bf16)],
        scratch_shapes=[pltpu.VMEM(x.shape, x.dtype) for x in late]
        + [
            pltpu.VMEM((pairs // CYCLES, channels), f32),
            pltpu.SemaphoreType.DMA((len(late),)),
        ],
        compiler_params=params(ROOM),
        name="weights",
    )(recv, logits, bins_wide, hidden, w_out_t, normed_t, residual_t, w_head_t)


def pair_call(d_logit, hidden, pair_rep, w_in, w_out, w_head_t, n_row, n_col):
    row_count, col_count, channels = pair_rep.shape
    pairs, hidden_count = hidden.shape
    cycled = pair_rep.reshape(CYCLES, n_col, col_count, channels)
    return pl.pallas_call(
        pair_kernel,
        out_shape=jax.ShapeDtypeStruct(cycled.shape, bf16),
        scratch_shapes=[pltpu.VMEM((CYCLES, n_col, CYCLES, n_row, channels), f32)],
        compiler_params=params(ROOM),
        cost_estimate=pl.CostEstimate(
            flops=2 * pairs * 2 * channels * hidden_count, bytes_accessed=5 * 2**20, transcendentals=0
        ),
        name="pair",
    )(d_logit, *[in_hbm(x) for x in (hidden, cycled, w_in, w_out, w_head_t)])


def middle_call(part, w_head_t, n_col):
    n_far = part.shape[0] // ACROSS
    shape = (n_far * n_col * 4, part.shape[-1])
    return pl.pallas_call(
        middle_kernel,
        out_shape=jax.ShapeDtypeStruct(shape, bf16),
        scratch_shapes=[pltpu.VMEM((n_far, 2, 128, 128), f32), pltpu.VMEM(shape, f32)],
        compiler_params=params(ROOM),
        name="sum_x",
    )(part, w_head_t)


def final_call(share, scale, shapes):
    return pl.pallas_call(
        functools.partial(final_kernel, scale),
        out_shape=[jax.ShapeDtypeStruct(shape, f32) for shape in shapes],
        compiler_params=params(ROOM),
        name="sum_rest",
    )(share)


def shards(pair_rep, true_bins, w_in, w_out, w_head):
    row_count, col_count, channels = pair_rep.shape
    n_row = lax.axis_size("row")
    n_col = lax.axis_size("col")
    hidden_count = w_in.shape[1]
    bins_count = w_head.shape[1]
    w_head_t = w_head.T

    send = forward_call(pair_rep, w_in, w_out, w_head_t, n_row, n_col)
    recv = lax.all_to_all(
        send.reshape(n_row * n_col, CYCLES, channels),
        ("row", "col"),
        split_axis=0,
        concat_axis=0,
        tiled=True,
    ).reshape(n_row, CYCLES * n_col, channels)
    (hidden, logits, bins_wide, w_out_t), (hidden_far, normed_t, residual_t) = (
        prepare_call(pair_rep, true_bins, w_in, w_out, w_head_t, n_row, n_col)
    )
    d_logit, part = weights_call(
        recv, (logits, bins_wide, hidden, w_out_t), normed_t, residual_t, w_head_t
    )
    n_far = n_row // ACROSS
    part = lax.all_to_all(
        part,
        "row",
        split_axis=0,
        concat_axis=0,
        tiled=True,
        axis_index_groups=[[far * ACROSS + x for x in range(ACROSS)] for far in range(n_far)],
    )
    share = middle_call(part, w_head_t, n_col)
    share = lax.all_to_all(
        share.reshape(n_far * n_col, 4, channels),
        ("row", "col"),
        split_axis=0,
        concat_axis=0,
        tiled=True,
        axis_index_groups=[
            [(far * ACROSS + x) * n_col + c for far in range(n_far) for c in range(n_col)]
            for x in range(ACROSS)
        ],
    ).reshape(n_far * n_col * 4, channels)
    d_pair = pair_call(d_logit, hidden_far, pair_rep, w_in, w_out, w_head_t, n_row, n_col)
    grad_in, grad_out_t, grad_head_t = final_call(
        share,
        1.0 / (row_count * n_row),
        [
            (channels // n_row, hidden_count // n_col),
            (channels // n_col, hidden_count // n_row),
            (bins_count // n_col, channels // n_row),
        ],
    )
    return (
        d_pair.reshape(row_count, col_count, channels),
        grad_in,
        grad_out_t.T,
        grad_head_t.T,
    )


def solution(mesh):
    placed = (P("row", "col", None), P("row", "col"), P(), P(), P())
    return jax.shard_map(
        shards,
        mesh=mesh,
        in_specs=placed,
        out_specs=(P("row", "col", None), P("row", "col"), P("row", "col"), P("row", "col")),
        check_vma=False,
    )
```

```python
import functools

import jax
import jax.numpy as jnp
from jax import lax
from jax.experimental import pallas as pl
from jax.experimental.pallas import tpu as pltpu
from jax.sharding import PartitionSpec as P

epsilon = 1e-05
f32 = jnp.float32
bf16 = jnp.bfloat16

code_steps = 2350.0

CYCLES = 2

ACROSS = 4


def dot(first, second):
    return jnp.dot(first, second, preferred_element_type=f32)


def dot_t(first, second):
    return lax.dot_general(first, second, (((1,), (1,)), ((), ())), preferred_element_type=f32)


def widen(w_head_t):
    blank = jnp.zeros_like(w_head_t)
    return jnp.concatenate(
        [
            jnp.concatenate([w_head_t, blank], axis=1),
            jnp.concatenate([blank, w_head_t], axis=1),
        ],
        axis=0,
    )


def encode(values):
    size = jnp.log(1.0 + jnp.abs(values)) * code_steps + 0.5
    return jnp.where(values < 0.0, -size, size).astype(jnp.int32)


def decode(codes):
    codes = codes.astype(f32)
    size = jnp.exp(jnp.abs(codes) * (1.0 / code_steps)) - 1.0
    return jnp.where(codes < 0.0, -size, size)


def normalize(values):
    centred = values - jnp.mean(values, axis=-1, keepdims=True)
    variance = jnp.mean(centred * centred, axis=-1, keepdims=True)
    inv_std = lax.rsqrt(variance + epsilon)
    return (centred * inv_std, inv_std)


def send_kernel(pair_ref, w_in_ref, w_out_ref, w_head_t_ref, send_ref, rows_ref):
    n_row = send_ref.shape[0]
    span = send_ref.shape[1]
    channels = pair_ref.shape[-1]
    values = pair_ref[...].reshape(-1, channels).astype(f32)
    half = values.shape[0] // CYCLES
    x_hat, _ = normalize(values)
    hidden = jnp.maximum(dot(x_hat.astype(bf16), w_in_ref[...]), 0.0).astype(bf16)
    residual = (values + dot(hidden, w_out_ref[...])).astype(bf16)
    wide = jnp.concatenate([residual[:half], residual[half:]], axis=1)
    rows_ref[...] = encode(dot_t(wide, widen(w_head_t_ref[...])))
    for r in range(n_row):
        send_ref[r] = rows_ref[pl.ds(r, span, stride=n_row), :].astype(jnp.int16)


def prepare_kernel(
    pair_ref,
    bins_ref,
    w_in_ref,
    w_out_ref,
    w_head_t_ref,
    hidden_ref,
    logits_ref,
    bins_wide_ref,
    w_out_t_ref,
    hidden_hbm,
    normed_t_hbm,
    residual_t_hbm,
    normed_t_ref,
    residual_t_ref,
    values_ref,
    sems,
):
    kept = (
        (hidden_ref, hidden_hbm),
        (normed_t_ref, normed_t_hbm),
        (residual_t_ref, residual_t_hbm),
    )
    copies = [
        pltpu.make_async_copy(source, target, sems.at[i])
        for i, (source, target) in enumerate(kept)
    ]
    channels = pair_ref.shape[-1]
    n_row = pair_ref.shape[2] // CYCLES
    count = pair_ref.shape[1]
    for a in range(CYCLES):
        for b in range(CYCLES):
            values_ref[a, :, b] = pair_ref[b, :, a * n_row : (a + 1) * n_row, :].astype(f32)
    values = values_ref[...].reshape(-1, channels)
    half = values.shape[0] // CYCLES
    x_hat, _ = normalize(values)
    normed = x_hat.astype(bf16)
    hidden = jnp.maximum(dot(normed, w_in_ref[...]), 0.0).astype(bf16)
    residual = (values + dot(hidden, w_out_ref[...])).astype(bf16)
    hidden_ref[...] = hidden
    w_out_t_ref[...] = w_out_ref[...].T
    normed_t_ref[...] = normed.T
    residual_t_ref[...] = residual.T
    logits_ref[...] = dot_t(
        jnp.concatenate([residual[:half], residual[half:]], axis=1), widen(w_head_t_ref[...])
    )
    for copy in copies:
        copy.start()
    columns = bins_ref.shape[-1]
    row_of = lax.broadcasted_iota(jnp.int32, (1, n_row, columns), 1)
    column_of = lax.broadcasted_iota(jnp.int32, (1, n_row, columns), 2)
    own = column_of % n_row == row_of
    lane = lax.broadcasted_iota(jnp.int32, (columns, channels), 1)
    source = lax.broadcasted_iota(jnp.int32, (columns, channels), 0)
    spread = (lane // (channels // CYCLES) == source // n_row).astype(f32).astype(bf16)
    for b in range(CYCLES):
        bins = bins_ref[b].astype(f32)
        picked = jnp.where(own, jnp.broadcast_to(bins[:, None, :], (count, n_row, columns)), 0.0)
        wide = dot(picked.reshape(count * n_row, columns).astype(bf16), spread)
        bins_wide_ref[:, b] = wide.astype(bf16).reshape(count, n_row, channels)
    for copy in copies:
        copy.wait()


def weights_kernel(
    recv_ref,
    logits_ref,
    bins_wide_ref,
    hidden_ref,
    w_out_t_ref,
    normed_t_hbm,
    residual_t_hbm,
    w_head_t_ref,
    d_logit_ref,
    part_ref,
    normed_t_ref,
    residual_t_ref,
    rows_ref,
    sems,
):
    n_row, span, channels = recv_ref.shape
    bins_count = channels // CYCLES
    half = span * n_row
    copies = [
        pltpu.make_async_copy(source, target, sems.at[i])
        for i, (source, target) in enumerate(
            ((normed_t_hbm, normed_t_ref), (residual_t_hbm, residual_t_ref))
        )
    ]
    for copy in copies:
        copy.start()

    for r in range(n_row):
        rows_ref[pl.ds(r, span, stride=n_row), :] = decode(recv_ref[r])
    sym = logits_ref[...] + rows_ref[...]
    lane = lax.broadcasted_iota(jnp.int32, (1, channels), 1)
    left = lane < bins_count
    low = jnp.max(jnp.where(left, sym, -jnp.inf), axis=-1, keepdims=True)
    high = jnp.max(jnp.where(left, -jnp.inf, sym), axis=-1, keepdims=True)
    grown = jnp.exp(sym - jnp.where(left, low, high))
    low = jnp.sum(jnp.where(left, grown, 0.0), axis=-1, keepdims=True)
    high = jnp.sum(jnp.where(left, 0.0, grown), axis=-1, keepdims=True)
    probability = grown / jnp.where(left, low, high)
    own_bin = (lane % bins_count).astype(f32)
    bins = bins_wide_ref[...].reshape(half, channels).astype(f32)
    d_sym = probability - jnp.where(bins == own_bin, 1.0, 0.0)
    d_logit = (d_sym + d_sym).astype(bf16)
    d_logit_ref[...] = d_logit

    d_update = pair_gradient(d_logit, w_head_t_ref[...]).astype(bf16)
    hidden = hidden_ref[...]
    d_hidden = hidden_gradient(dot(d_update, w_out_t_ref[...]), hidden)
    for copy in copies:
        copy.wait()
    g_head = jnp.where(
        left,
        dot(residual_t_ref[:, :half], d_logit),
        dot(residual_t_ref[:, half:], d_logit),
    )
    g_in = dot(normed_t_ref[...], d_hidden)
    d_logit_t = d_logit.T
    g_mid = (
        dot(d_logit_t, hidden[:half])[:bins_count] + dot(d_logit_t, hidden[half:])[bins_count:]
    )
    rows = channels // n_row
    tiles = hidden.shape[1] // channels
    long = tiles * rows
    paired = jnp.concatenate([g_mid, jnp.roll(g_mid, -long // 2, axis=1)], axis=0).T
    for r in range(n_row):
        slot = r % ACROSS * (n_row // ACROSS) + r // ACROSS
        mine = g_in[r * rows : (r + 1) * rows, :]
        part_ref[slot, 0:long, :] = jnp.concatenate(
            [mine[:, t * channels : (t + 1) * channels] for t in range(tiles)], axis=0
        ).astype(bf16)
        part_ref[slot, long : long + long // 2, :] = paired[
            r * long : r * long + long // 2, :
        ].astype(bf16)
        mine = g_head[r * rows : (r + 1) * rows, :]
        part_ref[slot, long + long // 2 :, :] = jnp.concatenate(
            [mine, jnp.zeros_like(mine)], axis=0
        ).astype(bf16)


def pair_gradient(d_logit, w_head_t):
    wide = dot(d_logit, widen(w_head_t))
    channels = wide.shape[1] // CYCLES
    return jnp.concatenate([wide[:, :channels], wide[:, channels:]], axis=0)


def hidden_gradient(back, hidden):
    back = back.astype(bf16)
    return jnp.where(hidden > 0, back, jnp.zeros_like(back))


def pair_kernel(
    d_logit_ref, hidden_ref, pair_ref, w_in_ref, w_out_ref, w_head_t_ref, grad_ref, values_ref
):
    channels = grad_ref.shape[-1]
    count = grad_ref.shape[1]
    n_row = grad_ref.shape[2] // CYCLES
    d_resid = pair_gradient(d_logit_ref[...], w_head_t_ref[...])
    d_hidden = hidden_gradient(dot_t(d_resid.astype(bf16), w_out_ref[...]), hidden_ref[...])
    d_normed = dot_t(d_hidden, w_in_ref[...])
    for a in range(CYCLES):
        for b in range(CYCLES):
            values_ref[a, :, b] = pair_ref[b, :, a * n_row : (a + 1) * n_row, :].astype(f32)
    x_hat, inv_std = normalize(values_ref[...].reshape(-1, channels))
    first_mean = jnp.mean(d_normed, axis=-1, keepdims=True)
    second_mean = jnp.mean(d_normed * x_hat, axis=-1, keepdims=True)
    d_pair = d_resid + inv_std * (d_normed - first_mean - x_hat * second_mean)
    d_pair = d_pair.astype(bf16).reshape(CYCLES, count, CYCLES, n_row, channels)
    for a in range(CYCLES):
        for b in range(CYCLES):
            grad_ref[b, :, a * n_row : (a + 1) * n_row, :] = d_pair[a, :, b]


def lanes_of(shape, axis):
    return lax.broadcasted_iota(jnp.int32, shape, axis)


def fold_matrix(width, kind):
    shape = (128, 128)
    return (lanes_of(shape, 0) % width == lanes_of(shape, 1) % width).astype(f32).astype(kind)


def middle_kernel(recv_ref, w_head_t_ref, out_ref, rows_ref, send_ref):
    n_far = recv_ref.shape[0] // ACROSS
    for far in range(n_far):
        total = recv_ref[far].astype(f32)
        for x in range(1, ACROSS):
            total = total + recv_ref[x * n_far + far].astype(f32)
        pack(total, w_head_t_ref[...], rows_ref.at[far], send_ref, far)
    out_ref[...] = send_ref[...].astype(bf16)


def pack(total, w_head_t, rows_ref, send_ref, far):
    n_col = total.shape[0] // 2
    base = far * n_col * 4
    rows, tiles = 8, 4
    mine = total[: rows * tiles]
    group = lanes_of((1, rows, 128), 2) // 16 == lanes_of((1, rows, 128), 1)
    spread = jnp.where(group, jnp.broadcast_to(mine[:, None, :], (rows * tiles, rows, 128)), 0.0)
    folded = dot(spread.reshape(-1, 128).astype(bf16), fold_matrix(16, bf16))
    folded = folded.reshape(tiles, rows, rows, 128)
    slot = lanes_of((1, rows, 1, 128), 3) // 16 == (8 - lanes_of((1, rows, 1, 128), 1)) % 8
    part_in = jnp.sum(jnp.where(slot, folded, 0.0), axis=1).reshape(n_col, 128)
    send_ref[pl.ds(base + 0, n_col, stride=4), :] = part_in
    lane = lanes_of((1, 128), 1)
    mid = total[32:48]
    mid = jnp.concatenate([jnp.where(lane < 64, mid, 0.0), jnp.where(lane < 64, 0.0, mid)], axis=0)
    twice = jnp.concatenate([w_head_t, w_head_t], axis=0)
    high = mid.astype(bf16)
    low = (mid - high.astype(f32)).astype(bf16)
    mine = dot(high, twice) + dot(low, twice)
    rows_ref[0] = jnp.concatenate([mine] * 4, axis=0).T
    part_out = rows_ref[0, pl.ds(0, n_col, stride=4), :]
    for j in range(1, 4):
        part_out = jnp.where(
            lane // 32 == 4 - j, rows_ref[0, pl.ds(j, n_col, stride=4), :], part_out
        )
    send_ref[pl.ds(base + 1, n_col, stride=4), :] = part_out
    mine = total[48:56]
    mine = mine + pltpu.roll(mine, 64, 1)
    rows_ref[1] = jnp.concatenate([mine] * 16, axis=0).T
    part_head = jnp.where(
        lane // 8 == 15,
        rows_ref[1, pl.ds(1, n_col, stride=2), :],
        rows_ref[1, pl.ds(0, n_col, stride=2), :],
    )
    send_ref[pl.ds(base + 2, n_col, stride=4), :] = part_head
    send_ref[pl.ds(base + 3, n_col, stride=4), :] = jnp.zeros_like(part_head)


def final_kernel(scale, recv_ref, in_ref, out_t_ref, head_t_ref):
    values = recv_ref[...].astype(f32)
    total = values[0:8]
    for c in range(1, values.shape[0] // 8):
        total = total + values[c * 8 : (c + 1) * 8]
    total = (total[0:4] + total[4:8]) * scale

    def unfold(row, out):
        count, width = out.shape
        if width * 8 <= 128:
            spread = jnp.broadcast_to(row, (8, 128))
            spread = pltpu.roll(spread, 0, 1, stride=width, stride_axis=0)
        else:
            spread = jnp.concatenate(
                [pltpu.roll(row, i * width, 1) if i else row for i in range(count)], axis=0
            )
        out[...] = spread[:count, :width]

    unfold(total[0:1], in_ref)
    unfold(total[1:2], out_t_ref)
    unfold(total[2:3], head_t_ref)


ROOM = 48 * 1024 * 1024


def params(limit=62 * 1024 * 1024):
    return pltpu.CompilerParams(vmem_limit_bytes=limit)


def in_hbm(array):
    return pltpu.with_memory_space_constraint(array, pltpu.HBM)


def forward_call(pair_rep, w_in, w_out, w_head_t, n_row, n_col):
    row_count, col_count, channels = pair_rep.shape
    return pl.pallas_call(
        send_kernel,
        out_shape=jax.ShapeDtypeStruct((n_row, CYCLES * n_col, channels), jnp.int16),
        scratch_shapes=[pltpu.VMEM((CYCLES * n_col * n_row, channels), jnp.int32)],
        compiler_params=params(),
        name="forward",
    )(pair_rep.reshape(CYCLES, n_col, col_count, channels), w_in, w_out, w_head_t)


HERE = pl.BlockSpec()
THERE = pl.BlockSpec(memory_space=pl.ANY)


def prepare_call(pair_rep, true_bins, w_in, w_out, w_head_t, n_row, n_col):
    row_count, col_count, channels = pair_rep.shape
    pairs = row_count * col_count
    hidden_count = w_in.shape[1]
    away = [
        jax.ShapeDtypeStruct((pairs, hidden_count), bf16),
        jax.ShapeDtypeStruct((channels, pairs), bf16),
        jax.ShapeDtypeStruct((channels, pairs), bf16),
    ]
    results = pl.pallas_call(
        prepare_kernel,
        in_specs=[HERE] * 5,
        out_specs=[HERE] * 4 + [pl.BlockSpec(memory_space=pltpu.HBM)] * 3,
        out_shape=[
            jax.ShapeDtypeStruct((pairs, hidden_count), bf16),
            jax.ShapeDtypeStruct((pairs // CYCLES, channels), f32),
            jax.ShapeDtypeStruct((n_col, CYCLES, n_row, channels), bf16),
            jax.ShapeDtypeStruct((channels, hidden_count), bf16),
            *away,
        ],
        scratch_shapes=[pltpu.VMEM(x.shape, x.dtype) for x in away[1:]]
        + [
            pltpu.VMEM((CYCLES, n_col, CYCLES, n_row, channels), f32),
            pltpu.SemaphoreType.DMA((len(away),)),
        ],
        compiler_params=params(ROOM),
        cost_estimate=pl.CostEstimate(
            flops=2 * pairs * 2 * channels * hidden_count, bytes_accessed=8 * 2**20, transcendentals=0
        ),
        name="prepare",
    )(
        in_hbm(pair_rep.reshape(CYCLES, n_col, col_count, channels)),
        true_bins.reshape(CYCLES, n_col, col_count),
        in_hbm(w_in),
        in_hbm(w_out),
        in_hbm(w_head_t),
    )
    return results[:4], [in_hbm(x) for x in results[4:]]


def weights_call(recv, near, normed_t, residual_t, w_head_t):
    logits, bins_wide, hidden, w_out_t = near
    n_row, span, channels = recv.shape
    pairs, hidden_count = hidden.shape
    part_rows = 2 * (hidden_count // n_row)
    d_logit = jax.ShapeDtypeStruct((pairs // CYCLES, channels), bf16)
    late = (normed_t, residual_t)
    return pl.pallas_call(
        weights_kernel,
        in_specs=[HERE] * 5 + [THERE] * 2 + [HERE],
        out_specs=[HERE, HERE],
        out_shape=[d_logit, jax.ShapeDtypeStruct((n_row, part_rows, channels), bf16)],
        scratch_shapes=[pltpu.VMEM(x.shape, x.dtype) for x in late]
        + [
            pltpu.VMEM((pairs // CYCLES, channels), f32),
            pltpu.SemaphoreType.DMA((len(late),)),
        ],
        compiler_params=params(ROOM),
        name="weights",
    )(recv, logits, bins_wide, hidden, w_out_t, normed_t, residual_t, w_head_t)


def pair_call(d_logit, hidden, pair_rep, w_in, w_out, w_head_t, n_row, n_col):
    row_count, col_count, channels = pair_rep.shape
    pairs, hidden_count = hidden.shape
    cycled = pair_rep.reshape(CYCLES, n_col, col_count, channels)
    return pl.pallas_call(
        pair_kernel,
        out_shape=jax.ShapeDtypeStruct(cycled.shape, bf16),
        scratch_shapes=[pltpu.VMEM((CYCLES, n_col, CYCLES, n_row, channels), f32)],
        compiler_params=params(ROOM),
        cost_estimate=pl.CostEstimate(
            flops=2 * pairs * 2 * channels * hidden_count, bytes_accessed=5 * 2**20, transcendentals=0
        ),
        name="pair",
    )(d_logit, *[in_hbm(x) for x in (hidden, cycled, w_in, w_out, w_head_t)])


def middle_call(part, w_head_t, done, n_col):
    part, _ = lax.optimization_barrier((part, done))
    n_far = part.shape[0] // ACROSS
    shape = (n_far * n_col * 4, part.shape[-1])
    return pl.pallas_call(
        middle_kernel,
        out_shape=jax.ShapeDtypeStruct(shape, bf16),
        scratch_shapes=[pltpu.VMEM((n_far, 2, 128, 128), f32), pltpu.VMEM(shape, f32)],
        compiler_params=params(ROOM),
        name="sum_x",
    )(part, w_head_t)


def final_call(share, scale, shapes):
    return pl.pallas_call(
        functools.partial(final_kernel, scale),
        out_shape=[jax.ShapeDtypeStruct(shape, f32) for shape in shapes],
        compiler_params=params(ROOM),
        name="sum_rest",
    )(share)


def shards(pair_rep, true_bins, w_in, w_out, w_head):
    row_count, col_count, channels = pair_rep.shape
    n_row = lax.axis_size("row")
    n_col = lax.axis_size("col")
    hidden_count = w_in.shape[1]
    bins_count = w_head.shape[1]
    w_head_t = w_head.T

    send = forward_call(pair_rep, w_in, w_out, w_head_t, n_row, n_col)
    recv = lax.all_to_all(
        send.reshape(n_row * n_col, CYCLES, channels),
        ("row", "col"),
        split_axis=0,
        concat_axis=0,
        tiled=True,
    ).reshape(n_row, CYCLES * n_col, channels)
    (hidden, logits, bins_wide, w_out_t), (hidden_far, normed_t, residual_t) = (
        prepare_call(pair_rep, true_bins, w_in, w_out, w_head_t, n_row, n_col)
    )
    d_logit, part = weights_call(
        recv, (logits, bins_wide, hidden, w_out_t), normed_t, residual_t, w_head_t
    )
    n_far = n_row // ACROSS
    part = lax.all_to_all(
        part,
        "row",
        split_axis=0,
        concat_axis=0,
        tiled=True,
        axis_index_groups=[[far * ACROSS + x for x in range(ACROSS)] for far in range(n_far)],
    )
    d_pair = pair_call(d_logit, hidden_far, pair_rep, w_in, w_out, w_head_t, n_row, n_col)
    share = middle_call(part, w_head_t, d_pair, n_col)
    share = lax.all_to_all(
        share.reshape(n_far * n_col, 4, channels),
        ("row", "col"),
        split_axis=0,
        concat_axis=0,
        tiled=True,
        axis_index_groups=[
            [(far * ACROSS + x) * n_col + c for far in range(n_far) for c in range(n_col)]
            for x in range(ACROSS)
        ],
    ).reshape(n_far * n_col * 4, channels)
    grad_in, grad_out_t, grad_head_t = final_call(
        share,
        1.0 / (row_count * n_row),
        [
            (channels // n_row, hidden_count // n_col),
            (channels // n_col, hidden_count // n_row),
            (bins_count // n_col, channels // n_row),
        ],
    )
    return (
        d_pair.reshape(row_count, col_count, channels),
        grad_in,
        grad_out_t.T,
        grad_head_t.T,
    )


def solution(mesh):
    placed = (P("row", "col", None), P("row", "col"), P(), P(), P())
    return jax.shard_map(
        shards,
        mesh=mesh,
        in_specs=placed,
        out_specs=(P("row", "col", None), P("row", "col"), P("row", "col"), P("row", "col")),
        check_vma=False,
    )
```

```python
import functools

import jax
import jax.numpy as jnp
from jax import lax
from jax.experimental import pallas as pl
from jax.experimental.pallas import tpu as pltpu
from jax.sharding import PartitionSpec as P

epsilon = 1e-05
f32 = jnp.float32
bf16 = jnp.bfloat16

code_steps = 2350.0

CYCLES = 2

ACROSS = 4


def dot(first, second):
    return jnp.dot(first, second, preferred_element_type=f32)


def dot_t(first, second):
    return lax.dot_general(first, second, (((1,), (1,)), ((), ())), preferred_element_type=f32)


def widen(w_head_t):
    blank = jnp.zeros_like(w_head_t)
    return jnp.concatenate(
        [
            jnp.concatenate([w_head_t, blank], axis=1),
            jnp.concatenate([blank, w_head_t], axis=1),
        ],
        axis=0,
    )


def encode(values):
    size = jnp.log(1.0 + jnp.abs(values)) * code_steps + 0.5
    return jnp.where(values < 0.0, -size, size).astype(jnp.int32)


def decode(codes):
    codes = codes.astype(f32)
    size = jnp.exp(jnp.abs(codes) * (1.0 / code_steps)) - 1.0
    return jnp.where(codes < 0.0, -size, size)


def normalize(values):
    centred = values - jnp.mean(values, axis=-1, keepdims=True)
    variance = jnp.mean(centred * centred, axis=-1, keepdims=True)
    inv_std = lax.rsqrt(variance + epsilon)
    return (centred * inv_std, inv_std)


def send_kernel(pair_ref, w_in_ref, w_out_ref, w_head_t_ref, send_ref, rows_ref):
    n_row = send_ref.shape[0]
    span = send_ref.shape[1]
    channels = pair_ref.shape[-1]
    values = pair_ref[...].reshape(-1, channels).astype(f32)
    half = values.shape[0] // CYCLES
    x_hat, _ = normalize(values)
    hidden = jnp.maximum(dot(x_hat.astype(bf16), w_in_ref[...]), 0.0).astype(bf16)
    residual = (values + dot(hidden, w_out_ref[...])).astype(bf16)
    wide = jnp.concatenate([residual[:half], residual[half:]], axis=1)
    rows_ref[...] = encode(dot_t(wide, widen(w_head_t_ref[...])))
    for r in range(n_row):
        send_ref[r] = rows_ref[pl.ds(r, span, stride=n_row), :].astype(jnp.int16)


def prepare_kernel(
    pair_ref,
    bins_ref,
    w_in_ref,
    w_out_ref,
    w_head_t_ref,
    hidden_ref,
    logits_ref,
    bins_wide_ref,
    w_out_t_ref,
    normed_t_hbm,
    residual_t_hbm,
    normed_t_ref,
    residual_t_ref,
    values_ref,
    sems,
):
    kept = (
        (normed_t_ref, normed_t_hbm),
        (residual_t_ref, residual_t_hbm),
    )
    copies = [
        pltpu.make_async_copy(source, target, sems.at[i])
        for i, (source, target) in enumerate(kept)
    ]
    channels = pair_ref.shape[-1]
    n_row = pair_ref.shape[2] // CYCLES
    count = pair_ref.shape[1]
    for a in range(CYCLES):
        for b in range(CYCLES):
            values_ref[a, :, b] = pair_ref[b, :, a * n_row : (a + 1) * n_row, :].astype(f32)
    values = values_ref[...].reshape(-1, channels)
    half = values.shape[0] // CYCLES
    x_hat, _ = normalize(values)
    normed = x_hat.astype(bf16)
    hidden = jnp.maximum(dot(normed, w_in_ref[...]), 0.0).astype(bf16)
    residual = (values + dot(hidden, w_out_ref[...])).astype(bf16)
    hidden_ref[...] = hidden
    w_out_t_ref[...] = w_out_ref[...].T
    normed_t_ref[...] = normed.T
    residual_t_ref[...] = residual.T
    logits_ref[...] = dot_t(
        jnp.concatenate([residual[:half], residual[half:]], axis=1), widen(w_head_t_ref[...])
    )
    for copy in copies:
        copy.start()
    columns = bins_ref.shape[-1]
    row_of = lax.broadcasted_iota(jnp.int32, (1, n_row, columns), 1)
    column_of = lax.broadcasted_iota(jnp.int32, (1, n_row, columns), 2)
    own = column_of % n_row == row_of
    lane = lax.broadcasted_iota(jnp.int32, (columns, channels), 1)
    source = lax.broadcasted_iota(jnp.int32, (columns, channels), 0)
    spread = (lane // (channels // CYCLES) == source // n_row).astype(f32).astype(bf16)
    for b in range(CYCLES):
        bins = bins_ref[b].astype(f32)
        picked = jnp.where(own, jnp.broadcast_to(bins[:, None, :], (count, n_row, columns)), 0.0)
        wide = dot(picked.reshape(count * n_row, columns).astype(bf16), spread)
        bins_wide_ref[:, b] = wide.astype(bf16).reshape(count, n_row, channels)
    for copy in copies:
        copy.wait()


def weights_kernel(
    recv_ref,
    logits_ref,
    bins_wide_ref,
    hidden_ref,
    w_out_t_ref,
    normed_t_hbm,
    residual_t_hbm,
    w_head_t_ref,
    d_logit_ref,
    part_ref,
    normed_t_ref,
    residual_t_ref,
    rows_ref,
    sems,
):
    n_row, span, channels = recv_ref.shape
    bins_count = channels // CYCLES
    half = span * n_row
    copies = [
        pltpu.make_async_copy(source, target, sems.at[i])
        for i, (source, target) in enumerate(
            ((normed_t_hbm, normed_t_ref), (residual_t_hbm, residual_t_ref))
        )
    ]
    for copy in copies:
        copy.start()

    for r in range(n_row):
        rows_ref[pl.ds(r, span, stride=n_row), :] = decode(recv_ref[r])
    sym = logits_ref[...] + rows_ref[...]
    lane = lax.broadcasted_iota(jnp.int32, (1, channels), 1)
    left = lane < bins_count
    low = jnp.max(jnp.where(left, sym, -jnp.inf), axis=-1, keepdims=True)
    high = jnp.max(jnp.where(left, -jnp.inf, sym), axis=-1, keepdims=True)
    grown = jnp.exp(sym - jnp.where(left, low, high))
    low = jnp.sum(jnp.where(left, grown, 0.0), axis=-1, keepdims=True)
    high = jnp.sum(jnp.where(left, 0.0, grown), axis=-1, keepdims=True)
    probability = grown / jnp.where(left, low, high)
    own_bin = (lane % bins_count).astype(f32)
    bins = bins_wide_ref[...].reshape(half, channels).astype(f32)
    d_sym = probability - jnp.where(bins == own_bin, 1.0, 0.0)
    d_logit = (d_sym + d_sym).astype(bf16)
    d_logit_ref[...] = d_logit

    d_update = pair_gradient(d_logit, w_head_t_ref[...]).astype(bf16)
    hidden = hidden_ref[...]
    d_hidden = hidden_gradient(dot(d_update, w_out_t_ref[...]), hidden)
    for copy in copies:
        copy.wait()
    g_head = jnp.where(
        left,
        dot(residual_t_ref[:, :half], d_logit),
        dot(residual_t_ref[:, half:], d_logit),
    )
    g_in = dot(normed_t_ref[...], d_hidden)
    d_logit_t = d_logit.T
    g_mid = (
        dot(d_logit_t, hidden[:half])[:bins_count] + dot(d_logit_t, hidden[half:])[bins_count:]
    )
    rows = channels // n_row
    tiles = hidden.shape[1] // channels
    long = tiles * rows
    paired = jnp.concatenate([g_mid, jnp.roll(g_mid, -long // 2, axis=1)], axis=0).T
    for r in range(n_row):
        slot = r % ACROSS * (n_row // ACROSS) + r // ACROSS
        mine = g_in[r * rows : (r + 1) * rows, :]
        part_ref[slot, 0:long, :] = jnp.concatenate(
            [mine[:, t * channels : (t + 1) * channels] for t in range(tiles)], axis=0
        ).astype(bf16)
        part_ref[slot, long : long + long // 2, :] = paired[
            r * long : r * long + long // 2, :
        ].astype(bf16)
        mine = g_head[r * rows : (r + 1) * rows, :]
        part_ref[slot, long + long // 2 :, :] = jnp.concatenate(
            [mine, jnp.zeros_like(mine)], axis=0
        ).astype(bf16)


def pair_gradient(d_logit, w_head_t):
    wide = dot(d_logit, widen(w_head_t))
    channels = wide.shape[1] // CYCLES
    return jnp.concatenate([wide[:, :channels], wide[:, channels:]], axis=0)


def hidden_gradient(back, hidden):
    back = back.astype(bf16)
    return jnp.where(hidden > 0, back, jnp.zeros_like(back))


def pair_kernel(
    d_logit_ref, hidden_ref, pair_ref, w_in_ref, w_out_ref, w_head_t_ref, grad_ref, values_ref
):
    channels = grad_ref.shape[-1]
    count = grad_ref.shape[1]
    n_row = grad_ref.shape[2] // CYCLES
    d_resid = pair_gradient(d_logit_ref[...], w_head_t_ref[...])
    d_hidden = hidden_gradient(dot_t(d_resid.astype(bf16), w_out_ref[...]), hidden_ref[...])
    d_normed = dot_t(d_hidden, w_in_ref[...])
    for a in range(CYCLES):
        for b in range(CYCLES):
            values_ref[a, :, b] = pair_ref[b, :, a * n_row : (a + 1) * n_row, :].astype(f32)
    x_hat, inv_std = normalize(values_ref[...].reshape(-1, channels))
    first_mean = jnp.mean(d_normed, axis=-1, keepdims=True)
    second_mean = jnp.mean(d_normed * x_hat, axis=-1, keepdims=True)
    d_pair = d_resid + inv_std * (d_normed - first_mean - x_hat * second_mean)
    d_pair = d_pair.astype(bf16).reshape(CYCLES, count, CYCLES, n_row, channels)
    for a in range(CYCLES):
        for b in range(CYCLES):
            grad_ref[b, :, a * n_row : (a + 1) * n_row, :] = d_pair[a, :, b]


def lanes_of(shape, axis):
    return lax.broadcasted_iota(jnp.int32, shape, axis)


def fold_matrix(width, kind):
    shape = (128, 128)
    return (lanes_of(shape, 0) % width == lanes_of(shape, 1) % width).astype(f32).astype(kind)


def middle_kernel(recv_ref, w_head_t_ref, out_ref, rows_ref, send_ref):
    n_far = recv_ref.shape[0] // ACROSS
    for far in range(n_far):
        total = recv_ref[far].astype(f32)
        for x in range(1, ACROSS):
            total = total + recv_ref[x * n_far + far].astype(f32)
        pack(total, w_head_t_ref[...], rows_ref.at[far], send_ref, far)
    out_ref[...] = send_ref[...].astype(bf16)


def pack(total, w_head_t, rows_ref, send_ref, far):
    n_col = total.shape[0] // 2
    base = far * n_col * 4
    rows, tiles = 8, 4
    mine = total[: rows * tiles]
    group = lanes_of((1, rows, 128), 2) // 16 == lanes_of((1, rows, 128), 1)
    spread = jnp.where(group, jnp.broadcast_to(mine[:, None, :], (rows * tiles, rows, 128)), 0.0)
    folded = dot(spread.reshape(-1, 128).astype(bf16), fold_matrix(16, bf16))
    folded = folded.reshape(tiles, rows, rows, 128)
    slot = lanes_of((1, rows, 1, 128), 3) // 16 == (8 - lanes_of((1, rows, 1, 128), 1)) % 8
    part_in = jnp.sum(jnp.where(slot, folded, 0.0), axis=1).reshape(n_col, 128)
    send_ref[pl.ds(base + 0, n_col, stride=4), :] = part_in
    lane = lanes_of((1, 128), 1)
    mid = total[32:48]
    mid = jnp.concatenate([jnp.where(lane < 64, mid, 0.0), jnp.where(lane < 64, 0.0, mid)], axis=0)
    twice = jnp.concatenate([w_head_t, w_head_t], axis=0)
    high = mid.astype(bf16)
    low = (mid - high.astype(f32)).astype(bf16)
    mine = dot(high, twice) + dot(low, twice)
    rows_ref[0] = jnp.concatenate([mine] * 4, axis=0).T
    part_out = rows_ref[0, pl.ds(0, n_col, stride=4), :]
    for j in range(1, 4):
        part_out = jnp.where(
            lane // 32 == 4 - j, rows_ref[0, pl.ds(j, n_col, stride=4), :], part_out
        )
    send_ref[pl.ds(base + 1, n_col, stride=4), :] = part_out
    mine = total[48:56]
    mine = mine + pltpu.roll(mine, 64, 1)
    rows_ref[1] = jnp.concatenate([mine] * 16, axis=0).T
    part_head = jnp.where(
        lane // 8 == 15,
        rows_ref[1, pl.ds(1, n_col, stride=2), :],
        rows_ref[1, pl.ds(0, n_col, stride=2), :],
    )
    send_ref[pl.ds(base + 2, n_col, stride=4), :] = part_head
    send_ref[pl.ds(base + 3, n_col, stride=4), :] = jnp.zeros_like(part_head)


def final_kernel(scale, recv_ref, in_ref, out_t_ref, head_t_ref):
    values = recv_ref[...].astype(f32)
    total = values[0:8]
    for c in range(1, values.shape[0] // 8):
        total = total + values[c * 8 : (c + 1) * 8]
    total = (total[0:4] + total[4:8]) * scale

    def unfold(row, out):
        count, width = out.shape
        if width * 8 <= 128:
            spread = jnp.broadcast_to(row, (8, 128))
            spread = pltpu.roll(spread, 0, 1, stride=width, stride_axis=0)
        else:
            spread = jnp.concatenate(
                [pltpu.roll(row, i * width, 1) if i else row for i in range(count)], axis=0
            )
        out[...] = spread[:count, :width]

    unfold(total[0:1], in_ref)
    unfold(total[1:2], out_t_ref)
    unfold(total[2:3], head_t_ref)


ROOM = 48 * 1024 * 1024


def params(limit=62 * 1024 * 1024):
    return pltpu.CompilerParams(vmem_limit_bytes=limit)


def in_hbm(array):
    return pltpu.with_memory_space_constraint(array, pltpu.HBM)


def forward_call(pair_rep, w_in, w_out, w_head_t, n_row, n_col):
    row_count, col_count, channels = pair_rep.shape
    return pl.pallas_call(
        send_kernel,
        out_shape=jax.ShapeDtypeStruct((n_row, CYCLES * n_col, channels), jnp.int16),
        scratch_shapes=[pltpu.VMEM((CYCLES * n_col * n_row, channels), jnp.int32)],
        compiler_params=params(),
        name="forward",
    )(pair_rep.reshape(CYCLES, n_col, col_count, channels), w_in, w_out, w_head_t)


HERE = pl.BlockSpec()
THERE = pl.BlockSpec(memory_space=pl.ANY)


def prepare_call(pair_rep, true_bins, w_in, w_out, w_head_t, n_row, n_col):
    row_count, col_count, channels = pair_rep.shape
    pairs = row_count * col_count
    hidden_count = w_in.shape[1]
    away = [
        jax.ShapeDtypeStruct((channels, pairs), bf16),
        jax.ShapeDtypeStruct((channels, pairs), bf16),
    ]
    results = pl.pallas_call(
        prepare_kernel,
        in_specs=[HERE] * 5,
        out_specs=[HERE] * 4 + [pl.BlockSpec(memory_space=pltpu.HBM)] * 2,
        out_shape=[
            jax.ShapeDtypeStruct((pairs, hidden_count), bf16),
            jax.ShapeDtypeStruct((pairs // CYCLES, channels), f32),
            jax.ShapeDtypeStruct((n_col, CYCLES, n_row, channels), bf16),
            jax.ShapeDtypeStruct((channels, hidden_count), bf16),
            *away,
        ],
        scratch_shapes=[pltpu.VMEM(x.shape, x.dtype) for x in away]
        + [
            pltpu.VMEM((CYCLES, n_col, CYCLES, n_row, channels), f32),
            pltpu.SemaphoreType.DMA((len(away),)),
        ],
        compiler_params=params(ROOM),
        cost_estimate=pl.CostEstimate(
            flops=2 * pairs * 2 * channels * hidden_count, bytes_accessed=8 * 2**20, transcendentals=0
        ),
        name="prepare",
    )(
        in_hbm(pair_rep.reshape(CYCLES, n_col, col_count, channels)),
        true_bins.reshape(CYCLES, n_col, col_count),
        in_hbm(w_in),
        in_hbm(w_out),
        in_hbm(w_head_t),
    )
    return results[:4], [in_hbm(x) for x in results[4:]]


def weights_call(recv, near, normed_t, residual_t, w_head_t):
    logits, bins_wide, hidden, w_out_t = near
    n_row, span, channels = recv.shape
    pairs, hidden_count = hidden.shape
    part_rows = 2 * (hidden_count // n_row)
    d_logit = jax.ShapeDtypeStruct((pairs // CYCLES, channels), bf16)
    late = (normed_t, residual_t)
    return pl.pallas_call(
        weights_kernel,
        in_specs=[HERE] * 5 + [THERE] * 2 + [HERE],
        out_specs=[HERE, HERE],
        out_shape=[d_logit, jax.ShapeDtypeStruct((n_row, part_rows, channels), bf16)],
        scratch_shapes=[pltpu.VMEM(x.shape, x.dtype) for x in late]
        + [
            pltpu.VMEM((pairs // CYCLES, channels), f32),
            pltpu.SemaphoreType.DMA((len(late),)),
        ],
        compiler_params=params(ROOM),
        name="weights",
    )(recv, logits, bins_wide, hidden, w_out_t, normed_t, residual_t, w_head_t)


def pair_call(d_logit, hidden, pair_rep, w_in, w_out, w_head_t, n_row, n_col):
    row_count, col_count, channels = pair_rep.shape
    pairs, hidden_count = hidden.shape
    cycled = pair_rep.reshape(CYCLES, n_col, col_count, channels)
    return pl.pallas_call(
        pair_kernel,
        out_shape=jax.ShapeDtypeStruct(cycled.shape, bf16),
        scratch_shapes=[pltpu.VMEM((CYCLES, n_col, CYCLES, n_row, channels), f32)],
        compiler_params=params(ROOM),
        cost_estimate=pl.CostEstimate(
            flops=2 * pairs * 2 * channels * hidden_count, bytes_accessed=5 * 2**20, transcendentals=0
        ),
        name="pair",
    )(d_logit, hidden, *[in_hbm(x) for x in (cycled, w_in, w_out, w_head_t)])


def middle_call(part, w_head_t, done, n_col):
    part, _ = lax.optimization_barrier((part, done))
    n_far = part.shape[0] // ACROSS
    shape = (n_far * n_col * 4, part.shape[-1])
    return pl.pallas_call(
        middle_kernel,
        out_shape=jax.ShapeDtypeStruct(shape, bf16),
        scratch_shapes=[pltpu.VMEM((n_far, 2, 128, 128), f32), pltpu.VMEM(shape, f32)],
        compiler_params=params(ROOM),
        name="sum_x",
    )(part, w_head_t)


def final_call(share, scale, shapes):
    return pl.pallas_call(
        functools.partial(final_kernel, scale),
        out_shape=[jax.ShapeDtypeStruct(shape, f32) for shape in shapes],
        compiler_params=params(ROOM),
        name="sum_rest",
    )(share)


def shards(pair_rep, true_bins, w_in, w_out, w_head):
    row_count, col_count, channels = pair_rep.shape
    n_row = lax.axis_size("row")
    n_col = lax.axis_size("col")
    hidden_count = w_in.shape[1]
    bins_count = w_head.shape[1]
    w_head_t = w_head.T

    send = forward_call(pair_rep, w_in, w_out, w_head_t, n_row, n_col)
    recv = lax.all_to_all(
        send.reshape(n_row * n_col, CYCLES, channels),
        ("row", "col"),
        split_axis=0,
        concat_axis=0,
        tiled=True,
    ).reshape(n_row, CYCLES * n_col, channels)
    (hidden, logits, bins_wide, w_out_t), (normed_t, residual_t) = (
        prepare_call(pair_rep, true_bins, w_in, w_out, w_head_t, n_row, n_col)
    )
    d_logit, part = weights_call(
        recv, (logits, bins_wide, hidden, w_out_t), normed_t, residual_t, w_head_t
    )
    n_far = n_row // ACROSS
    part = lax.all_to_all(
        part,
        "row",
        split_axis=0,
        concat_axis=0,
        tiled=True,
        axis_index_groups=[[far * ACROSS + x for x in range(ACROSS)] for far in range(n_far)],
    )
    d_pair = pair_call(d_logit, hidden, pair_rep, w_in, w_out, w_head_t, n_row, n_col)
    share = middle_call(part, w_head_t, d_pair, n_col)
    share = lax.all_to_all(
        share.reshape(n_far * n_col, 4, channels),
        ("row", "col"),
        split_axis=0,
        concat_axis=0,
        tiled=True,
        axis_index_groups=[
            [(far * ACROSS + x) * n_col + c for far in range(n_far) for c in range(n_col)]
            for x in range(ACROSS)
        ],
    ).reshape(n_far * n_col * 4, channels)
    grad_in, grad_out_t, grad_head_t = final_call(
        share,
        1.0 / (row_count * n_row),
        [
            (channels // n_row, hidden_count // n_col),
            (channels // n_col, hidden_count // n_row),
            (bins_count // n_col, channels // n_row),
        ],
    )
    return (
        d_pair.reshape(row_count, col_count, channels),
        grad_in,
        grad_out_t.T,
        grad_head_t.T,
    )


def solution(mesh):
    placed = (P("row", "col", None), P("row", "col"), P(), P(), P())
    return jax.shard_map(
        shards,
        mesh=mesh,
        in_specs=placed,
        out_specs=(P("row", "col", None), P("row", "col"), P("row", "col"), P("row", "col")),
        check_vma=False,
    )
```

```python
import functools

import jax
import jax.numpy as jnp
from jax import lax
from jax.experimental import pallas as pl
from jax.experimental.pallas import tpu as pltpu
from jax.sharding import PartitionSpec as P

epsilon = 1e-05
f32 = jnp.float32
bf16 = jnp.bfloat16

code_steps = 2350.0

CYCLES = 2

ACROSS = 4
HALVES = 2


def dot(first, second):
    return jnp.dot(first, second, preferred_element_type=f32)


def dot_t(first, second):
    return lax.dot_general(first, second, (((1,), (1,)), ((), ())), preferred_element_type=f32)


def widen(w_head_t):
    blank = jnp.zeros_like(w_head_t)
    return jnp.concatenate(
        [
            jnp.concatenate([w_head_t, blank], axis=1),
            jnp.concatenate([blank, w_head_t], axis=1),
        ],
        axis=0,
    )


def encode(values):
    size = jnp.log(1.0 + jnp.abs(values)) * code_steps + 0.5
    return jnp.where(values < 0.0, -size, size).astype(jnp.int32)


def decode(codes):
    codes = codes.astype(f32)
    size = jnp.exp(jnp.abs(codes) * (1.0 / code_steps)) - 1.0
    return jnp.where(codes < 0.0, -size, size)


def normalize(values):
    centred = values - jnp.mean(values, axis=-1, keepdims=True)
    variance = jnp.mean(centred * centred, axis=-1, keepdims=True)
    inv_std = lax.rsqrt(variance + epsilon)
    return (centred * inv_std, inv_std)


def send_kernel(pair_ref, w_in_ref, w_out_ref, w_head_t_ref, send_ref, rows_ref):
    n_row = send_ref.shape[0]
    span = send_ref.shape[1]
    channels = pair_ref.shape[-1]
    values = pair_ref[...].reshape(-1, channels).astype(f32)
    half = values.shape[0] // CYCLES
    x_hat, _ = normalize(values)
    hidden = jnp.maximum(dot(x_hat.astype(bf16), w_in_ref[...]), 0.0).astype(bf16)
    residual = (values + dot(hidden, w_out_ref[...])).astype(bf16)
    wide = jnp.concatenate([residual[:half], residual[half:]], axis=1)
    rows_ref[...] = encode(dot_t(wide, widen(w_head_t_ref[...])))
    for r in range(n_row):
        send_ref[r] = rows_ref[pl.ds(r, span, stride=n_row), :].astype(jnp.int16)


def prepare_kernel(
    pair_ref,
    bins_ref,
    w_in_ref,
    w_out_ref,
    w_head_t_ref,
    hidden_ref,
    logits_ref,
    bins_wide_ref,
    w_out_t_ref,
    normed_t_hbm,
    residual_t_hbm,
    normed_t_ref,
    residual_t_ref,
    values_ref,
    sems,
):
    kept = (
        (normed_t_ref, normed_t_hbm),
        (residual_t_ref, residual_t_hbm),
    )
    copies = [
        pltpu.make_async_copy(source, target, sems.at[i])
        for i, (source, target) in enumerate(kept)
    ]
    channels = pair_ref.shape[-1]
    n_row = pair_ref.shape[2] // CYCLES
    count = pair_ref.shape[1]
    for a in range(CYCLES):
        for b in range(CYCLES):
            values_ref[a, :, b] = pair_ref[b, :, a * n_row : (a + 1) * n_row, :].astype(f32)
    values = values_ref[...].reshape(-1, channels)
    half = values.shape[0] // CYCLES
    x_hat, _ = normalize(values)
    normed = x_hat.astype(bf16)
    hidden = jnp.maximum(dot(normed, w_in_ref[...]), 0.0).astype(bf16)
    residual = (values + dot(hidden, w_out_ref[...])).astype(bf16)
    hidden_ref[...] = hidden
    w_out_t_ref[...] = w_out_ref[...].T
    normed_t_ref[...] = normed.T
    residual_t_ref[...] = residual.T
    logits_ref[...] = dot_t(
        jnp.concatenate([residual[:half], residual[half:]], axis=1), widen(w_head_t_ref[...])
    )
    for copy in copies:
        copy.start()
    columns = bins_ref.shape[-1]
    row_of = lax.broadcasted_iota(jnp.int32, (1, n_row, columns), 1)
    column_of = lax.broadcasted_iota(jnp.int32, (1, n_row, columns), 2)
    own = column_of % n_row == row_of
    lane = lax.broadcasted_iota(jnp.int32, (columns, channels), 1)
    source = lax.broadcasted_iota(jnp.int32, (columns, channels), 0)
    spread = (lane // (channels // CYCLES) == source // n_row).astype(f32).astype(bf16)
    for b in range(CYCLES):
        bins = bins_ref[b].astype(f32)
        picked = jnp.where(own, jnp.broadcast_to(bins[:, None, :], (count, n_row, columns)), 0.0)
        wide = dot(picked.reshape(count * n_row, columns).astype(bf16), spread)
        bins_wide_ref[:, b] = wide.astype(bf16).reshape(count, n_row, channels)
    for copy in copies:
        copy.wait()


def weights_kernel(
    recv_ref,
    logits_ref,
    bins_wide_ref,
    hidden_ref,
    w_out_t_ref,
    normed_t_hbm,
    residual_t_hbm,
    w_head_t_ref,
    d_logit_ref,
    part_ref,
    normed_t_ref,
    residual_t_ref,
    rows_ref,
    sems,
):
    n_row, span, channels = recv_ref.shape
    bins_count = channels // CYCLES
    half = span * n_row
    copies = [
        pltpu.make_async_copy(source, target, sems.at[i])
        for i, (source, target) in enumerate(
            ((normed_t_hbm, normed_t_ref), (residual_t_hbm, residual_t_ref))
        )
    ]
    for copy in copies:
        copy.start()

    for r in range(n_row):
        rows_ref[pl.ds(r, span, stride=n_row), :] = decode(recv_ref[r])
    sym = logits_ref[...] + rows_ref[...]
    lane = lax.broadcasted_iota(jnp.int32, (1, channels), 1)
    left = lane < bins_count
    low = jnp.max(jnp.where(left, sym, -jnp.inf), axis=-1, keepdims=True)
    high = jnp.max(jnp.where(left, -jnp.inf, sym), axis=-1, keepdims=True)
    grown = jnp.exp(sym - jnp.where(left, low, high))
    low = jnp.sum(jnp.where(left, grown, 0.0), axis=-1, keepdims=True)
    high = jnp.sum(jnp.where(left, 0.0, grown), axis=-1, keepdims=True)
    probability = grown / jnp.where(left, low, high)
    own_bin = (lane % bins_count).astype(f32)
    bins = bins_wide_ref[...].reshape(half, channels).astype(f32)
    d_sym = probability - jnp.where(bins == own_bin, 1.0, 0.0)
    d_logit = (d_sym + d_sym).astype(bf16)
    d_logit_ref[...] = d_logit

    d_update = pair_gradient(d_logit, w_head_t_ref[...]).astype(bf16)
    hidden = hidden_ref[...]
    d_hidden = hidden_gradient(dot(d_update, w_out_t_ref[...]), hidden)
    for copy in copies:
        copy.wait()
    g_head = jnp.where(
        left,
        dot(residual_t_ref[:, :half], d_logit),
        dot(residual_t_ref[:, half:], d_logit),
    )
    g_in = dot(normed_t_ref[...], d_hidden)
    d_logit_t = d_logit.T
    g_mid = (
        dot(d_logit_t, hidden[:half])[:bins_count] + dot(d_logit_t, hidden[half:])[bins_count:]
    )
    high = g_mid.astype(bf16)
    rest = (g_mid - high.astype(f32)).astype(bf16)
    w_head = w_head_t_ref[...].T
    g_out = (dot(w_head, high) + dot(w_head, rest)).T
    g_out_turned = pltpu.roll(g_out, bins_count, 1)
    g_head = g_head + pltpu.roll(g_head, bins_count, 1)
    g_head_turned = pltpu.roll(g_head, channels - bins_count // HALVES, 1)
    rows = channels // n_row
    tiles = hidden.shape[1] // channels // HALVES
    wide = tiles * rows
    long = g_out.shape[0] // n_row
    n_far = n_row // ACROSS
    for z in range(HALVES):
        for x in range(ACROSS):
            slot = z * ACROSS + x
            heads = []
            for far in range(n_far):
                r = far * ACROSS + x
                base = far * (wide + long // 2)
                mine = g_in[r * rows : (r + 1) * rows, :]
                part_ref[slot, base : base + wide, :] = jnp.concatenate(
                    [mine[:, t * channels : (t + 1) * channels] for t in range(z * tiles, (z + 1) * tiles)],
                    axis=0,
                ).astype(bf16)
                first = slice(r * long, r * long + long // 2)
                second = slice(r * long + long // 2, (r + 1) * long)
                part_ref[slot, base + wide : base + wide + long // 2, :] = jnp.where(
                    left,
                    (g_out if z == 0 else g_out_turned)[first],
                    (g_out_turned if z == 0 else g_out)[second],
                ).astype(bf16)
                heads.append((g_head if z == 0 else g_head_turned)[r * rows : (r + 1) * rows])
            part_ref[slot, n_far * (wide + long // 2) :, :] = jnp.concatenate(heads, axis=0).astype(
                bf16
            )


def pair_gradient(d_logit, w_head_t):
    wide = dot(d_logit, widen(w_head_t))
    channels = wide.shape[1] // CYCLES
    return jnp.concatenate([wide[:, :channels], wide[:, channels:]], axis=0)


def hidden_gradient(back, hidden):
    back = back.astype(bf16)
    return jnp.where(hidden > 0, back, jnp.zeros_like(back))


def pair_kernel(
    d_logit_ref, hidden_ref, pair_ref, w_in_ref, w_out_ref, w_head_t_ref, grad_ref, values_ref
):
    channels = grad_ref.shape[-1]
    count = grad_ref.shape[1]
    n_row = grad_ref.shape[2] // CYCLES
    d_resid = pair_gradient(d_logit_ref[...], w_head_t_ref[...])
    d_hidden = hidden_gradient(dot_t(d_resid.astype(bf16), w_out_ref[...]), hidden_ref[...])
    d_normed = dot_t(d_hidden, w_in_ref[...])
    for a in range(CYCLES):
        for b in range(CYCLES):
            values_ref[a, :, b] = pair_ref[b, :, a * n_row : (a + 1) * n_row, :].astype(f32)
    x_hat, inv_std = normalize(values_ref[...].reshape(-1, channels))
    first_mean = jnp.mean(d_normed, axis=-1, keepdims=True)
    second_mean = jnp.mean(d_normed * x_hat, axis=-1, keepdims=True)
    d_pair = d_resid + inv_std * (d_normed - first_mean - x_hat * second_mean)
    d_pair = d_pair.astype(bf16).reshape(CYCLES, count, CYCLES, n_row, channels)
    for a in range(CYCLES):
        for b in range(CYCLES):
            grad_ref[b, :, a * n_row : (a + 1) * n_row, :] = d_pair[a, :, b]


def lanes_of(shape, axis):
    return lax.broadcasted_iota(jnp.int32, shape, axis)


def fold_matrix(width, kind):
    shape = (128, 128)
    return (lanes_of(shape, 0) % width == lanes_of(shape, 1) % width).astype(f32).astype(kind)


def middle_kernel(recv_ref, out_ref, rows_ref, send_ref):
    total = recv_ref[0].astype(f32)
    for source in range(1, recv_ref.shape[0]):
        total = total + recv_ref[source].astype(f32)
    n_far = rows_ref.shape[0]
    for far in range(n_far):
        pack(
            total[far * 32 : far * 32 + 16],
            total[far * 32 + 16 : far * 32 + 32],
            total[n_far * 32 + far * 8 : n_far * 32 + far * 8 + 8],
            rows_ref.at[far],
            send_ref,
            far * 64,
        )
    out_ref[...] = send_ref[...].astype(bf16)


def pack(wide, long, head, rows_ref, send_ref, base):
    count = 16
    rows, tiles = 8, 2
    group = lanes_of((1, rows, 128), 2) // 16 == lanes_of((1, rows, 128), 1)
    spread = jnp.where(group, jnp.broadcast_to(wide[:, None, :], (rows * tiles, rows, 128)), 0.0)
    folded = dot(spread.reshape(-1, 128).astype(bf16), fold_matrix(16, bf16))
    folded = folded.reshape(tiles, rows, rows, 128)
    slot = lanes_of((1, rows, 1, 128), 3) // 16 == (8 - lanes_of((1, rows, 1, 128), 1)) % 8
    part_in = jnp.sum(jnp.where(slot, folded, 0.0), axis=1).reshape(count, 128)
    send_ref[pl.ds(base, count, stride=4), :] = part_in
    lane = lanes_of((1, 128), 1)
    mine = jnp.concatenate([long, pltpu.roll(long, 64, 1)], axis=0)
    rows_ref[0] = jnp.concatenate([mine] * 4, axis=0).T
    part_out = rows_ref[0, pl.ds(0, count, stride=4), :]
    for j in range(1, 4):
        part_out = jnp.where(
            lane // 32 == 4 - j, rows_ref[0, pl.ds(j, count, stride=4), :], part_out
        )
    send_ref[pl.ds(base + 1, count, stride=4), :] = part_out
    rows_ref[1] = jnp.concatenate([head] * 16, axis=0).T
    part_head = jnp.where(
        lane // 8 == 15,
        rows_ref[1, pl.ds(1, count, stride=2), :],
        rows_ref[1, pl.ds(0, count, stride=2), :],
    )
    send_ref[pl.ds(base + 2, count, stride=4), :] = part_head
    send_ref[pl.ds(base + 3, count, stride=4), :] = jnp.zeros_like(part_head)


def final_kernel(scale, recv_ref, in_ref, out_t_ref, head_t_ref):
    values = recv_ref[...].astype(f32)
    total = values[0:8]
    for c in range(1, values.shape[0] // 8):
        total = total + values[c * 8 : (c + 1) * 8]
    total = (total[0:4] + total[4:8]) * scale

    def unfold(row, out):
        count, width = out.shape
        if width * 8 <= 128:
            spread = jnp.broadcast_to(row, (8, 128))
            spread = pltpu.roll(spread, 0, 1, stride=width, stride_axis=0)
        else:
            spread = jnp.concatenate(
                [pltpu.roll(row, i * width, 1) if i else row for i in range(count)], axis=0
            )
        out[...] = spread[:count, :width]

    unfold(total[0:1], in_ref)
    unfold(total[1:2], out_t_ref)
    unfold(total[2:3], head_t_ref)


ROOM = 48 * 1024 * 1024


def params(limit=62 * 1024 * 1024):
    return pltpu.CompilerParams(vmem_limit_bytes=limit)


def in_hbm(array):
    return pltpu.with_memory_space_constraint(array, pltpu.HBM)


def forward_call(pair_rep, w_in, w_out, w_head_t, n_row, n_col):
    row_count, col_count, channels = pair_rep.shape
    return pl.pallas_call(
        send_kernel,
        out_shape=jax.ShapeDtypeStruct((n_row, CYCLES * n_col, channels), jnp.int16),
        scratch_shapes=[pltpu.VMEM((CYCLES * n_col * n_row, channels), jnp.int32)],
        compiler_params=params(),
        name="forward",
    )(pair_rep.reshape(CYCLES, n_col, col_count, channels), w_in, w_out, w_head_t)


HERE = pl.BlockSpec()
THERE = pl.BlockSpec(memory_space=pl.ANY)


def prepare_call(pair_rep, true_bins, w_in, w_out, w_head_t, n_row, n_col):
    row_count, col_count, channels = pair_rep.shape
    pairs = row_count * col_count
    hidden_count = w_in.shape[1]
    away = [
        jax.ShapeDtypeStruct((channels, pairs), bf16),
        jax.ShapeDtypeStruct((channels, pairs), bf16),
    ]
    results = pl.pallas_call(
        prepare_kernel,
        in_specs=[HERE] * 5,
        out_specs=[HERE] * 4 + [pl.BlockSpec(memory_space=pltpu.HBM)] * 2,
        out_shape=[
            jax.ShapeDtypeStruct((pairs, hidden_count), bf16),
            jax.ShapeDtypeStruct((pairs // CYCLES, channels), f32),
            jax.ShapeDtypeStruct((n_col, CYCLES, n_row, channels), bf16),
            jax.ShapeDtypeStruct((channels, hidden_count), bf16),
            *away,
        ],
        scratch_shapes=[pltpu.VMEM(x.shape, x.dtype) for x in away]
        + [
            pltpu.VMEM((CYCLES, n_col, CYCLES, n_row, channels), f32),
            pltpu.SemaphoreType.DMA((len(away),)),
        ],
        compiler_params=params(ROOM),
        cost_estimate=pl.CostEstimate(
            flops=2 * pairs * 2 * channels * hidden_count, bytes_accessed=8 * 2**20, transcendentals=0
        ),
        name="prepare",
    )(
        in_hbm(pair_rep.reshape(CYCLES, n_col, col_count, channels)),
        true_bins.reshape(CYCLES, n_col, col_count),
        in_hbm(w_in),
        in_hbm(w_out),
        in_hbm(w_head_t),
    )
    return results[:4], [in_hbm(x) for x in results[4:]]


def weights_call(recv, near, normed_t, residual_t, w_head_t):
    logits, bins_wide, hidden, w_out_t = near
    n_row, span, channels = recv.shape
    pairs, hidden_count = hidden.shape
    far_rows = hidden_count // n_row // 2 + channels // n_row * (hidden_count // channels) // HALVES
    part_rows = n_row // ACROSS * (far_rows + channels // n_row)
    d_logit = jax.ShapeDtypeStruct((pairs // CYCLES, channels), bf16)
    late = (normed_t, residual_t)
    return pl.pallas_call(
        weights_kernel,
        in_specs=[HERE] * 5 + [THERE] * 2 + [HERE],
        out_specs=[HERE, HERE],
        out_shape=[d_logit, jax.ShapeDtypeStruct((HALVES * ACROSS, part_rows, channels), bf16)],
        scratch_shapes=[pltpu.VMEM(x.shape, x.dtype) for x in late]
        + [
            pltpu.VMEM((pairs // CYCLES, channels), f32),
            pltpu.SemaphoreType.DMA((len(late),)),
        ],
        compiler_params=params(ROOM),
        name="weights",
    )(recv, logits, bins_wide, hidden, w_out_t, normed_t, residual_t, w_head_t)


def pair_call(d_logit, hidden, pair_rep, w_in, w_out, w_head_t, n_row, n_col):
    row_count, col_count, channels = pair_rep.shape
    pairs, hidden_count = hidden.shape
    cycled = pair_rep.reshape(CYCLES, n_col, col_count, channels)
    return pl.pallas_call(
        pair_kernel,
        out_shape=jax.ShapeDtypeStruct(cycled.shape, bf16),
        scratch_shapes=[pltpu.VMEM((CYCLES, n_col, CYCLES, n_row, channels), f32)],
        compiler_params=params(ROOM),
        cost_estimate=pl.CostEstimate(
            flops=2 * pairs * 2 * channels * hidden_count, bytes_accessed=5 * 2**20, transcendentals=0
        ),
        name="pair",
    )(d_logit, hidden, *[in_hbm(x) for x in (cycled, w_in, w_out, w_head_t)])


def middle_call(part, done, n_row, n_col):
    part, _ = lax.optimization_barrier((part, done))
    n_far = n_row // ACROSS
    shape = (n_far * (n_col // HALVES) * 4, part.shape[-1])
    return pl.pallas_call(
        middle_kernel,
        out_shape=jax.ShapeDtypeStruct(shape, bf16),
        scratch_shapes=[pltpu.VMEM((n_far, 2, 128, 128), f32), pltpu.VMEM(shape, f32)],
        compiler_params=params(ROOM),
        name="sum_near",
    )(part)


def final_call(share, scale, shapes):
    return pl.pallas_call(
        functools.partial(final_kernel, scale),
        out_shape=[jax.ShapeDtypeStruct(shape, f32) for shape in shapes],
        compiler_params=params(ROOM),
        name="sum_rest",
    )(share)


def shards(pair_rep, true_bins, w_in, w_out, w_head):
    row_count, col_count, channels = pair_rep.shape
    n_row = lax.axis_size("row")
    n_col = lax.axis_size("col")
    hidden_count = w_in.shape[1]
    bins_count = w_head.shape[1]
    w_head_t = w_head.T

    send = forward_call(pair_rep, w_in, w_out, w_head_t, n_row, n_col)
    recv = lax.all_to_all(
        send.reshape(n_row * n_col, CYCLES, channels),
        ("row", "col"),
        split_axis=0,
        concat_axis=0,
        tiled=True,
    ).reshape(n_row, CYCLES * n_col, channels)
    (hidden, logits, bins_wide, w_out_t), (normed_t, residual_t) = (
        prepare_call(pair_rep, true_bins, w_in, w_out, w_head_t, n_row, n_col)
    )
    d_logit, part = weights_call(
        recv, (logits, bins_wide, hidden, w_out_t), normed_t, residual_t, w_head_t
    )
    n_far, n_half = n_row // ACROSS, n_col // HALVES
    part = lax.all_to_all(
        part,
        ("row", "col"),
        split_axis=0,
        concat_axis=0,
        tiled=True,
        axis_index_groups=[
            [
                (far * ACROSS + x) * n_col + z * n_half + c
                for z in range(HALVES)
                for x in range(ACROSS)
            ]
            for far in range(n_far)
            for c in range(n_half)
        ],
    )
    d_pair = pair_call(d_logit, hidden, pair_rep, w_in, w_out, w_head_t, n_row, n_col)
    share = middle_call(part, d_pair, n_row, n_col)
    share = lax.all_to_all(
        share.reshape(n_far * n_half, 4, channels),
        ("row", "col"),
        split_axis=0,
        concat_axis=0,
        tiled=True,
        axis_index_groups=[
            [
                (far * ACROSS + x) * n_col + z * n_half + c
                for far in range(n_far)
                for c in range(n_half)
            ]
            for z in range(HALVES)
            for x in range(ACROSS)
        ],
    ).reshape(n_far * n_half * 4, channels)
    grad_in, grad_out_t, grad_head_t = final_call(
        share,
        1.0 / (row_count * n_row),
        [
            (channels // n_row, hidden_count // n_col),
            (channels // n_col, hidden_count // n_row),
            (bins_count // n_col, channels // n_row),
        ],
    )
    return (
        d_pair.reshape(row_count, col_count, channels),
        grad_in,
        grad_out_t.T,
        grad_head_t.T,
    )


def solution(mesh):
    placed = (P("row", "col", None), P("row", "col"), P(), P(), P())
    return jax.shard_map(
        shards,
        mesh=mesh,
        in_specs=placed,
        out_specs=(P("row", "col", None), P("row", "col"), P("row", "col"), P("row", "col")),
        check_vma=False,
    )
```

```python
import functools

import jax
import jax.numpy as jnp
from jax import lax
from jax.experimental import pallas as pl
from jax.experimental.pallas import tpu as pltpu
from jax.sharding import PartitionSpec as P

epsilon = 1e-05
f32 = jnp.float32
bf16 = jnp.bfloat16

code_steps = 2350.0

CYCLES = 2

ACROSS = 4
HALVES = 2


def dot(first, second):
    return jnp.dot(first, second, preferred_element_type=f32)


def dot_t(first, second):
    return lax.dot_general(first, second, (((1,), (1,)), ((), ())), preferred_element_type=f32)


def widen(w_head_t):
    blank = jnp.zeros_like(w_head_t)
    return jnp.concatenate(
        [
            jnp.concatenate([w_head_t, blank], axis=1),
            jnp.concatenate([blank, w_head_t], axis=1),
        ],
        axis=0,
    )


def encode(values):
    size = jnp.log(1.0 + jnp.abs(values)) * code_steps + 0.5
    return jnp.where(values < 0.0, -size, size).astype(jnp.int32)


def decode(codes):
    codes = codes.astype(f32)
    size = jnp.exp(jnp.abs(codes) * (1.0 / code_steps)) - 1.0
    return jnp.where(codes < 0.0, -size, size)


def normalize(values):
    centred = values - jnp.mean(values, axis=-1, keepdims=True)
    variance = jnp.mean(centred * centred, axis=-1, keepdims=True)
    inv_std = lax.rsqrt(variance + epsilon)
    return (centred * inv_std, inv_std)


def send_kernel(pair_ref, w_in_ref, w_out_ref, w_head_t_ref, send_ref, rows_ref):
    n_row = send_ref.shape[0]
    span = send_ref.shape[1]
    channels = pair_ref.shape[-1]
    values = pair_ref[...].reshape(-1, channels).astype(f32)
    half = values.shape[0] // CYCLES
    x_hat, _ = normalize(values)
    hidden = jnp.maximum(dot(x_hat.astype(bf16), w_in_ref[...]), 0.0).astype(bf16)
    residual = (values + dot(hidden, w_out_ref[...])).astype(bf16)
    wide = jnp.concatenate([residual[:half], residual[half:]], axis=1)
    rows_ref[...] = encode(dot_t(wide, widen(w_head_t_ref[...])))
    for r in range(n_row):
        send_ref[r] = rows_ref[pl.ds(r, span, stride=n_row), :].astype(jnp.int16)


def prepare_kernel(
    pair_ref,
    bins_ref,
    w_in_ref,
    w_out_ref,
    w_head_t_ref,
    hidden_ref,
    logits_ref,
    bins_wide_ref,
    w_out_t_ref,
    normed_t_hbm,
    residual_t_hbm,
    normed_t_ref,
    residual_t_ref,
    values_ref,
    sems,
):
    kept = (
        (normed_t_ref, normed_t_hbm),
        (residual_t_ref, residual_t_hbm),
    )
    copies = [
        pltpu.make_async_copy(source, target, sems.at[i])
        for i, (source, target) in enumerate(kept)
    ]
    channels = pair_ref.shape[-1]
    n_row = pair_ref.shape[2] // CYCLES
    count = pair_ref.shape[1]
    for a in range(CYCLES):
        for b in range(CYCLES):
            values_ref[a, :, b] = pair_ref[b, :, a * n_row : (a + 1) * n_row, :].astype(f32)
    values = values_ref[...].reshape(-1, channels)
    half = values.shape[0] // CYCLES
    x_hat, _ = normalize(values)
    normed = x_hat.astype(bf16)
    hidden = jnp.maximum(dot(normed, w_in_ref[...]), 0.0).astype(bf16)
    residual = (values + dot(hidden, w_out_ref[...])).astype(bf16)
    hidden_ref[...] = hidden
    w_out_t_ref[...] = w_out_ref[...].T
    normed_t_ref[...] = normed.T
    residual_t_ref[...] = residual.T
    logits_ref[...] = dot_t(
        jnp.concatenate([residual[:half], residual[half:]], axis=1), widen(w_head_t_ref[...])
    )
    for copy in copies:
        copy.start()
    columns = bins_ref.shape[-1]
    row_of = lax.broadcasted_iota(jnp.int32, (1, n_row, columns), 1)
    column_of = lax.broadcasted_iota(jnp.int32, (1, n_row, columns), 2)
    own = column_of % n_row == row_of
    lane = lax.broadcasted_iota(jnp.int32, (columns, channels), 1)
    source = lax.broadcasted_iota(jnp.int32, (columns, channels), 0)
    spread = (lane // (channels // CYCLES) == source // n_row).astype(f32).astype(bf16)
    for b in range(CYCLES):
        bins = bins_ref[b].astype(f32)
        picked = jnp.where(own, jnp.broadcast_to(bins[:, None, :], (count, n_row, columns)), 0.0)
        wide = dot(picked.reshape(count * n_row, columns).astype(bf16), spread)
        bins_wide_ref[:, b] = wide.astype(bf16).reshape(count, n_row, channels)
    for copy in copies:
        copy.wait()


def weights_kernel(
    recv_ref,
    logits_ref,
    bins_wide_ref,
    hidden_ref,
    w_out_t_ref,
    normed_t_hbm,
    residual_t_hbm,
    w_head_t_ref,
    d_logit_ref,
    part_ref,
    normed_t_ref,
    residual_t_ref,
    rows_ref,
    sems,
):
    n_row, span, channels = recv_ref.shape
    bins_count = channels // CYCLES
    half = span * n_row
    copies = [
        pltpu.make_async_copy(source, target, sems.at[i])
        for i, (source, target) in enumerate(
            ((normed_t_hbm, normed_t_ref), (residual_t_hbm, residual_t_ref))
        )
    ]
    for copy in copies:
        copy.start()

    for r in range(n_row):
        rows_ref[pl.ds(r, span, stride=n_row), :] = decode(recv_ref[r])
    sym = logits_ref[...] + rows_ref[...]
    lane = lax.broadcasted_iota(jnp.int32, (1, channels), 1)
    left = lane < bins_count
    low = jnp.max(jnp.where(left, sym, -jnp.inf), axis=-1, keepdims=True)
    high = jnp.max(jnp.where(left, -jnp.inf, sym), axis=-1, keepdims=True)
    grown = jnp.exp(sym - jnp.where(left, low, high))
    low = jnp.sum(jnp.where(left, grown, 0.0), axis=-1, keepdims=True)
    high = jnp.sum(jnp.where(left, 0.0, grown), axis=-1, keepdims=True)
    probability = grown / jnp.where(left, low, high)
    own_bin = (lane % bins_count).astype(f32)
    bins = bins_wide_ref[...].reshape(half, channels).astype(f32)
    d_sym = probability - jnp.where(bins == own_bin, 1.0, 0.0)
    d_logit = (d_sym + d_sym).astype(bf16)
    d_logit_ref[...] = d_logit

    d_update = pair_gradient(d_logit, w_head_t_ref[...]).astype(bf16)
    hidden = hidden_ref[...]
    d_hidden = hidden_gradient(dot(d_update, w_out_t_ref[...]), hidden)
    for copy in copies:
        copy.wait()
    g_head = jnp.where(
        left,
        dot(residual_t_ref[:, :half], d_logit),
        dot(residual_t_ref[:, half:], d_logit),
    )
    g_in = dot(normed_t_ref[...], d_hidden)
    d_logit_t = d_logit.T
    g_mid = (
        dot(d_logit_t, hidden[:half])[:bins_count] + dot(d_logit_t, hidden[half:])[bins_count:]
    )
    high = g_mid.astype(bf16)
    rest = (g_mid - high.astype(f32)).astype(bf16)
    w_head = w_head_t_ref[...].T
    g_out = (dot(w_head, high) + dot(w_head, rest)).T
    g_out_turned = pltpu.roll(g_out, bins_count, 1)
    g_head = g_head + pltpu.roll(g_head, bins_count, 1)
    g_head_turned = pltpu.roll(g_head, channels - bins_count // HALVES, 1)
    rows = channels // n_row
    tiles = hidden.shape[1] // channels // HALVES
    wide = tiles * rows
    long = g_out.shape[0] // n_row
    n_far = n_row // ACROSS
    for z in range(HALVES):
        for x in range(ACROSS):
            slot = z * ACROSS + x
            heads = []
            for far in range(n_far):
                r = far * ACROSS + x
                base = far * (wide + long // 2)
                mine = g_in[r * rows : (r + 1) * rows, :]
                part_ref[slot, base : base + wide, :] = jnp.concatenate(
                    [mine[:, t * channels : (t + 1) * channels] for t in range(z * tiles, (z + 1) * tiles)],
                    axis=0,
                ).astype(bf16)
                first = slice(r * long, r * long + long // 2)
                second = slice(r * long + long // 2, (r + 1) * long)
                part_ref[slot, base + wide : base + wide + long // 2, :] = jnp.where(
                    left,
                    (g_out if z == 0 else g_out_turned)[first],
                    (g_out_turned if z == 0 else g_out)[second],
                ).astype(bf16)
                heads.append((g_head if z == 0 else g_head_turned)[r * rows : (r + 1) * rows])
            part_ref[slot, n_far * (wide + long // 2) :, :] = jnp.concatenate(heads, axis=0).astype(
                bf16
            )


def pair_gradient(d_logit, w_head_t):
    wide = dot(d_logit, widen(w_head_t))
    channels = wide.shape[1] // CYCLES
    return jnp.concatenate([wide[:, :channels], wide[:, channels:]], axis=0)


def hidden_gradient(back, hidden):
    back = back.astype(bf16)
    return jnp.where(hidden > 0, back, jnp.zeros_like(back))


def pair_kernel(
    d_logit_ref, hidden_ref, pair_ref, w_in_ref, w_out_ref, w_head_t_ref, grad_ref, values_ref
):
    channels = grad_ref.shape[-1]
    count = grad_ref.shape[1]
    n_row = grad_ref.shape[2] // CYCLES
    d_resid = pair_gradient(d_logit_ref[...], w_head_t_ref[...])
    d_hidden = hidden_gradient(dot_t(d_resid.astype(bf16), w_out_ref[...]), hidden_ref[...])
    d_normed = dot_t(d_hidden, w_in_ref[...])
    for a in range(CYCLES):
        for b in range(CYCLES):
            values_ref[a, :, b] = pair_ref[b, :, a * n_row : (a + 1) * n_row, :].astype(f32)
    x_hat, inv_std = normalize(values_ref[...].reshape(-1, channels))
    first_mean = jnp.mean(d_normed, axis=-1, keepdims=True)
    second_mean = jnp.mean(d_normed * x_hat, axis=-1, keepdims=True)
    d_pair = d_resid + inv_std * (d_normed - first_mean - x_hat * second_mean)
    d_pair = d_pair.astype(bf16).reshape(CYCLES, count, CYCLES, n_row, channels)
    for a in range(CYCLES):
        for b in range(CYCLES):
            grad_ref[b, :, a * n_row : (a + 1) * n_row, :] = d_pair[a, :, b]


def lanes_of(shape, axis):
    return lax.broadcasted_iota(jnp.int32, shape, axis)


def fold_matrix(width, kind):
    shape = (128, 128)
    return (lanes_of(shape, 0) % width == lanes_of(shape, 1) % width).astype(f32).astype(kind)


def middle_kernel(recv_ref, out_ref, rows_ref, send_ref):
    total = recv_ref[0].astype(f32)
    for source in range(1, recv_ref.shape[0]):
        total = total + recv_ref[source].astype(f32)
    n_far = rows_ref.shape[0]
    for far in range(n_far):
        pack(
            total[far * 32 : far * 32 + 16],
            total[far * 32 + 16 : far * 32 + 32],
            total[n_far * 32 + far * 8 : n_far * 32 + far * 8 + 8],
            rows_ref.at[far],
            send_ref,
            far * 64,
        )
    out_ref[...] = send_ref[...].astype(bf16)


def pack(wide, long, head, rows_ref, send_ref, base):
    count = 16
    rows, tiles = 8, 2
    group = lanes_of((1, rows, 128), 2) // 16 == lanes_of((1, rows, 128), 1)
    spread = jnp.where(group, jnp.broadcast_to(wide[:, None, :], (rows * tiles, rows, 128)), 0.0)
    folded = dot(spread.reshape(-1, 128).astype(bf16), fold_matrix(16, bf16))
    folded = folded.reshape(tiles, rows, rows, 128)
    slot = lanes_of((1, rows, 1, 128), 3) // 16 == (8 - lanes_of((1, rows, 1, 128), 1)) % 8
    part_in = jnp.sum(jnp.where(slot, folded, 0.0), axis=1).reshape(count, 128)
    send_ref[pl.ds(base, count, stride=4), :] = part_in
    lane = lanes_of((1, 128), 1)
    mine = jnp.concatenate([long, pltpu.roll(long, 64, 1)], axis=0)
    rows_ref[0] = jnp.concatenate([mine] * 4, axis=0).T
    part_out = rows_ref[0, pl.ds(0, count, stride=4), :]
    for j in range(1, 4):
        part_out = jnp.where(
            lane // 32 == 4 - j, rows_ref[0, pl.ds(j, count, stride=4), :], part_out
        )
    send_ref[pl.ds(base + 1, count, stride=4), :] = part_out
    rows_ref[1] = jnp.concatenate([head] * 16, axis=0).T
    part_head = jnp.where(
        lane // 8 == 15,
        rows_ref[1, pl.ds(1, count, stride=2), :],
        rows_ref[1, pl.ds(0, count, stride=2), :],
    )
    send_ref[pl.ds(base + 2, count, stride=4), :] = part_head
    send_ref[pl.ds(base + 3, count, stride=4), :] = jnp.zeros_like(part_head)


def final_kernel(scale, recv_ref, in_ref, out_t_ref, head_t_ref):
    values = recv_ref[...].astype(f32)
    total = values[0:8]
    for c in range(1, values.shape[0] // 8):
        total = total + values[c * 8 : (c + 1) * 8]
    total = (total[0:4] + total[4:8]) * scale

    def unfold(row, out):
        count, width = out.shape
        if width * 8 <= 128:
            spread = jnp.broadcast_to(row, (8, 128))
            spread = pltpu.roll(spread, 0, 1, stride=width, stride_axis=0)
        else:
            spread = jnp.concatenate(
                [pltpu.roll(row, i * width, 1) if i else row for i in range(count)], axis=0
            )
        out[...] = spread[:count, :width]

    unfold(total[0:1], in_ref)
    unfold(total[1:2], out_t_ref)
    unfold(total[2:3], head_t_ref)


ROOM = 48 * 1024 * 1024


def params(limit=62 * 1024 * 1024):
    return pltpu.CompilerParams(vmem_limit_bytes=limit)


def in_hbm(array):
    return pltpu.with_memory_space_constraint(array, pltpu.HBM)


def forward_call(pair_rep, w_in, w_out, w_head_t, n_row, n_col):
    row_count, col_count, channels = pair_rep.shape
    return pl.pallas_call(
        send_kernel,
        out_shape=jax.ShapeDtypeStruct((n_row, CYCLES * n_col, channels), jnp.int16),
        scratch_shapes=[pltpu.VMEM((CYCLES * n_col * n_row, channels), jnp.int32)],
        compiler_params=params(),
        name="forward",
    )(pair_rep.reshape(CYCLES, n_col, col_count, channels), w_in, w_out, w_head_t)


HERE = pl.BlockSpec()
THERE = pl.BlockSpec(memory_space=pl.ANY)


def prepare_call(pair_rep, true_bins, w_in, w_out, w_head_t, n_row, n_col):
    row_count, col_count, channels = pair_rep.shape
    pairs = row_count * col_count
    hidden_count = w_in.shape[1]
    away = [
        jax.ShapeDtypeStruct((channels, pairs), bf16),
        jax.ShapeDtypeStruct((channels, pairs), bf16),
    ]
    results = pl.pallas_call(
        prepare_kernel,
        in_specs=[HERE] * 5,
        out_specs=[HERE] * 4 + [pl.BlockSpec(memory_space=pltpu.HBM)] * 2,
        out_shape=[
            jax.ShapeDtypeStruct((pairs, hidden_count), bf16),
            jax.ShapeDtypeStruct((pairs // CYCLES, channels), f32),
            jax.ShapeDtypeStruct((n_col, CYCLES, n_row, channels), bf16),
            jax.ShapeDtypeStruct((channels, hidden_count), bf16),
            *away,
        ],
        scratch_shapes=[pltpu.VMEM(x.shape, x.dtype) for x in away]
        + [
            pltpu.VMEM((CYCLES, n_col, CYCLES, n_row, channels), f32),
            pltpu.SemaphoreType.DMA((len(away),)),
        ],
        compiler_params=params(ROOM),
        cost_estimate=pl.CostEstimate(
            flops=2 * pairs * 2 * channels * hidden_count, bytes_accessed=8 * 2**20, transcendentals=0
        ),
        name="prepare",
    )(
        in_hbm(pair_rep.reshape(CYCLES, n_col, col_count, channels)),
        true_bins.reshape(CYCLES, n_col, col_count),
        in_hbm(w_in),
        in_hbm(w_out),
        in_hbm(w_head_t),
    )
    return results[:4], [in_hbm(x) for x in results[4:]]


def weights_call(recv, near, normed_t, residual_t, w_head_t):
    logits, bins_wide, hidden, w_out_t = near
    n_row, span, channels = recv.shape
    pairs, hidden_count = hidden.shape
    far_rows = hidden_count // n_row // 2 + channels // n_row * (hidden_count // channels) // HALVES
    part_rows = n_row // ACROSS * (far_rows + channels // n_row)
    d_logit = jax.ShapeDtypeStruct((pairs // CYCLES, channels), bf16)
    late = (normed_t, residual_t)
    return pl.pallas_call(
        weights_kernel,
        in_specs=[HERE] * 5 + [THERE] * 2 + [HERE],
        out_specs=[HERE, HERE],
        out_shape=[d_logit, jax.ShapeDtypeStruct((HALVES * ACROSS, part_rows, channels), bf16)],
        scratch_shapes=[pltpu.VMEM(x.shape, x.dtype) for x in late]
        + [
            pltpu.VMEM((pairs // CYCLES, channels), f32),
            pltpu.SemaphoreType.DMA((len(late),)),
        ],
        compiler_params=params(ROOM),
        name="weights",
    )(recv, logits, bins_wide, hidden, w_out_t, normed_t, residual_t, w_head_t)


def pair_call(d_logit, hidden, pair_rep, w_in, w_out, w_head_t, n_row, n_col):
    row_count, col_count, channels = pair_rep.shape
    pairs, hidden_count = hidden.shape
    cycled = pair_rep.reshape(CYCLES, n_col, col_count, channels)
    return pl.pallas_call(
        pair_kernel,
        out_shape=jax.ShapeDtypeStruct(cycled.shape, bf16),
        scratch_shapes=[pltpu.VMEM((CYCLES, n_col, CYCLES, n_row, channels), f32)],
        compiler_params=params(ROOM),
        cost_estimate=pl.CostEstimate(
            flops=2 * pairs * 2 * channels * hidden_count, bytes_accessed=5 * 2**20, transcendentals=0
        ),
        name="pair",
    )(d_logit, hidden, *[in_hbm(x) for x in (cycled, w_in, w_out, w_head_t)])


def middle_call(part, n_row, n_col):
    n_far = n_row // ACROSS
    shape = (n_far * (n_col // HALVES) * 4, part.shape[-1])
    return pl.pallas_call(
        middle_kernel,
        out_shape=jax.ShapeDtypeStruct(shape, bf16),
        scratch_shapes=[pltpu.VMEM((n_far, 2, 128, 128), f32), pltpu.VMEM(shape, f32)],
        compiler_params=params(ROOM),
        name="sum_near",
    )(part)


def final_call(share, scale, shapes):
    return pl.pallas_call(
        functools.partial(final_kernel, scale),
        out_shape=[jax.ShapeDtypeStruct(shape, f32) for shape in shapes],
        compiler_params=params(ROOM),
        name="sum_rest",
    )(share)


def shards(pair_rep, true_bins, w_in, w_out, w_head):
    row_count, col_count, channels = pair_rep.shape
    n_row = lax.axis_size("row")
    n_col = lax.axis_size("col")
    hidden_count = w_in.shape[1]
    bins_count = w_head.shape[1]
    w_head_t = w_head.T

    send = forward_call(pair_rep, w_in, w_out, w_head_t, n_row, n_col)
    recv = lax.all_to_all(
        send.reshape(n_row * n_col, CYCLES, channels),
        ("row", "col"),
        split_axis=0,
        concat_axis=0,
        tiled=True,
    ).reshape(n_row, CYCLES * n_col, channels)
    (hidden, logits, bins_wide, w_out_t), (normed_t, residual_t) = (
        prepare_call(pair_rep, true_bins, w_in, w_out, w_head_t, n_row, n_col)
    )
    d_logit, part = weights_call(
        recv, (logits, bins_wide, hidden, w_out_t), normed_t, residual_t, w_head_t
    )
    n_far, n_half = n_row // ACROSS, n_col // HALVES
    part = lax.all_to_all(
        part,
        ("row", "col"),
        split_axis=0,
        concat_axis=0,
        tiled=True,
        axis_index_groups=[
            [
                (far * ACROSS + x) * n_col + z * n_half + c
                for z in range(HALVES)
                for x in range(ACROSS)
            ]
            for far in range(n_far)
            for c in range(n_half)
        ],
    )
    share = middle_call(part, n_row, n_col)
    share = lax.all_to_all(
        share.reshape(n_far * n_half, 4, channels),
        ("row", "col"),
        split_axis=0,
        concat_axis=0,
        tiled=True,
        axis_index_groups=[
            [
                (far * ACROSS + x) * n_col + z * n_half + c
                for far in range(n_far)
                for c in range(n_half)
            ]
            for z in range(HALVES)
            for x in range(ACROSS)
        ],
    ).reshape(n_far * n_half * 4, channels)
    d_pair = pair_call(d_logit, hidden, pair_rep, w_in, w_out, w_head_t, n_row, n_col)
    grad_in, grad_out_t, grad_head_t = final_call(
        share,
        1.0 / (row_count * n_row),
        [
            (channels // n_row, hidden_count // n_col),
            (channels // n_col, hidden_count // n_row),
            (bins_count // n_col, channels // n_row),
        ],
    )
    return (
        d_pair.reshape(row_count, col_count, channels),
        grad_in,
        grad_out_t.T,
        grad_head_t.T,
    )


def solution(mesh):
    placed = (P("row", "col", None), P("row", "col"), P(), P(), P())
    return jax.shard_map(
        shards,
        mesh=mesh,
        in_specs=placed,
        out_specs=(P("row", "col", None), P("row", "col"), P("row", "col"), P("row", "col")),
        check_vma=False,
    )
```

```python
import functools

import jax
import jax.numpy as jnp
from jax import lax
from jax.experimental import pallas as pl
from jax.experimental.pallas import tpu as pltpu
from jax.sharding import PartitionSpec as P

epsilon = 1e-05
f32 = jnp.float32
bf16 = jnp.bfloat16

code_steps = 2350.0

CYCLES = 2
CHUNKS = 2

ACROSS = 4
HALVES = 2


def dot(first, second):
    return jnp.dot(first, second, preferred_element_type=f32)


def dot_t(first, second):
    return lax.dot_general(first, second, (((1,), (1,)), ((), ())), preferred_element_type=f32)


def widen(w_head_t):
    blank = jnp.zeros_like(w_head_t)
    return jnp.concatenate(
        [
            jnp.concatenate([w_head_t, blank], axis=1),
            jnp.concatenate([blank, w_head_t], axis=1),
        ],
        axis=0,
    )


def encode(values):
    size = jnp.log(1.0 + jnp.abs(values)) * code_steps + 0.5
    return jnp.where(values < 0.0, -size, size).astype(jnp.int32)


def decode(codes):
    codes = codes.astype(f32)
    size = jnp.exp(jnp.abs(codes) * (1.0 / code_steps)) - 1.0
    return jnp.where(codes < 0.0, -size, size)


def normalize(values):
    centred = values - jnp.mean(values, axis=-1, keepdims=True)
    variance = jnp.mean(centred * centred, axis=-1, keepdims=True)
    inv_std = lax.rsqrt(variance + epsilon)
    return (centred * inv_std, inv_std)


def send_kernel(pair_ref, w_in_ref, w_out_ref, w_head_t_ref, send_ref, rows_ref):
    n_row = send_ref.shape[0]
    span = send_ref.shape[1]
    channels = pair_ref.shape[-1]
    count = pair_ref.shape[1] // CHUNKS
    half = count * pair_ref.shape[2]
    w_wide = widen(w_head_t_ref[...])
    for g in range(CHUNKS):
        values = pair_ref[:, g * count : (g + 1) * count].reshape(-1, channels).astype(f32)
        x_hat, _ = normalize(values)
        hidden = jnp.maximum(dot(x_hat.astype(bf16), w_in_ref[...]), 0.0).astype(bf16)
        residual = (values + dot(hidden, w_out_ref[...])).astype(bf16)
        wide = jnp.concatenate([residual[:half], residual[half:]], axis=1)
        rows_ref[g * half : (g + 1) * half] = encode(dot_t(wide, w_wide))
    for r in range(n_row):
        send_ref[r] = rows_ref[pl.ds(r, span, stride=n_row), :].astype(jnp.int16)


def prepare_kernel(
    pair_ref,
    bins_ref,
    w_in_ref,
    w_out_ref,
    w_head_t_ref,
    hidden_ref,
    logits_ref,
    bins_wide_ref,
    w_out_t_ref,
    normed_t_hbm,
    residual_t_hbm,
    normed_t_ref,
    residual_t_ref,
    values_ref,
    sems,
):
    kept = (
        (normed_t_ref, normed_t_hbm),
        (residual_t_ref, residual_t_hbm),
    )
    copies = [
        pltpu.make_async_copy(source, target, sems.at[i])
        for i, (source, target) in enumerate(kept)
    ]
    channels = pair_ref.shape[-1]
    n_row = pair_ref.shape[2] // CYCLES
    count = pair_ref.shape[1]
    for a in range(CYCLES):
        for b in range(CYCLES):
            values_ref[a, :, b] = pair_ref[b, :, a * n_row : (a + 1) * n_row, :].astype(f32)
    values = values_ref[...].reshape(-1, channels)
    half = values.shape[0] // CYCLES
    x_hat, _ = normalize(values)
    normed = x_hat.astype(bf16)
    hidden = jnp.maximum(dot(normed, w_in_ref[...]), 0.0).astype(bf16)
    residual = (values + dot(hidden, w_out_ref[...])).astype(bf16)
    hidden_ref[...] = hidden
    w_out_t_ref[...] = w_out_ref[...].T
    normed_t_ref[...] = normed.T
    residual_t_ref[...] = residual.T
    logits_ref[...] = dot_t(
        jnp.concatenate([residual[:half], residual[half:]], axis=1), widen(w_head_t_ref[...])
    )
    for copy in copies:
        copy.start()
    columns = bins_ref.shape[-1]
    row_of = lax.broadcasted_iota(jnp.int32, (1, n_row, columns), 1)
    column_of = lax.broadcasted_iota(jnp.int32, (1, n_row, columns), 2)
    own = column_of % n_row == row_of
    lane = lax.broadcasted_iota(jnp.int32, (columns, channels), 1)
    source = lax.broadcasted_iota(jnp.int32, (columns, channels), 0)
    spread = (lane // (channels // CYCLES) == source // n_row).astype(f32).astype(bf16)
    for b in range(CYCLES):
        bins = bins_ref[b].astype(f32)
        picked = jnp.where(own, jnp.broadcast_to(bins[:, None, :], (count, n_row, columns)), 0.0)
        wide = dot(picked.reshape(count * n_row, columns).astype(bf16), spread)
        bins_wide_ref[:, b] = wide.astype(bf16).reshape(count, n_row, channels)
    for copy in copies:
        copy.wait()


def weights_kernel(
    recv_ref,
    logits_ref,
    bins_wide_ref,
    hidden_ref,
    w_out_t_ref,
    normed_t_hbm,
    residual_t_hbm,
    w_head_t_ref,
    d_logit_ref,
    part_ref,
    normed_t_ref,
    residual_t_ref,
    rows_ref,
    sems,
):
    n_row, span, channels = recv_ref.shape
    bins_count = channels // CYCLES
    half = span * n_row
    copies = [
        pltpu.make_async_copy(source, target, sems.at[i])
        for i, (source, target) in enumerate(
            ((normed_t_hbm, normed_t_ref), (residual_t_hbm, residual_t_ref))
        )
    ]
    for copy in copies:
        copy.start()

    for r in range(n_row):
        rows_ref[pl.ds(r, span, stride=n_row), :] = decode(recv_ref[r])
    sym = logits_ref[...] + rows_ref[...]
    lane = lax.broadcasted_iota(jnp.int32, (1, channels), 1)
    left = lane < bins_count
    low = jnp.max(jnp.where(left, sym, -jnp.inf), axis=-1, keepdims=True)
    high = jnp.max(jnp.where(left, -jnp.inf, sym), axis=-1, keepdims=True)
    grown = jnp.exp(sym - jnp.where(left, low, high))
    low = jnp.sum(jnp.where(left, grown, 0.0), axis=-1, keepdims=True)
    high = jnp.sum(jnp.where(left, 0.0, grown), axis=-1, keepdims=True)
    probability = grown / jnp.where(left, low, high)
    own_bin = (lane % bins_count).astype(f32)
    bins = bins_wide_ref[...].reshape(half, channels).astype(f32)
    d_sym = probability - jnp.where(bins == own_bin, 1.0, 0.0)
    d_logit = (d_sym + d_sym).astype(bf16)
    d_logit_ref[...] = d_logit

    d_update = pair_gradient(d_logit, w_head_t_ref[...]).astype(bf16)
    hidden = hidden_ref[...]
    d_hidden = hidden_gradient(dot(d_update, w_out_t_ref[...]), hidden)
    for copy in copies:
        copy.wait()
    g_head = jnp.where(
        left,
        dot(residual_t_ref[:, :half], d_logit),
        dot(residual_t_ref[:, half:], d_logit),
    )
    d_logit_t = d_logit.T
    g_mid = (
        dot(d_logit_t, hidden[:half])[:bins_count] + dot(d_logit_t, hidden[half:])[bins_count:]
    )
    g_in = dot(normed_t_ref[...], d_hidden)
    high = g_mid.astype(bf16)
    rest = (g_mid - high.astype(f32)).astype(bf16)
    w_head = w_head_t_ref[...].T
    g_out = (dot(w_head, high) + dot(w_head, rest)).T
    g_out_turned = pltpu.roll(g_out, bins_count, 1)
    g_head = g_head + pltpu.roll(g_head, bins_count, 1)
    g_head_turned = pltpu.roll(g_head, channels - bins_count // HALVES, 1)
    rows = channels // n_row
    tiles = hidden.shape[1] // channels // HALVES
    wide = tiles * rows
    long = g_out.shape[0] // n_row
    n_far = n_row // ACROSS
    for z in range(HALVES):
        for x in range(ACROSS):
            slot = z * ACROSS + x
            heads = []
            for far in range(n_far):
                r = far * ACROSS + x
                base = far * (wide + long // 2)
                mine = g_in[r * rows : (r + 1) * rows, :]
                part_ref[slot, base : base + wide, :] = jnp.concatenate(
                    [mine[:, t * channels : (t + 1) * channels] for t in range(z * tiles, (z + 1) * tiles)],
                    axis=0,
                ).astype(bf16)
                first = slice(r * long, r * long + long // 2)
                second = slice(r * long + long // 2, (r + 1) * long)
                part_ref[slot, base + wide : base + wide + long // 2, :] = jnp.where(
                    left,
                    (g_out if z == 0 else g_out_turned)[first],
                    (g_out_turned if z == 0 else g_out)[second],
                ).astype(bf16)
                heads.append((g_head if z == 0 else g_head_turned)[r * rows : (r + 1) * rows])
            part_ref[slot, n_far * (wide + long // 2) :, :] = jnp.concatenate(heads, axis=0).astype(
                bf16
            )


def pair_gradient(d_logit, w_head_t):
    wide = dot(d_logit, widen(w_head_t))
    channels = wide.shape[1] // CYCLES
    return jnp.concatenate([wide[:, :channels], wide[:, channels:]], axis=0)


def hidden_gradient(back, hidden):
    back = back.astype(bf16)
    return jnp.where(hidden > 0, back, jnp.zeros_like(back))


def pair_kernel(
    d_logit_ref, hidden_ref, pair_ref, w_in_ref, w_out_ref, w_head_t_ref, grad_ref, values_ref
):
    channels = grad_ref.shape[-1]
    count = grad_ref.shape[1]
    n_row = grad_ref.shape[2] // CYCLES
    d_resid = pair_gradient(d_logit_ref[...], w_head_t_ref[...])
    d_hidden = hidden_gradient(dot_t(d_resid.astype(bf16), w_out_ref[...]), hidden_ref[...])
    d_normed = dot_t(d_hidden, w_in_ref[...])
    for a in range(CYCLES):
        for b in range(CYCLES):
            values_ref[a, :, b] = pair_ref[b, :, a * n_row : (a + 1) * n_row, :].astype(f32)
    x_hat, inv_std = normalize(values_ref[...].reshape(-1, channels))
    first_mean = jnp.mean(d_normed, axis=-1, keepdims=True)
    second_mean = jnp.mean(d_normed * x_hat, axis=-1, keepdims=True)
    d_pair = d_resid + inv_std * (d_normed - first_mean - x_hat * second_mean)
    d_pair = d_pair.astype(bf16).reshape(CYCLES, count, CYCLES, n_row, channels)
    for a in range(CYCLES):
        for b in range(CYCLES):
            grad_ref[b, :, a * n_row : (a + 1) * n_row, :] = d_pair[a, :, b]


def lanes_of(shape, axis):
    return lax.broadcasted_iota(jnp.int32, shape, axis)


def fold_matrix(width, kind):
    shape = (128, 128)
    return (lanes_of(shape, 0) % width == lanes_of(shape, 1) % width).astype(f32).astype(kind)


def middle_kernel(recv_ref, out_ref, rows_ref, send_ref):
    total = recv_ref[0].astype(f32)
    for source in range(1, recv_ref.shape[0]):
        total = total + recv_ref[source].astype(f32)
    n_far = rows_ref.shape[0]
    for far in range(n_far):
        pack(
            total[far * 32 : far * 32 + 16],
            total[far * 32 + 16 : far * 32 + 32],
            total[n_far * 32 + far * 8 : n_far * 32 + far * 8 + 8],
            rows_ref.at[far],
            send_ref,
            far * 64,
        )
    out_ref[...] = send_ref[...].astype(bf16)


def pack(wide, long, head, rows_ref, send_ref, base):
    count = 16
    rows, tiles = 8, 2
    group = lanes_of((1, rows, 128), 2) // 16 == lanes_of((1, rows, 128), 1)
    spread = jnp.where(group, jnp.broadcast_to(wide[:, None, :], (rows * tiles, rows, 128)), 0.0)
    folded = dot(spread.reshape(-1, 128).astype(bf16), fold_matrix(16, bf16))
    folded = folded.reshape(tiles, rows, rows, 128)
    slot = lanes_of((1, rows, 1, 128), 3) // 16 == (8 - lanes_of((1, rows, 1, 128), 1)) % 8
    part_in = jnp.sum(jnp.where(slot, folded, 0.0), axis=1).reshape(count, 128)
    send_ref[pl.ds(base, count, stride=4), :] = part_in
    lane = lanes_of((1, 128), 1)
    mine = jnp.concatenate([long, pltpu.roll(long, 64, 1)], axis=0)
    rows_ref[0] = jnp.concatenate([mine] * 4, axis=0).T
    part_out = rows_ref[0, pl.ds(0, count, stride=4), :]
    for j in range(1, 4):
        part_out = jnp.where(
            lane // 32 == 4 - j, rows_ref[0, pl.ds(j, count, stride=4), :], part_out
        )
    send_ref[pl.ds(base + 1, count, stride=4), :] = part_out
    rows_ref[1] = jnp.concatenate([head] * 16, axis=0).T
    part_head = jnp.where(
        lane // 8 == 15,
        rows_ref[1, pl.ds(1, count, stride=2), :],
        rows_ref[1, pl.ds(0, count, stride=2), :],
    )
    send_ref[pl.ds(base + 2, count, stride=4), :] = part_head
    send_ref[pl.ds(base + 3, count, stride=4), :] = jnp.zeros_like(part_head)


def final_kernel(scale, recv_ref, in_ref, out_t_ref, head_t_ref):
    values = recv_ref[...].astype(f32)
    total = values[0:8]
    for c in range(1, values.shape[0] // 8):
        total = total + values[c * 8 : (c + 1) * 8]
    total = (total[0:4] + total[4:8]) * scale

    def unfold(row, out):
        count, width = out.shape
        if width * 8 <= 128:
            spread = jnp.broadcast_to(row, (8, 128))
            spread = pltpu.roll(spread, 0, 1, stride=width, stride_axis=0)
        else:
            spread = jnp.concatenate(
                [pltpu.roll(row, i * width, 1) if i else row for i in range(count)], axis=0
            )
        out[...] = spread[:count, :width]

    unfold(total[0:1], in_ref)
    unfold(total[1:2], out_t_ref)
    unfold(total[2:3], head_t_ref)


ROOM = 48 * 1024 * 1024


def params(limit=62 * 1024 * 1024):
    return pltpu.CompilerParams(vmem_limit_bytes=limit)


def in_hbm(array):
    return pltpu.with_memory_space_constraint(array, pltpu.HBM)


def forward_call(pair_rep, w_in, w_out, w_head_t, n_row, n_col):
    row_count, col_count, channels = pair_rep.shape
    return pl.pallas_call(
        send_kernel,
        out_shape=jax.ShapeDtypeStruct((n_row, CYCLES * n_col, channels), jnp.int16),
        scratch_shapes=[pltpu.VMEM((CYCLES * n_col * n_row, channels), jnp.int32)],
        compiler_params=params(),
        name="forward",
    )(pair_rep.reshape(CYCLES, n_col, col_count, channels), w_in, w_out, w_head_t)


HERE = pl.BlockSpec()
THERE = pl.BlockSpec(memory_space=pl.ANY)


def prepare_call(pair_rep, true_bins, w_in, w_out, w_head_t, n_row, n_col):
    row_count, col_count, channels = pair_rep.shape
    pairs = row_count * col_count
    hidden_count = w_in.shape[1]
    away = [
        jax.ShapeDtypeStruct((channels, pairs), bf16),
        jax.ShapeDtypeStruct((channels, pairs), bf16),
    ]
    results = pl.pallas_call(
        prepare_kernel,
        in_specs=[HERE] * 5,
        out_specs=[HERE] * 4 + [pl.BlockSpec(memory_space=pltpu.HBM)] * 2,
        out_shape=[
            jax.ShapeDtypeStruct((pairs, hidden_count), bf16),
            jax.ShapeDtypeStruct((pairs // CYCLES, channels), f32),
            jax.ShapeDtypeStruct((n_col, CYCLES, n_row, channels), bf16),
            jax.ShapeDtypeStruct((channels, hidden_count), bf16),
            *away,
        ],
        scratch_shapes=[pltpu.VMEM(x.shape, x.dtype) for x in away]
        + [
            pltpu.VMEM((CYCLES, n_col, CYCLES, n_row, channels), f32),
            pltpu.SemaphoreType.DMA((len(away),)),
        ],
        compiler_params=params(ROOM),
        cost_estimate=pl.CostEstimate(
            flops=2 * pairs * 2 * channels * hidden_count, bytes_accessed=8 * 2**20, transcendentals=0
        ),
        name="prepare",
    )(
        in_hbm(pair_rep.reshape(CYCLES, n_col, col_count, channels)),
        true_bins.reshape(CYCLES, n_col, col_count),
        in_hbm(w_in),
        in_hbm(w_out),
        in_hbm(w_head_t),
    )
    return results[:4], [in_hbm(x) for x in results[4:]]


def weights_call(recv, near, normed_t, residual_t, w_head_t):
    logits, bins_wide, hidden, w_out_t = near
    n_row, span, channels = recv.shape
    pairs, hidden_count = hidden.shape
    far_rows = hidden_count // n_row // 2 + channels // n_row * (hidden_count // channels) // HALVES
    part_rows = n_row // ACROSS * (far_rows + channels // n_row)
    d_logit = jax.ShapeDtypeStruct((pairs // CYCLES, channels), bf16)
    late = (normed_t, residual_t)
    return pl.pallas_call(
        weights_kernel,
        in_specs=[HERE] * 5 + [THERE] * 2 + [HERE],
        out_specs=[HERE, HERE],
        out_shape=[d_logit, jax.ShapeDtypeStruct((HALVES * ACROSS, part_rows, channels), bf16)],
        scratch_shapes=[pltpu.VMEM(x.shape, x.dtype) for x in late]
        + [
            pltpu.VMEM((pairs // CYCLES, channels), f32),
            pltpu.SemaphoreType.DMA((len(late),)),
        ],
        compiler_params=params(ROOM),
        name="weights",
    )(recv, logits, bins_wide, hidden, w_out_t, normed_t, residual_t, w_head_t)


def pair_call(d_logit, hidden, pair_rep, w_in, w_out, w_head_t, n_row, n_col):
    row_count, col_count, channels = pair_rep.shape
    pairs, hidden_count = hidden.shape
    cycled = pair_rep.reshape(CYCLES, n_col, col_count, channels)
    return pl.pallas_call(
        pair_kernel,
        out_shape=jax.ShapeDtypeStruct(cycled.shape, bf16),
        scratch_shapes=[pltpu.VMEM((CYCLES, n_col, CYCLES, n_row, channels), f32)],
        compiler_params=params(ROOM),
        cost_estimate=pl.CostEstimate(
            flops=2 * pairs * 2 * channels * hidden_count, bytes_accessed=5 * 2**20, transcendentals=0
        ),
        name="pair",
    )(d_logit, hidden, *[in_hbm(x) for x in (cycled, w_in, w_out, w_head_t)])


def middle_call(part, n_row, n_col):
    n_far = n_row // ACROSS
    shape = (n_far * (n_col // HALVES) * 4, part.shape[-1])
    return pl.pallas_call(
        middle_kernel,
        out_shape=jax.ShapeDtypeStruct(shape, bf16),
        scratch_shapes=[pltpu.VMEM((n_far, 2, 128, 128), f32), pltpu.VMEM(shape, f32)],
        compiler_params=params(ROOM),
        name="sum_near",
    )(part)


def final_call(share, scale, shapes):
    return pl.pallas_call(
        functools.partial(final_kernel, scale),
        out_shape=[jax.ShapeDtypeStruct(shape, f32) for shape in shapes],
        compiler_params=params(ROOM),
        name="sum_rest",
    )(share)


def shards(pair_rep, true_bins, w_in, w_out, w_head):
    row_count, col_count, channels = pair_rep.shape
    n_row = lax.axis_size("row")
    n_col = lax.axis_size("col")
    hidden_count = w_in.shape[1]
    bins_count = w_head.shape[1]
    w_head_t = w_head.T

    send = forward_call(pair_rep, w_in, w_out, w_head_t, n_row, n_col)
    recv = lax.all_to_all(
        send.reshape(n_row * n_col, CYCLES, channels),
        ("row", "col"),
        split_axis=0,
        concat_axis=0,
        tiled=True,
    ).reshape(n_row, CYCLES * n_col, channels)
    (hidden, logits, bins_wide, w_out_t), (normed_t, residual_t) = (
        prepare_call(pair_rep, true_bins, w_in, w_out, w_head_t, n_row, n_col)
    )
    d_logit, part = weights_call(
        recv, (logits, bins_wide, hidden, w_out_t), normed_t, residual_t, w_head_t
    )
    n_far, n_half = n_row // ACROSS, n_col // HALVES
    part = lax.all_to_all(
        part,
        ("row", "col"),
        split_axis=0,
        concat_axis=0,
        tiled=True,
        axis_index_groups=[
            [
                (far * ACROSS + x) * n_col + z * n_half + c
                for z in range(HALVES)
                for x in range(ACROSS)
            ]
            for far in range(n_far)
            for c in range(n_half)
        ],
    )
    share = middle_call(part, n_row, n_col)
    share = lax.all_to_all(
        share.reshape(n_far * n_half, 4, channels),
        ("row", "col"),
        split_axis=0,
        concat_axis=0,
        tiled=True,
        axis_index_groups=[
            [
                (far * ACROSS + x) * n_col + z * n_half + c
                for far in range(n_far)
                for c in range(n_half)
            ]
            for z in range(HALVES)
            for x in range(ACROSS)
        ],
    ).reshape(n_far * n_half * 4, channels)
    d_pair = pair_call(d_logit, hidden, pair_rep, w_in, w_out, w_head_t, n_row, n_col)
    grad_in, grad_out_t, grad_head_t = final_call(
        share,
        1.0 / (row_count * n_row),
        [
            (channels // n_row, hidden_count // n_col),
            (channels // n_col, hidden_count // n_row),
            (bins_count // n_col, channels // n_row),
        ],
    )
    return (
        d_pair.reshape(row_count, col_count, channels),
        grad_in,
        grad_out_t.T,
        grad_head_t.T,
    )


def solution(mesh):
    placed = (P("row", "col", None), P("row", "col"), P(), P(), P())
    return jax.shard_map(
        shards,
        mesh=mesh,
        in_specs=placed,
        out_specs=(P("row", "col", None), P("row", "col"), P("row", "col"), P("row", "col")),
        check_vma=False,
    )
```

```python
import functools

import jax
import jax.numpy as jnp
from jax import lax
from jax.experimental import pallas as pl
from jax.experimental.pallas import tpu as pltpu
from jax.sharding import PartitionSpec as P

epsilon = 1e-05
f32 = jnp.float32
bf16 = jnp.bfloat16

code_steps = 2350.0

CYCLES = 2
CHUNKS = 2

ACROSS = 4
HALVES = 2


def dot(first, second):
    return jnp.dot(first, second, preferred_element_type=f32)


def dot_t(first, second):
    return lax.dot_general(first, second, (((1,), (1,)), ((), ())), preferred_element_type=f32)


def widen(w_head_t):
    blank = jnp.zeros_like(w_head_t)
    return jnp.concatenate(
        [
            jnp.concatenate([w_head_t, blank], axis=1),
            jnp.concatenate([blank, w_head_t], axis=1),
        ],
        axis=0,
    )


def encode(values):
    size = jnp.log(1.0 + jnp.abs(values)) * code_steps + 0.5
    return jnp.where(values < 0.0, -size, size).astype(jnp.int32)


def decode(codes):
    codes = codes.astype(f32)
    size = jnp.exp(jnp.abs(codes) * (1.0 / code_steps)) - 1.0
    return jnp.where(codes < 0.0, -size, size)


def normalize(values):
    centred = values - jnp.mean(values, axis=-1, keepdims=True)
    variance = jnp.mean(centred * centred, axis=-1, keepdims=True)
    inv_std = lax.rsqrt(variance + epsilon)
    return (centred * inv_std, inv_std)


def send_kernel(pair_ref, w_in_ref, w_out_ref, w_head_t_ref, send_ref, rows_ref):
    n_row = send_ref.shape[0]
    span = send_ref.shape[1]
    channels = pair_ref.shape[-1]
    count = pair_ref.shape[1] // CHUNKS
    half = count * pair_ref.shape[2]
    w_wide = widen(w_head_t_ref[...])
    for g in range(CHUNKS):
        values = pair_ref[:, g * count : (g + 1) * count].reshape(-1, channels).astype(f32)
        x_hat, _ = normalize(values)
        hidden = jnp.maximum(dot(x_hat.astype(bf16), w_in_ref[...]), 0.0).astype(bf16)
        residual = (values + dot(hidden, w_out_ref[...])).astype(bf16)
        wide = jnp.concatenate([residual[:half], residual[half:]], axis=1)
        rows_ref[g * half : (g + 1) * half] = encode(dot_t(wide, w_wide))
    for r in range(n_row):
        send_ref[r] = rows_ref[pl.ds(r, span, stride=n_row), :].astype(jnp.int16)


def prepare_kernel(
    pair_ref,
    bins_ref,
    w_in_ref,
    w_out_ref,
    w_head_t_ref,
    hidden_ref,
    logits_ref,
    bins_wide_ref,
    w_out_t_ref,
    normed_t_hbm,
    residual_t_hbm,
    normed_t_ref,
    residual_t_ref,
    values_ref,
    sems,
):
    kept = (
        (normed_t_ref, normed_t_hbm),
        (residual_t_ref, residual_t_hbm),
    )
    copies = [
        pltpu.make_async_copy(source, target, sems.at[i])
        for i, (source, target) in enumerate(kept)
    ]
    channels = pair_ref.shape[-1]
    n_row = pair_ref.shape[2] // CYCLES
    count = pair_ref.shape[1]
    for a in range(CYCLES):
        for b in range(CYCLES):
            values_ref[a, :, b] = pair_ref[b, :, a * n_row : (a + 1) * n_row, :].astype(f32)
    values = values_ref[...].reshape(-1, channels)
    half = values.shape[0] // CYCLES
    x_hat, _ = normalize(values)
    normed = x_hat.astype(bf16)
    hidden = jnp.maximum(dot(normed, w_in_ref[...]), 0.0).astype(bf16)
    residual = (values + dot(hidden, w_out_ref[...])).astype(bf16)
    hidden_ref[...] = hidden
    w_out_t_ref[...] = w_out_ref[...].T
    normed_t_ref[...] = normed.T
    residual_t_ref[...] = residual.T
    logits_ref[...] = dot_t(
        jnp.concatenate([residual[:half], residual[half:]], axis=1), widen(w_head_t_ref[...])
    )
    for copy in copies:
        copy.start()
    columns = bins_ref.shape[-1]
    row_of = lax.broadcasted_iota(jnp.int32, (1, n_row, columns), 1)
    column_of = lax.broadcasted_iota(jnp.int32, (1, n_row, columns), 2)
    own = column_of % n_row == row_of
    lane = lax.broadcasted_iota(jnp.int32, (columns, channels), 1)
    source = lax.broadcasted_iota(jnp.int32, (columns, channels), 0)
    spread = (lane // (channels // CYCLES) == source // n_row).astype(f32).astype(bf16)
    for b in range(CYCLES):
        bins = bins_ref[b].astype(f32)
        picked = jnp.where(own, jnp.broadcast_to(bins[:, None, :], (count, n_row, columns)), 0.0)
        wide = dot(picked.reshape(count * n_row, columns).astype(bf16), spread)
        bins_wide_ref[:, b] = wide.astype(bf16).reshape(count, n_row, channels)
    for copy in copies:
        copy.wait()


def weights_kernel(
    recv_ref,
    logits_ref,
    bins_wide_ref,
    hidden_ref,
    w_out_t_ref,
    normed_t_hbm,
    residual_t_hbm,
    w_head_t_ref,
    d_logit_ref,
    part_ref,
    normed_t_ref,
    residual_t_ref,
    rows_ref,
    sems,
):
    n_row, span, channels = recv_ref.shape
    bins_count = channels // CYCLES
    half = span * n_row
    copies = [
        pltpu.make_async_copy(source, target, sems.at[i])
        for i, (source, target) in enumerate(
            ((normed_t_hbm, normed_t_ref), (residual_t_hbm, residual_t_ref))
        )
    ]
    for copy in copies:
        copy.start()

    for r in range(n_row):
        rows_ref[pl.ds(r, span, stride=n_row), :] = decode(recv_ref[r])
    sym = logits_ref[...] + rows_ref[0:half, :]
    lane = lax.broadcasted_iota(jnp.int32, (1, channels), 1)
    left = lane < bins_count
    low = jnp.max(jnp.where(left, sym, -jnp.inf), axis=-1, keepdims=True)
    high = jnp.max(jnp.where(left, -jnp.inf, sym), axis=-1, keepdims=True)
    grown = jnp.exp(sym - jnp.where(left, low, high))
    low = jnp.sum(jnp.where(left, grown, 0.0), axis=-1, keepdims=True)
    high = jnp.sum(jnp.where(left, 0.0, grown), axis=-1, keepdims=True)
    probability = grown / jnp.where(left, low, high)
    own_bin = (lane % bins_count).astype(f32)
    bins = bins_wide_ref[...].reshape(half, channels).astype(f32)
    d_sym = probability - jnp.where(bins == own_bin, 1.0, 0.0)
    d_logit = (d_sym + d_sym).astype(bf16)
    d_logit_ref[...] = d_logit

    d_update = pair_gradient(d_logit, w_head_t_ref[...]).astype(bf16)
    hidden = hidden_ref[...]
    d_hidden = hidden_gradient(dot(d_update, w_out_t_ref[...]), hidden)
    for copy in copies:
        copy.wait()
    g_head = jnp.where(
        left,
        dot(residual_t_ref[:, :half], d_logit),
        dot(residual_t_ref[:, half:], d_logit),
    )
    d_logit_t = d_logit.T
    g_mid = (
        dot(d_logit_t, hidden[:half])[:bins_count] + dot(d_logit_t, hidden[half:])[bins_count:]
    )
    g_in = dot(normed_t_ref[...], d_hidden)
    high = g_mid.astype(bf16)
    rest = (g_mid - high.astype(f32)).astype(bf16)
    w_head = w_head_t_ref[...].T
    g_out = (dot(w_head, high) + dot(w_head, rest)).T
    g_out_turned = pltpu.roll(g_out, bins_count, 1)
    g_head = g_head + pltpu.roll(g_head, bins_count, 1)
    g_head_turned = pltpu.roll(g_head, channels - bins_count // HALVES, 1)
    rows = channels // n_row
    tiles = hidden.shape[1] // channels // HALVES
    wide = tiles * rows
    long = g_out.shape[0] // n_row
    n_far = n_row // ACROSS
    for z in range(HALVES):
        for x in range(ACROSS):
            slot = z * ACROSS + x
            heads = []
            for far in range(n_far):
                r = far * ACROSS + x
                base = far * (wide + long // 2)
                mine = g_in[r * rows : (r + 1) * rows, :]
                part_ref[slot, base : base + wide, :] = jnp.concatenate(
                    [mine[:, t * channels : (t + 1) * channels] for t in range(z * tiles, (z + 1) * tiles)],
                    axis=0,
                ).astype(bf16)
                first = slice(r * long, r * long + long // 2)
                second = slice(r * long + long // 2, (r + 1) * long)
                part_ref[slot, base + wide : base + wide + long // 2, :] = jnp.where(
                    left,
                    (g_out if z == 0 else g_out_turned)[first],
                    (g_out_turned if z == 0 else g_out)[second],
                ).astype(bf16)
                heads.append((g_head if z == 0 else g_head_turned)[r * rows : (r + 1) * rows])
            part_ref[slot, n_far * (wide + long // 2) :, :] = jnp.concatenate(heads, axis=0).astype(
                bf16
            )


def pair_gradient(d_logit, w_head_t):
    wide = dot(d_logit, widen(w_head_t))
    channels = wide.shape[1] // CYCLES
    return jnp.concatenate([wide[:, :channels], wide[:, channels:]], axis=0)


def hidden_gradient(back, hidden):
    back = back.astype(bf16)
    return jnp.where(hidden > 0, back, jnp.zeros_like(back))


def pair_kernel(
    d_logit_ref, hidden_ref, pair_ref, w_in_ref, w_out_ref, w_head_t_ref, grad_ref, values_ref
):
    channels = grad_ref.shape[-1]
    count = grad_ref.shape[1]
    n_row = grad_ref.shape[2] // CYCLES
    d_resid = pair_gradient(d_logit_ref[...], w_head_t_ref[...])
    d_hidden = hidden_gradient(dot_t(d_resid.astype(bf16), w_out_ref[...]), hidden_ref[...])
    d_normed = dot_t(d_hidden, w_in_ref[...])
    for a in range(CYCLES):
        for b in range(CYCLES):
            values_ref[a, :, b] = pair_ref[b, :, a * n_row : (a + 1) * n_row, :].astype(f32)
    x_hat, inv_std = normalize(values_ref[...].reshape(-1, channels))
    first_mean = jnp.mean(d_normed, axis=-1, keepdims=True)
    second_mean = jnp.mean(d_normed * x_hat, axis=-1, keepdims=True)
    d_pair = d_resid + inv_std * (d_normed - first_mean - x_hat * second_mean)
    d_pair = d_pair.astype(bf16).reshape(CYCLES, count, CYCLES, n_row, channels)
    for a in range(CYCLES):
        for b in range(CYCLES):
            grad_ref[b, :, a * n_row : (a + 1) * n_row, :] = d_pair[a, :, b]


def lanes_of(shape, axis):
    return lax.broadcasted_iota(jnp.int32, shape, axis)


def fold_matrix(width, kind):
    shape = (128, 128)
    return (lanes_of(shape, 0) % width == lanes_of(shape, 1) % width).astype(f32).astype(kind)


def middle_kernel(recv_ref, out_ref, rows_ref, send_ref):
    total = recv_ref[0].astype(f32)
    for source in range(1, recv_ref.shape[0]):
        total = total + recv_ref[source].astype(f32)
    n_far = rows_ref.shape[0]
    for far in range(n_far):
        pack(
            total[far * 32 : far * 32 + 16],
            total[far * 32 + 16 : far * 32 + 32],
            total[n_far * 32 + far * 8 : n_far * 32 + far * 8 + 8],
            rows_ref.at[far],
            send_ref,
            far * 64,
        )
    out_ref[...] = send_ref[0 : out_ref.shape[0], :].astype(bf16)


def pack(wide, long, head, rows_ref, send_ref, base):
    count = 16
    rows, tiles = 8, 2
    group = lanes_of((1, rows, 128), 2) // 16 == lanes_of((1, rows, 128), 1)
    spread = jnp.where(group, jnp.broadcast_to(wide[:, None, :], (rows * tiles, rows, 128)), 0.0)
    folded = dot(spread.reshape(-1, 128).astype(bf16), fold_matrix(16, bf16))
    folded = folded.reshape(tiles, rows, rows, 128)
    slot = lanes_of((1, rows, 1, 128), 3) // 16 == (8 - lanes_of((1, rows, 1, 128), 1)) % 8
    part_in = jnp.sum(jnp.where(slot, folded, 0.0), axis=1).reshape(count, 128)
    send_ref[pl.ds(base, count, stride=4), :] = part_in
    lane = lanes_of((1, 128), 1)
    mine = jnp.concatenate([long, pltpu.roll(long, 64, 1)], axis=0)
    rows_ref[0] = jnp.concatenate([mine] * 4, axis=0).T
    part_out = rows_ref[0, pl.ds(0, count, stride=4), :]
    for j in range(1, 4):
        part_out = jnp.where(
            lane // 32 == 4 - j, rows_ref[0, pl.ds(j, count, stride=4), :], part_out
        )
    send_ref[pl.ds(base + 1, count, stride=4), :] = part_out
    rows_ref[1] = jnp.concatenate([head] * 16, axis=0).T
    part_head = jnp.where(
        lane // 8 == 15,
        rows_ref[1, pl.ds(1, count, stride=2), :],
        rows_ref[1, pl.ds(0, count, stride=2), :],
    )
    send_ref[pl.ds(base + 2, count, stride=4), :] = part_head
    send_ref[pl.ds(base + 3, count, stride=4), :] = jnp.zeros_like(part_head)


def final_kernel(scale, recv_ref, in_ref, out_t_ref, head_t_ref):
    values = recv_ref[...].astype(f32)
    total = values[0:8]
    for c in range(1, values.shape[0] // 8):
        total = total + values[c * 8 : (c + 1) * 8]
    total = (total[0:4] + total[4:8]) * scale

    def unfold(row, out):
        count, width = out.shape
        if width * 8 <= 128:
            spread = jnp.broadcast_to(row, (8, 128))
            spread = pltpu.roll(spread, 0, 1, stride=width, stride_axis=0)
        else:
            spread = jnp.concatenate(
                [pltpu.roll(row, i * width, 1) if i else row for i in range(count)], axis=0
            )
        out[...] = spread[:count, :width]

    unfold(total[0:1], in_ref)
    unfold(total[1:2], out_t_ref)
    unfold(total[2:3], head_t_ref)


ROOM = 48 * 1024 * 1024


def params(limit=62 * 1024 * 1024):
    return pltpu.CompilerParams(vmem_limit_bytes=limit)


def in_hbm(array):
    return pltpu.with_memory_space_constraint(array, pltpu.HBM)


def forward_call(pair_rep, w_in, w_out, w_head_t, n_row, n_col):
    row_count, col_count, channels = pair_rep.shape
    return pl.pallas_call(
        send_kernel,
        out_shape=jax.ShapeDtypeStruct((n_row, CYCLES * n_col, channels), jnp.int16),
        scratch_shapes=[pltpu.VMEM((CYCLES * n_col * n_row + n_row, channels), jnp.int32)],
        compiler_params=params(),
        name="forward",
    )(pair_rep.reshape(CYCLES, n_col, col_count, channels), w_in, w_out, w_head_t)


HERE = pl.BlockSpec()
THERE = pl.BlockSpec(memory_space=pl.ANY)


def prepare_call(pair_rep, true_bins, w_in, w_out, w_head_t, n_row, n_col):
    row_count, col_count, channels = pair_rep.shape
    pairs = row_count * col_count
    hidden_count = w_in.shape[1]
    away = [
        jax.ShapeDtypeStruct((channels, pairs), bf16),
        jax.ShapeDtypeStruct((channels, pairs), bf16),
    ]
    results = pl.pallas_call(
        prepare_kernel,
        in_specs=[HERE] * 5,
        out_specs=[HERE] * 4 + [pl.BlockSpec(memory_space=pltpu.HBM)] * 2,
        out_shape=[
            jax.ShapeDtypeStruct((pairs, hidden_count), bf16),
            jax.ShapeDtypeStruct((pairs // CYCLES, channels), f32),
            jax.ShapeDtypeStruct((n_col, CYCLES, n_row, channels), bf16),
            jax.ShapeDtypeStruct((channels, hidden_count), bf16),
            *away,
        ],
        scratch_shapes=[pltpu.VMEM(x.shape, x.dtype) for x in away]
        + [
            pltpu.VMEM((CYCLES, n_col, CYCLES, n_row, channels), f32),
            pltpu.SemaphoreType.DMA((len(away),)),
        ],
        compiler_params=params(ROOM),
        cost_estimate=pl.CostEstimate(
            flops=2 * pairs * 2 * channels * hidden_count, bytes_accessed=8 * 2**20, transcendentals=0
        ),
        name="prepare",
    )(
        in_hbm(pair_rep.reshape(CYCLES, n_col, col_count, channels)),
        true_bins.reshape(CYCLES, n_col, col_count),
        in_hbm(w_in),
        in_hbm(w_out),
        in_hbm(w_head_t),
    )
    return results[:4], [in_hbm(x) for x in results[4:]]


def weights_call(recv, near, normed_t, residual_t, w_head_t):
    logits, bins_wide, hidden, w_out_t = near
    n_row, span, channels = recv.shape
    pairs, hidden_count = hidden.shape
    far_rows = hidden_count // n_row // 2 + channels // n_row * (hidden_count // channels) // HALVES
    part_rows = n_row // ACROSS * (far_rows + channels // n_row)
    d_logit = jax.ShapeDtypeStruct((pairs // CYCLES, channels), bf16)
    late = (normed_t, residual_t)
    return pl.pallas_call(
        weights_kernel,
        in_specs=[HERE] * 5 + [THERE] * 2 + [HERE],
        out_specs=[HERE, HERE],
        out_shape=[d_logit, jax.ShapeDtypeStruct((HALVES * ACROSS, part_rows, channels), bf16)],
        scratch_shapes=[pltpu.VMEM(x.shape, x.dtype) for x in late]
        + [
            pltpu.VMEM((pairs // CYCLES + n_row, channels), f32),
            pltpu.SemaphoreType.DMA((len(late),)),
        ],
        compiler_params=params(ROOM),
        name="weights",
    )(recv, logits, bins_wide, hidden, w_out_t, normed_t, residual_t, w_head_t)


def pair_call(d_logit, hidden, pair_rep, w_in, w_out, w_head_t, n_row, n_col):
    row_count, col_count, channels = pair_rep.shape
    pairs, hidden_count = hidden.shape
    cycled = pair_rep.reshape(CYCLES, n_col, col_count, channels)
    return pl.pallas_call(
        pair_kernel,
        out_shape=jax.ShapeDtypeStruct(cycled.shape, bf16),
        scratch_shapes=[pltpu.VMEM((CYCLES, n_col, CYCLES, n_row, channels), f32)],
        compiler_params=params(ROOM),
        cost_estimate=pl.CostEstimate(
            flops=2 * pairs * 2 * channels * hidden_count, bytes_accessed=5 * 2**20, transcendentals=0
        ),
        name="pair",
    )(d_logit, hidden, *[in_hbm(x) for x in (cycled, w_in, w_out, w_head_t)])


def middle_call(part, n_row, n_col):
    n_far = n_row // ACROSS
    shape = (n_far * (n_col // HALVES) * 4, part.shape[-1])
    return pl.pallas_call(
        middle_kernel,
        out_shape=jax.ShapeDtypeStruct(shape, bf16),
        scratch_shapes=[
            pltpu.VMEM((n_far, 2, 128, 128), f32),
            pltpu.VMEM((shape[0] + 8, shape[1]), f32),
        ],
        compiler_params=params(ROOM),
        name="sum_near",
    )(part)


def final_call(share, scale, shapes):
    return pl.pallas_call(
        functools.partial(final_kernel, scale),
        out_shape=[jax.ShapeDtypeStruct(shape, f32) for shape in shapes],
        compiler_params=params(ROOM),
        name="sum_rest",
    )(share)


def shards(pair_rep, true_bins, w_in, w_out, w_head):
    row_count, col_count, channels = pair_rep.shape
    n_row = lax.axis_size("row")
    n_col = lax.axis_size("col")
    hidden_count = w_in.shape[1]
    bins_count = w_head.shape[1]
    w_head_t = w_head.T

    send = forward_call(pair_rep, w_in, w_out, w_head_t, n_row, n_col)
    recv = lax.all_to_all(
        send.reshape(n_row * n_col, CYCLES, channels),
        ("row", "col"),
        split_axis=0,
        concat_axis=0,
        tiled=True,
    ).reshape(n_row, CYCLES * n_col, channels)
    (hidden, logits, bins_wide, w_out_t), (normed_t, residual_t) = (
        prepare_call(pair_rep, true_bins, w_in, w_out, w_head_t, n_row, n_col)
    )
    d_logit, part = weights_call(
        recv, (logits, bins_wide, hidden, w_out_t), normed_t, residual_t, w_head_t
    )
    n_far, n_half = n_row // ACROSS, n_col // HALVES
    part = lax.all_to_all(
        part,
        ("row", "col"),
        split_axis=0,
        concat_axis=0,
        tiled=True,
        axis_index_groups=[
            [
                (far * ACROSS + x) * n_col + z * n_half + c
                for z in range(HALVES)
                for x in range(ACROSS)
            ]
            for far in range(n_far)
            for c in range(n_half)
        ],
    )
    share = middle_call(part, n_row, n_col)
    share = lax.all_to_all(
        share.reshape(n_far * n_half, 4, channels),
        ("row", "col"),
        split_axis=0,
        concat_axis=0,
        tiled=True,
        axis_index_groups=[
            [
                (far * ACROSS + x) * n_col + z * n_half + c
                for far in range(n_far)
                for c in range(n_half)
            ]
            for z in range(HALVES)
            for x in range(ACROSS)
        ],
    ).reshape(n_far * n_half * 4, channels)
    d_pair = pair_call(d_logit, hidden, pair_rep, w_in, w_out, w_head_t, n_row, n_col)
    grad_in, grad_out_t, grad_head_t = final_call(
        share,
        1.0 / (row_count * n_row),
        [
            (channels // n_row, hidden_count // n_col),
            (channels // n_col, hidden_count // n_row),
            (bins_count // n_col, channels // n_row),
        ],
    )
    return (
        d_pair.reshape(row_count, col_count, channels),
        grad_in,
        grad_out_t.T,
        grad_head_t.T,
    )


def solution(mesh):
    placed = (P("row", "col", None), P("row", "col"), P(), P(), P())
    return jax.shard_map(
        shards,
        mesh=mesh,
        in_specs=placed,
        out_specs=(P("row", "col", None), P("row", "col"), P("row", "col"), P("row", "col")),
        check_vma=False,
    )
```
